128 devices in a mesh: section: 2 (over core), dp: 8 (over y, z_lo), tensor: 8 (over z_hi, x).
Axes of the slice: x: 4, y: 4, z: 4 (z_hi: 2, z_lo: 2; z = z_hi * 2 + z_lo), core: 2. Of those that a mesh axis runs over, the one named last changes fastest.
Arguments:
- ends_in: bfloat16 [2, 16384, 1024], P('section', 'dp'), may hold values from -6 to 6
- ln_gains: float32 [2, 2, 1024], P('section'), may hold values from 0.1 to 1.9
- ln_biases: float32 [2, 2, 1024], P('section'), may hold values from -4 to 4
- qkv_weight: bfloat16 [2, 3, 1024, 1024], P('section', None, 'dp', 'tensor'), may hold values from -0.1875 to 0.1875
- qkv_bias: float32 [2, 3, 1024], P('section', None, 'tensor'), may hold values from -4 to 4
- dense_weight: bfloat16 [2, 1024, 1024], P('section', 'tensor', 'dp'), may hold values from -1.5 to 1.5
- up_weight: bfloat16 [2, 1024, 4096], P('section', 'dp', 'tensor'), may hold values from -0.1875 to 0.1875
- up_bias: float32 [2, 4096], P('section', 'tensor'), may hold values from -4 to 4
- down_weight: bfloat16 [2, 4096, 1024], P('section', 'tensor', 'dp'), may hold values from -0.09375 to 0.09375
- out_bias: float32 [2, 1024], P('section'), may hold values from -4 to 4
Outputs:
- ends_out: bfloat16 [2, 16384, 1024], P('section', 'dp')
- ln_gains_grad: float32 [2, 2, 1024], P('section')
- ln_biases_grad: float32 [2, 2, 1024], P('section')
- qkv_weight_grad: float32 [2, 3, 1024, 1024], P('section', None, 'dp', 'tensor')
- qkv_bias_grad: float32 [2, 3, 1024], P('section', None, 'tensor')
- dense_weight_grad: float32 [2, 1024, 1024], P('section', 'tensor', 'dp')
- up_weight_grad: float32 [2, 1024, 4096], P('section', 'dp', 'tensor')
- up_bias_grad: float32 [2, 4096], P('section', 'tensor')
- down_weight_grad: float32 [2, 4096, 1024], P('section', 'tensor', 'dp')
- out_bias_grad: float32 [2, 1024], P('section')
The draws below stay inside these ranges and needn't reach their ends.
All inputs are finite; a program needn't handle non-finite values.
Results may differ from the reference program's by a relative error of at most 0.02.
Values may be sent and summed in bfloat16 or wider, within the bound.
A program may use at most 192 MiB of HBM per device.

```python
import jax
import jax.numpy as jnp
from jax import lax

D = 1024
H = 16
HD = 64
FF = 4096
LEN = 1024
ROT = 16
TOKENS = 16384


def block_scale(stream_key, dims, shards, low, high):
    def one(axis_at, parts):
        draws = jax.random.uniform(jax.random.fold_in(jax.random.fold_in(stream_key, 6), axis_at), (parts,), jnp.float32, low / len(shards), high / len(shards))
        return jnp.repeat(jnp.exp(draws), dims[axis_at] // parts).reshape((-1,) + (1,) * (len(dims) - axis_at - 1))

    level = one(*shards[0])
    for cut in shards[1:]:
        level = level * one(*cut)
    return level


def scatter_about(rng, dims, scale, most, shards=(), kind=jnp.bfloat16):
    entries = scale * jax.random.normal(rng, dims, jnp.float32)
    if shards:
        entries = entries * block_scale(rng, dims, shards, -0.22, 0.18)
    return jnp.clip(entries, -most, most).astype(kind)


def setup_inputs(seed: int = 0) -> dict:
    keys = jax.random.split(jax.random.key(seed), 11)
    ends_in = scatter_about(keys[0], (2, TOKENS, D), 1.0, 6.0, ((0, 2), (1, 8)))
    ln_gains = jnp.clip(1.0 + 0.18 * jax.random.normal(keys[1], (2, 2, D), jnp.float32), 0.1, 1.9)
    ln_biases = scatter_about(keys[2], (2, 2, D), 0.3, 4.0, ((0, 2),), jnp.float32)
    qkv_weight = scatter_about(keys[3], (2, 3, D, H * HD), D ** -0.5, 0.1875, ((0, 2), (2, 8), (3, 8)))
    qkv_bias = scatter_about(keys[4], (2, 3, H * HD), 0.3, 4.0, ((0, 2), (2, 8)), jnp.float32)
    dense_weight = scatter_about(keys[5], (2, H * HD, D), (max(H * HD // 64, 1)) ** -0.5, 1.5, ((0, 2), (1, 8), (2, 8)))
    up_weight = scatter_about(keys[6], (2, D, FF), D ** -0.5, 0.1875, ((0, 2), (1, 8), (2, 8)))
    up_bias = scatter_about(keys[7], (2, FF), 0.3, 4.0, ((0, 2), (1, 8)), jnp.float32)
    down_weight = scatter_about(keys[8], (2, FF, D), FF ** -0.5, 0.09375, ((0, 2), (1, 8), (2, 8)))
    out_bias = scatter_about(keys[9], (2, D), 0.3, 4.0, ((0, 2),), jnp.float32)
    return {"ends_in": ends_in, "ln_gains": ln_gains, "ln_biases": ln_biases, "qkv_weight": qkv_weight, "qkv_bias": qkv_bias, "dense_weight": dense_weight, "up_weight": up_weight, "up_bias": up_bias, "down_weight": down_weight, "out_bias": out_bias}


@jax.custom_vjp
def low(v):
    return lax.optimization_barrier(v.astype(jnp.bfloat16)).astype(jnp.float32)

@jax.custom_vjp
def low_back(v):
    return v

def low_keep(v):
    return (low(v), None)

def low_pass(kept, grad):
    return (grad,)

def back_keep(v):
    return (v, None)

def back_low(kept, grad):
    return (low(grad),)
low.defvjp(low_keep, low_pass)
low_back.defvjp(back_keep, back_low)

def layer_norm(stream, gain_row, offset):
    center = lax.optimization_barrier(jnp.mean(stream, axis=-1, keepdims=True))
    centred = stream - center
    variance = lax.optimization_barrier(jnp.mean(centred * centred, axis=-1, keepdims=True))
    return centred * lax.rsqrt(variance + 1e-05) * gain_row + offset

def rotary_tables(length):
    position = jnp.arange(length, dtype=jnp.float32)[:, None]
    exponent = jnp.arange(ROT // 2, dtype=jnp.float32) * 2.0 / ROT
    angles = position * 10000.0 ** (-exponent)
    cosine_table = jnp.concatenate([jnp.cos(angles), jnp.cos(angles)], axis=-1)[:, None, :]
    sine_table = jnp.concatenate([jnp.sin(angles), jnp.sin(angles)], axis=-1)[:, None, :]
    return (cosine_table, sine_table)

def turn(values, cosine_table, sine_table):
    rotary = values[..., :ROT]
    former = rotary[..., :ROT // 2]
    latter = rotary[..., ROT // 2:]
    turned = jnp.concatenate([-latter, former], axis=-1)
    return jnp.concatenate([rotary * cosine_table + turned * sine_table, values[..., ROT:]], axis=-1)

def block(weights, stream, cosine_table, sine_table, allowed):
    gain_rows, offsets, qkv_w, qkv_b, dense_w, up_w, up_b, down_w, out_b = weights
    highest = lax.Precision.HIGHEST
    length = stream.shape[0]
    first_norm = low(layer_norm(stream, gain_rows[0], offsets[0]))
    second_norm = low(layer_norm(stream, gain_rows[1], offsets[1]))
    raw_proj = jnp.einsum('rd,cdn->crn', first_norm, qkv_w, precision=highest) + qkv_b[:, None, :]
    raw_proj = low_back(raw_proj).reshape(3, length, H, HD)
    queries = low(turn(raw_proj[0], cosine_table, sine_table))
    keys_all = low(turn(raw_proj[1], cosine_table, sine_table))
    values_all = low(raw_proj[2])
    scores = jnp.einsum('qhd,khd->hqk', queries, keys_all, precision=highest) * HD ** (-0.5)
    scores = jnp.where(allowed, low_back(scores), -1e+30)
    weights_soft = low(jax.nn.softmax(scores, axis=-1))
    context = jnp.einsum('hqk,khd->qhd', weights_soft, values_all, precision=highest).reshape(length, H * HD)
    context = low_back(low(context))
    hidden = low_back(jnp.dot(second_norm, up_w, precision=highest) + up_b)
    activation = low(jax.nn.gelu(hidden, approximate=False))
    branch = jnp.dot(context, dense_w, precision=highest) + jnp.dot(activation, down_w, precision=highest)
    return stream + low_back(branch) + out_b

def reference(ends_in, ln_gains, ln_biases, qkv_weight, qkv_bias, dense_weight, up_weight, up_bias, down_weight, out_bias):
    params = tuple((weight.astype(jnp.float32) for weight in (ln_gains, ln_biases, qkv_weight, qkv_bias, dense_weight, up_weight, up_bias, down_weight, out_bias)))
    inputs = ends_in[0].astype(jnp.float32).reshape(-1, LEN, D)
    cotangent = ends_in[1].astype(jnp.float32).reshape(-1, LEN, D)
    cosine_table, sine_table = rotary_tables(LEN)
    allowed = jnp.arange(LEN)[:, None] >= jnp.arange(LEN)[None, :]

    def model(weights, streams):
        first_layer = jax.tree.map(lambda matrix: matrix[0], weights)
        second_layer = jax.tree.map(lambda matrix: matrix[1], weights)

        def one_sequence(stream):
            middle = block(first_layer, stream, cosine_table, sine_table, allowed)
            return block(second_layer, low_back(low(middle)), cosine_table, sine_table, allowed)
        return lax.map(jax.checkpoint(one_sequence), streams)
    outputs, pullback = jax.vjp(model, params, inputs)
    gradients, input_grad = pullback(cotangent)
    ends_out = jnp.stack([input_grad.reshape(-1, D), outputs.reshape(-1, D)]).astype(jnp.bfloat16)
    return (ends_out, gradients[0], gradients[1], gradients[2], gradients[3], gradients[4], gradients[5], gradients[6], gradients[7], gradients[8])
```

```python
import functools

import jax
import jax.numpy as jnp
import numpy as np
from jax import lax
from jax.experimental import pallas as pl
from jax.experimental.pallas import tpu as pltpu
from jax.sharding import PartitionSpec as P

MESH = pl.DeviceIdType.MESH
BF = jnp.bfloat16
F32 = jnp.float32

D = 1024
LEN = 1024
HD = 64
ROT = 16
NIN = 896
NOUT = 640
NALL = NIN + NOUT
BQ = 256
NCH = 2
R = LEN // NCH
HALF = R // 2
QUARTER = R // 8
BM = min(256, HALF)
NB = HALF // BM
W_PARTS = (((0, NIN), (NIN, NALL)), ((0, NALL),))
G_PARTS = ((384, NALL), (0, 384))


def dot(a, b, ca, cb):
    return lax.dot_general(a, b, (((ca,), (cb,)), ((), ())), preferred_element_type=F32)


def rotary_tables():
    position = np.arange(LEN, dtype=np.float32)[:, None]
    exponent = np.arange(ROT // 2, dtype=np.float32) * np.float32(2.0) / np.float32(ROT)
    angles = (position * np.float32(10000.0) ** (-exponent)).astype(np.float32)
    cosine = np.ones((LEN, 2 * HD), np.float32)
    sine = np.zeros((LEN, 2 * HD), np.float32)
    for first in (0, 8, HD, HD + 8):
        cosine[:, first : first + 8] = np.cos(angles)
        sine[:, first : first + 8] = np.sin(angles)
    return cosine, sine


def lanes_of_head(shape):
    return lax.broadcasted_iota(jnp.int32, shape, 1) % HD


def turn(value, cosine, sine):
    lane = lanes_of_head(value.shape)
    partner = jnp.where(lane < 8, -pltpu.roll(value, 120, 1), pltpu.roll(value, 8, 1))
    return value * cosine + partner * sine


def turn_back(grad, cosine, sine):
    lane = lanes_of_head(grad.shape)
    moved = grad * sine
    partner = jnp.where(
        lane < 8, pltpu.roll(moved, 120, 1), jnp.where(lane < 16, -pltpu.roll(moved, 8, 1), 0.0)
    )
    return grad * cosine + partner


def gelu_and_slope(hidden):
    bell = jnp.exp(-0.5 * hidden * hidden)
    size = 1.0 + (0.3275911 * 0.7071067811865476) * jnp.abs(hidden)
    t = pltpu.reciprocal(size, approx=True)
    t = t * (2.0 - size * t)
    series = t * (
        0.254829592 * 0.5
        + t
        * (
            -0.284496736 * 0.5
            + t * (1.421413741 * 0.5 + t * (-1.453152027 * 0.5 + t * (1.061405429 * 0.5)))
        )
    )
    tail = series * bell
    below = jnp.where(hidden >= 0.0, 1.0 - tail, tail)
    return hidden * below, below + hidden * bell * 0.3989422804014327


def standardize(value):
    center = jnp.mean(value, axis=-1, keepdims=True)
    centred = value - center
    inverse = lax.rsqrt(jnp.mean(centred * centred, axis=-1, keepdims=True) + 1e-05)
    return centred * inverse, inverse


def stack_heads(value):
    lane = lax.broadcasted_iota(jnp.int32, value.shape, 1)
    wide = value.astype(F32)
    return jnp.concatenate(
        [jnp.where(lane < HD, wide, 0.0), jnp.where(lane >= HD, wide, 0.0)], axis=0
    ).astype(BF)


def split_heads(value):
    half = value.shape[1] // 2
    return jnp.concatenate([value[:HD, :half], value[HD:, half:]], axis=0)


def pair(i, j):
    return i * (i + 1) // 2 + j


def kernel(
    ends,
    qkv,
    dense,
    up,
    down,
    gains,
    offsets,
    qkv_b,
    up_b,
    out_b,
    cosine,
    sine,
    ends_out,
    g_gains,
    g_offsets,
    g_qkv,
    g_qkv_b,
    g_dense,
    g_up,
    g_up_b,
    g_down,
    g_out_b,
    shard,
    extra,
    extras,
    bias_row,
    out_row,
    weights,
    x_in,
    grads_in,
    xhat,
    y_mid,
    joined,
    slope,
    queries,
    keys,
    values,
    keys_t,
    values_t,
    soft,
    soft_scale,
    context_t,
    scores,
    d_context,
    d_joined,
    d_keys,
    d_values,
    part,
    core_part,
    ring_part,
    ends_low,
    w_grad,
    plane_a,
    plane_b,
    sum_a,
    sum_b,
    own_a,
    own_b,
    total,
    message,
    messages,
    bias_total,
    ln_own,
    ln_ring,
    ln_plane,
    local_sem,
    swap_s,
    swap_r,
    w1_s,
    w_r,
    w2a_s,
    w2b_s,
    extra_s,
    extra_r,
    core_s,
    core_r,
    ring_s,
    ring_r,
    gx_s,
    gx_r,
    gc_s,
    gc_r,
    out_s,
    out_r,
    across_s,
    across_r,
    direct_s,
    direct_r,
    direct2_s,
    direct2_r,
    msg_s,
    msg_r,
    p1a_s,
    p1a_r,
    p1b_s,
    p1b_r,
    p2a_s,
    p2a_r,
    p2b_s,
    p2b_r,
    ln1_s,
    ln1_r,
    ln2_s,
    ln2_r,
):
    core = lax.axis_index("section")
    dp = lax.axis_index("dp")
    t = lax.axis_index("tensor")
    y, z_lo = dp // 2, dp % 2
    z_hi, x = t // 4, t % 4
    z = 2 * z_hi + z_lo
    forwarder = core == z_hi

    def device(c_, y_, z_, x_):
        return {"section": c_, "dp": y_ * 2 + z_ % 2, "tensor": (z_ // 2) * 4 + x_}

    drains = {}

    def wait(ref, sem):
        pltpu.make_async_copy(ref, ref, sem).wait()

    def push(src, dst, send, recv, where, tag="end"):
        pltpu.make_async_remote_copy(
            src_ref=src, dst_ref=dst, send_sem=send, recv_sem=recv, device_id=where, device_id_type=MESH
        ).start()
        drains.setdefault(tag, []).append((None, src, send))

    def push_or_keep(own, src, dst, send, recv, where):
        other = jnp.logical_not(own)

        @pl.when(own)
        def _():
            pltpu.make_async_copy(src, dst, recv).start()

        @pl.when(other)
        def _():
            pltpu.make_async_remote_copy(
                src_ref=src,
                dst_ref=dst,
                send_sem=send,
                recv_sem=recv,
                device_id=where,
                device_id_type=MESH,
            ).start()

        drains.setdefault("end", []).append((other, src, send))

    def drain(tag):
        for condition, src, send in drains.pop(tag, []):
            if condition is None:
                wait(src, send)
            else:
                pl.when(condition)(functools.partial(wait, src, send))

    barrier = pltpu.get_barrier_semaphore()
    for dy in range(4):
        for dz in range(4):
            for c_ in range(2):
                if (dy, dz, c_) == (0, 0, 0):
                    continue
                pl.semaphore_signal(
                    barrier,
                    inc=1,
                    device_id=device((core + c_) % 2, (y + dy) % 4, (z + dz) % 4, x),
                    device_id_type=MESH,
                )
    for j in range(1, 4):
        pl.semaphore_signal(
            barrier, inc=1, device_id=device(core, y, z, (x + j) % 4), device_id_type=MESH
        )

    block = pl.ds(pl.multiple_of(dp * 128, 128), 128)

    def column(row):
        return jnp.broadcast_to(row, (128, 128)).T

    gain_cols = [column(gains[k : k + 1, block]) for k in range(2)]
    offset_cols = [column(offsets[k : k + 1, block]) for k in range(2)]

    def raw_tile(n):
        if n < 3:
            return qkv[n].astype(F32), 0, qkv_b[n]
        cols = slice((n - 3) * 128, (n - 2) * 128)
        return up[:, cols].astype(F32), 1, up_b[:, cols]

    extra[...] = jnp.zeros_like(extra)
    for n in range(7):
        tile, k, bias = raw_tile(n)
        shard[:, n * 128 : (n + 1) * 128] = (tile * gain_cols[k]).astype(BF)
        added = jnp.sum(tile * offset_cols[k], axis=0, keepdims=True) + 0.125 * bias
        extra[n // 2 : n // 2 + 1, (n % 2) * 128 : (n % 2) * 128 + 128] = added
    for n in range(4):
        extra[4 + n : 5 + n, :] = 0.125 * out_b[:, n * 256 : (n + 1) * 256]
    shard[:, NIN : NIN + 128] = dense[...].T
    shard[:, NIN + 128 : NALL] = down[...].T

    pl.semaphore_wait(barrier, 34)

    mine = ends.at[pl.ds(pl.multiple_of(z_hi * LEN, LEN), LEN)]
    for c_, buffer in ((0, x_in), (1, grads_in.at[1])):

        @pl.when(core == c_)
        def _(buffer=buffer):
            pltpu.make_async_copy(mine, buffer, local_sem).start()
            pltpu.make_async_remote_copy(
                src_ref=mine,
                dst_ref=buffer,
                send_sem=swap_s,
                recv_sem=swap_r,
                device_id=device(1 - core, y, z, x),
                device_id_type=MESH,
            ).start()

    def w_rows(l, p, dp_, half):
        rows = pl.ds(pl.multiple_of(dp_ * 128 + half * 64, 64), 64)
        return weights.at[l, rows, slice(*W_PARTS[l][p])]

    def gather_first(l):
        @pl.when(core == l)
        def _():
            for p, cols in enumerate(W_PARTS[l]):
                for half in range(2):
                    src = shard.at[half * 64 : half * 64 + 64, slice(*cols)]
                    dst = w_rows(l, p, dp, half)
                    recv = w_r.at[half, l, p, dp]

                    @pl.when(forwarder)
                    def _(src=src, dst=dst, recv=recv):
                        pltpu.make_async_copy(src, dst, recv).start()

                    for j in range(4):
                        if half == 0:
                            where = device(z_hi, (y + j) % 4, z, x)
                        else:
                            where = device(z_hi, y, (z + j) % 4, x)
                        copy = pltpu.make_async_remote_copy(
                            src_ref=src,
                            dst_ref=dst,
                            send_sem=w1_s.at[p, half, j],
                            recv_sem=recv,
                            device_id=where,
                            device_id_type=MESH,
                        )
                        if j == 0:
                            pl.when(jnp.logical_not(forwarder))(copy.start)
                        else:
                            copy.start()

    def drain_first():
        for l in range(2):

            @pl.when(core == l)
            def _(l=l):
                for p, cols in enumerate(W_PARTS[l]):
                    src = shard.at[0:64, slice(*cols)]
                    for half in range(2):
                        for j in range(4):
                            ended = functools.partial(wait, src, w1_s.at[p, half, j])
                            if j == 0:
                                pl.when(jnp.logical_not(forwarder))(ended)
                            else:
                                ended()

    def gather_second(l, p):
        for k in range(2):
            block_b = w_rows(l, p, y * 2 + k, 1)
            wait(block_b, w_r.at[1, l, p, y * 2 + k])
            for j in range(1, 4):
                push(
                    block_b,
                    block_b,
                    w2b_s.at[l, p, k, j - 1],
                    w_r.at[1, l, p, y * 2 + k],
                    device(core, (y + j) % 4, z, x),
                )

        @pl.when(forwarder)
        def _():
            for y_ in range(4):
                dp_ = y_ * 2 + z_lo
                block_a = w_rows(l, p, dp_, 0)
                wait(block_a, w_r.at[0, l, p, dp_])
                for j in range(1, 4):
                    pltpu.make_async_remote_copy(
                        src_ref=block_a,
                        dst_ref=block_a,
                        send_sem=w2a_s.at[l, p, y_, j - 1],
                        recv_sem=w_r.at[0, l, p, dp_],
                        device_id=device(core, y, (z + j) % 4, x),
                        device_id_type=MESH,
                    ).start()

    def drain_second():
        @pl.when(forwarder)
        def _():
            for l in range(2):
                for p in range(len(W_PARTS[l])):
                    for y_ in range(4):
                        for j in range(3):
                            wait(w_rows(l, p, 0, 0), w2a_s.at[l, p, y_, j])

    def gather_rest(l, p):
        for j in range(1, 4):
            for k in range(2):
                dp_ = ((y + j) % 4) * 2 + k
                wait(w_rows(l, p, dp_, 1), w_r.at[1, l, p, dp_])
        for y_ in range(4):
            dp_ = y_ * 2 + 1 - z_lo
            wait(w_rows(l, p, dp_, 0), w_r.at[0, l, p, dp_])

            @pl.when(jnp.logical_not(forwarder))
            def _(dp_=y_ * 2 + z_lo):
                wait(w_rows(l, p, dp_, 0), w_r.at[0, l, p, dp_])

        if p > 0:
            return
        for dp_ in range(8):
            wait(extras.at[l, dp_], extra_r.at[l, dp_])
        summed = extras[l, 0]
        for dp_ in range(1, 8):
            summed = summed + extras[l, dp_]
        for n in range(4):
            bias_row[l, :, n * 256 : (n + 1) * 256] = summed[n : n + 1, :]
            out_row[l, :, n * 256 : (n + 1) * 256] = summed[4 + n : 5 + n, :]

    gather_first(0)
    for l in range(2):

        @pl.when(core == l)
        def _(l=l):
            for dy in range(4):
                for dz in range(4):
                    where = device(z_hi, (y + dy) % 4, (z + dz) % 4, x)
                    dst = extras.at[l, dp]
                    recv = extra_r.at[l, dp]
                    copy = pltpu.make_async_remote_copy(
                        src_ref=extra,
                        dst_ref=dst,
                        send_sem=extra_s.at[dy * 4 + dz],
                        recv_sem=recv,
                        device_id=where,
                        device_id_type=MESH,
                    )
                    if (dy, dz) == (0, 0):
                        pl.when(forwarder)(pltpu.make_async_copy(extra, dst, recv).start)
                        pl.when(jnp.logical_not(forwarder))(copy.start)
                    else:
                        copy.start()

    def drain_extra():
        for k in range(16):
            if k == 0:
                pl.when(jnp.logical_not(forwarder))(
                    functools.partial(wait, extra, extra_s.at[k])
                )
            else:
                wait(extra, extra_s.at[k])

    wait(x_in, local_sem)
    wait(x_in, swap_r)

    gather_second(0, 0)

    def normalize_rows(i, carry):
        rows = pl.ds(pl.multiple_of(i * 128, 128), 128)
        xhat[0, rows, :] = standardize(x_in[rows, :].astype(F32))[0].astype(BF)
        return carry

    lax.fori_loop(0, LEN // 128, normalize_rows, 0)
    gather_second(0, 1)
    gather_first(1)
    gather_rest(0, 0)

    def project(l, i):
        rows = pl.ds(pl.multiple_of(i * BQ, BQ), BQ)
        low = xhat[l, rows, :]
        raw = dot(low, weights[l, :, 0:384], 1, 0) + bias_row[l, :, 0:384]
        cos_rows, sin_rows = cosine[rows, :], sine[rows, :]
        q = turn(raw[:, 0:128], cos_rows, sin_rows) * HD**-0.5
        k = turn(raw[:, 128:256], cos_rows, sin_rows)
        v = raw[:, 256:384]
        queries[l, rows, :] = q.astype(BF)
        keys[l, rows, :] = k.astype(BF)
        values[l, rows, :] = v.astype(BF)
        keys_t[l, :, rows] = k.T.astype(BF)
        values_t[l, :, rows] = v.T.astype(BF)
        hidden = dot(low, weights[l, :, 384:NIN], 1, 0) + bias_row[l, :, 384:NIN]
        act, gradient = gelu_and_slope(hidden)
        joined[l, rows, 128:NOUT] = act.astype(BF)
        slope[l, rows, :] = gradient.astype(BF)

    def attend(l, i):
        rows = slice(i * BQ, (i + 1) * BQ)
        stacked = stack_heads(queries[l, rows, :])
        largest = None
        for j in range(i + 1):
            tile = dot(keys[l, j * BQ : (j + 1) * BQ, :], stacked, 1, 1)
            if j == i:
                key_at = lax.broadcasted_iota(jnp.int32, tile.shape, 0)
                query_at = lax.broadcasted_iota(jnp.int32, tile.shape, 1) % BQ
                tile = jnp.where(key_at <= query_at, tile, -1e30)
            scores[j * BQ : (j + 1) * BQ, :] = tile
            top = jnp.max(tile, axis=0, keepdims=True)
            largest = top if largest is None else jnp.maximum(largest, top)
        summed = jnp.zeros((1, 2 * BQ), F32)
        outcome = jnp.zeros((2 * HD, 2 * BQ), F32)
        for j in range(i + 1):
            terms = jnp.exp(scores[j * BQ : (j + 1) * BQ, :] - largest)
            summed = summed + jnp.sum(terms, axis=0, keepdims=True)
            low = terms.astype(BF)
            soft[l, pair(i, j)] = low
            outcome = outcome + dot(values_t[l, :, j * BQ : (j + 1) * BQ], low, 1, 0)
        scale = 1.0 / summed
        soft_scale[l, i : i + 1, :] = scale
        context = split_heads(outcome * scale)
        context_t[l, :, rows] = context
        joined[l, rows, 0:128] = context.T.astype(BF)

    def attend_back(l, i):
        rows = slice(i * BQ, (i + 1) * BQ)
        grad_t = d_context[rows, :].astype(F32).T
        scale = soft_scale[l, i : i + 1, :]
        top = grad_t[:HD] * scale[:, :BQ]
        bottom = grad_t[HD:] * scale[:, BQ:]
        context = context_t[l, :, rows]
        delta = jnp.concatenate(
            [
                jnp.sum(context[:HD] * top, axis=0, keepdims=True),
                jnp.sum(context[HD:] * bottom, axis=0, keepdims=True),
            ],
            axis=1,
        )
        blank = jnp.zeros_like(top)
        spread_wide = jnp.concatenate(
            [jnp.concatenate([top, blank], axis=1), jnp.concatenate([blank, bottom], axis=1)], axis=0
        )
        spread_t = spread_wide.astype(BF)
        spread = spread_wide.T.astype(BF)
        stacked = stack_heads(queries[l, rows, :])
        d_query_t = jnp.zeros((2 * HD, 2 * BQ), F32)
        for j in range(i + 1):
            cols = slice(j * BQ, (j + 1) * BQ)
            terms = soft[l, pair(i, j)]
            d_terms = dot(values[l, cols, :], spread_t, 1, 0)
            d_scores = (terms.astype(F32) * (d_terms - delta)).astype(BF)
            d_key = dot(d_scores, stacked, 1, 0)
            d_value = dot(terms, spread, 1, 0)
            if i == LEN // BQ - 1:
                d_keys[cols, :] = d_key
                d_values[cols, :] = d_value
            else:
                d_keys[cols, :] += d_key
                d_values[cols, :] += d_value
            d_query_t = d_query_t + dot(keys_t[l, :, cols], d_scores, 1, 0)
        d_query = split_heads(d_query_t).T * HD**-0.5
        d_joined[rows, 0:128] = turn_back(d_query, cosine[rows, :], sine[rows, :]).astype(BF)

    def finish_keys(i, carry):
        rows = pl.ds(pl.multiple_of(i * BQ, BQ), BQ)
        d_joined[rows, 128:256] = turn_back(d_keys[rows, :], cosine[rows, :], sine[rows, :]).astype(
            BF
        )
        d_joined[rows, 256:384] = d_values[rows, :].astype(BF)
        return carry

    def blocks_of(ck):
        return range(ck * R // BQ, (ck + 1) * R // BQ)

    def forward(l, ck):
        def one(i, carry):
            project(l, i)
            return carry

        lax.fori_loop(ck * R // BQ, (ck + 1) * R // BQ, one, 0)
        for i in blocks_of(ck):
            attend(l, i)

    def backward_first(l, ck):
        def one(i, carry):
            rows = pl.ds(pl.multiple_of(i * BQ, BQ), BQ)
            both = dot(grads_in[l, rows, :], weights[l, :, NIN:NALL], 1, 0)
            d_context[rows, :] = both[:, 0:128].astype(BF)
            d_joined[rows, 384:NIN] = (both[:, 128:NOUT] * slope[l, rows, :].astype(F32)).astype(BF)
            return carry

        lax.fori_loop(ck * R // BQ, (ck + 1) * R // BQ, one, 0)

    def backward_second(l, ck):
        for i in reversed(blocks_of(ck)):
            attend_back(l, i)
        lax.fori_loop(ck * R // BQ, (ck + 1) * R // BQ, finish_keys, 0)

    def branch(l, rows):
        return dot(joined[l, rows, :], weights[l, :, NIN:NALL], 1, 1)

    def norm_grad(l, rows):
        return dot(d_joined[rows, :], weights[l, :, 0:NIN], 1, 1)

    def own_rows(ck, part_=None):
        first = ck * R + core * HALF + x * QUARTER
        return pl.ds(pl.multiple_of(first, QUARTER), QUARTER)

    def reduce_send(ph, ck, term):
        slot = ph % 2
        drain(("part", ck))
        for b in range(NB):
            rows = pl.ds(pl.multiple_of(ck * R + (1 - core) * HALF + b * BM, BM), BM)
            part[rows, :] = term(rows).astype(BF)
            push(
                part.at[rows],
                core_part.at[slot, ck * HALF + b * BM : ck * HALF + (b + 1) * BM],
                core_s.at[ph, ck, b],
                core_r.at[ph, ck, b],
                device(1 - core, y, z, x),
                ("part", ck),
            )
        for b in range(NB):
            rows = pl.ds(pl.multiple_of(ck * R + core * HALF + b * BM, BM), BM)
            value = term(rows)
            other = core_part.at[slot, ck * HALF + b * BM : ck * HALF + (b + 1) * BM]
            wait(other, core_r.at[ph, ck, b])
            part[rows, :] = (value + other[...].astype(F32)).astype(BF)
        for j in range(1, 4):
            to = (x + j) % 4
            first = ck * R + core * HALF + to * QUARTER
            push(
                part.at[pl.ds(pl.multiple_of(first, QUARTER), QUARTER)],
                ring_part.at[slot, j - 1, ck * QUARTER : (ck + 1) * QUARTER],
                ring_s.at[ph, ck, j - 1],
                ring_r.at[ph, ck, j - 1],
                device(core, y, z, to),
                ("part", ck),
            )

    def reduce_finish(ph, ck):
        slot = ph % 2
        summed = part[own_rows(ck), :].astype(F32)
        for j in range(3):
            piece = ring_part.at[slot, j, ck * QUARTER : (ck + 1) * QUARTER]
            wait(piece, ring_r.at[ph, ck, j])
            summed = summed + piece[...].astype(F32)
        return summed

    def gather_send(n, ck, buffer):
        rows = own_rows(ck)
        for j in range(1, 4):
            push(
                buffer.at[rows],
                buffer.at[rows],
                gx_s.at[n, ck, j - 1],
                gx_r.at[n, ck, j - 1],
                device(core, y, z, (x + j) % 4),
            )
        push(
            buffer.at[rows],
            buffer.at[rows],
            gc_s.at[n, ck, 0],
            gc_r.at[n, ck, 0],
            device(1 - core, y, z, x),
        )

    def gather_pass(n, ck, buffer):
        for j in range(1, 4):
            first = ck * R + core * HALF + ((x - j + 4) % 4) * QUARTER
            piece = buffer.at[pl.ds(pl.multiple_of(first, QUARTER), QUARTER)]
            wait(piece, gx_r.at[n, ck, j - 1])
            push(
                piece,
                piece,
                gc_s.at[n, ck, j],
                gc_r.at[n, ck, j],
                device(1 - core, y, z, x),
            )

    def gather_finish(n, ck, buffer):
        for j in range(4):
            wait(buffer.at[own_rows(ck)], gc_r.at[n, ck, j])

    def out_rows(seq, ck, c_, x_):
        first = seq * LEN + ck * R + c_ * HALF + x_ * QUARTER
        return ends_out.at[pl.ds(pl.multiple_of(first, QUARTER), QUARTER)]

    def give_out(n, ck):
        src = ends_low.at[n, ck * QUARTER : (ck + 1) * QUARTER]
        dst = out_rows(z_hi, ck, core, x)
        recv = out_r.at[ck, core * 4 + x]
        target = 1 - n
        for j in range(4):
            where, send = device(target, y, z, (x + j) % 4), out_s.at[n, ck, j]
            if j == 0:
                push_or_keep(core == target, src, dst, send, recv, where)
            else:
                push(src, dst, send, recv, where)

    def out_arrived(ck):
        for c_ in range(2):
            for x_ in range(4):
                wait(out_rows(z_hi, ck, c_, x_), out_r.at[ck, c_ * 4 + x_])

    def across_copy(n, ck):
        first = z_hi * LEN + ck * R
        rows = ends_out.at[pl.ds(pl.multiple_of(first, R), R)]
        return pltpu.make_async_remote_copy(
            src_ref=rows,
            dst_ref=rows,
            send_sem=across_s.at[ck],
            recv_sem=across_r.at[ck],
            device_id=device(1 - n, y, (z + 2) % 4, x),
            device_id_type=MESH,
        )

    def across(n, ck):
        @pl.when(core == 1 - n)
        def _():
            out_arrived(ck)
            across_copy(n, ck).start()

    def across_end(n, ck):
        @pl.when(core == 1 - n)
        def _():
            across_copy(n, ck).wait()

    def direct_first(n, ck):
        push(
            ends_low.at[n, ck * QUARTER : (ck + 1) * QUARTER],
            out_rows(z_hi, ck, core, x),
            direct_s.at[0],
            direct_r.at[core],
            device(1 - n, y, (z + 2) % 4, x),
        )

    def direct_copy(n, ck, c_, j):
        rows = out_rows(1 - z_hi, ck, c_, x)
        return pltpu.make_async_remote_copy(
            src_ref=rows,
            dst_ref=rows,
            send_sem=direct2_s.at[c_, j - 1],
            recv_sem=direct2_r.at[c_, j - 1],
            device_id=device(1 - n, y, z, (x + j) % 4),
            device_id_type=MESH,
        )

    def direct_second(n, ck):
        @pl.when(core == 1 - n)
        def _():
            for c_ in range(2):
                wait(out_rows(1 - z_hi, ck, c_, x), direct_r.at[c_])
                for j in range(1, 4):
                    direct_copy(n, ck, c_, j).start()

    def direct_end(n, ck):
        @pl.when(core == 1 - n)
        def _():
            out_arrived(ck)
            for c_ in range(2):
                for j in range(1, 4):
                    direct_copy(n, ck, c_, j).wait()

    def weight_grads(l, p):
        for i in range(4):
            cols = slice(i * BQ, (i + 1) * BQ)
            if p == 0:
                pieces = [
                    ((384, NIN), dot(xhat[l, :, cols], d_joined[:, 384:NIN], 0, 0)),
                    ((NIN, NALL), dot(grads_in[l, :, cols], joined[l], 0, 0)),
                ]
            else:
                pieces = [((0, 384), dot(xhat[l, :, cols], d_joined[:, 0:384], 0, 0))]
            for (first, last), piece in pieces:
                low = piece.astype(BF)
                for k in range(2):
                    for half in range(2):
                        rows = slice((k * 2 + half) * 64, (k * 2 + half) * 64 + 64)
                        w_grad[i, k, half, :, first:last] = low[rows]

    def plane_first(l, p):
        cols = slice(*G_PARTS[p])
        for k in range(2):
            z_ = 2 * core + k
            slot = (z_ - z + 3) % 4
            src, send = w_grad.at[:, k, 0, :, cols], p1a_s.at[l, p, k]
            other = z_ != z

            @pl.when(other)
            def _(src=src, send=send, z_=z_, slot=slot):
                pltpu.make_async_remote_copy(
                    src_ref=src,
                    dst_ref=plane_a.at[l, slot, :, :, cols],
                    send_sem=send,
                    recv_sem=p1a_r.at[l, p, slot],
                    device_id=device(core, y, z_, x),
                    device_id_type=MESH,
                ).start()

            drains.setdefault("grad", []).append((other, src, send))
        for j in range(1, 4):
            to = (y + j) % 4
            push(
                w_grad.at[to, :, 1, :, cols],
                plane_b.at[l, j - 1, :, :, cols],
                p1b_s.at[l, p, j - 1],
                p1b_r.at[l, p, j - 1],
                device(core, to, z, x),
                "grad",
            )

    def plane_second(l, p):
        cols = slice(*G_PARTS[p])

        @pl.when(forwarder)
        def _():
            for j in range(3):
                wait(plane_a.at[l, j, :, :, cols], p1a_r.at[l, p, j])

            def one(y_, carry):
                summed = w_grad[y_, z_lo, 0, :, cols].astype(F32)
                for j in range(3):
                    summed = summed + plane_a[l, j, y_, :, cols].astype(F32)
                sum_a[l, y_, :, cols] = summed.astype(BF)
                return carry

            lax.fori_loop(0, 4, one, 0)
            for j in range(4):
                to = (y + j) % 4
                src, dst = sum_a.at[l, to, :, cols], own_a.at[y, :, cols]
                copy = pltpu.make_async_remote_copy(
                    src_ref=src,
                    dst_ref=dst,
                    send_sem=p2a_s.at[l, p, j],
                    recv_sem=p2a_r.at[p, y],
                    device_id=device(l, to, z, x),
                    device_id_type=MESH,
                )
                if j == 0:
                    pl.when(core == l)(pltpu.make_async_copy(src, dst, p2a_r.at[p, y]).start)
                    pl.when(core != l)(copy.start)
                else:
                    copy.start()

        for j in range(3):
            wait(plane_b.at[l, j, :, :, cols], p1b_r.at[l, p, j])
        for k in range(2):
            summed = w_grad[y, k, 1, :, cols].astype(F32)
            for j in range(3):
                summed = summed + plane_b[l, j, k, :, cols].astype(F32)
            sum_b[l, k, :, cols] = summed.astype(BF)
            z_ = 2 * core + k
            push_or_keep(
                jnp.logical_and(core == l, z_ == z),
                sum_b.at[l, k, :, cols],
                own_b.at[z, :, cols],
                p2b_s.at[l, p, k],
                p2b_r.at[p, z],
                device(l, y, z_, x),
            )

    def drain_plane():
        @pl.when(forwarder)
        def _():
            for l in range(2):
                for p, cols in enumerate(G_PARTS):
                    src = sum_a.at[l, 0, :, slice(*cols)]
                    for j in range(4):
                        ended = functools.partial(wait, src, p2a_s.at[l, p, j])
                        if j == 0:
                            pl.when(core != l)(ended)
                        else:
                            ended()

    def send_small(l):
        message[l] = jnp.zeros((8, 256), F32)
        column_sum = jnp.zeros((1, NIN), F32)
        out_sum = jnp.zeros((1, D), F32)

        def one(i, carry):
            rows = pl.ds(pl.multiple_of(i * 128, 128), 128)
            a, b = carry
            a = a + jnp.sum(d_joined[rows, :].astype(F32), axis=0, keepdims=True)
            b = b + jnp.sum(grads_in[l, rows, :].astype(F32), axis=0, keepdims=True)
            return a, b

        column_sum, out_sum = lax.fori_loop(0, LEN // 128, one, (column_sum, out_sum))
        for n in range(7):
            message[l, n // 2 : n // 2 + 1, (n % 2) * 128 : (n % 2) * 128 + 128] = column_sum[
                :, n * 128 : (n + 1) * 128
            ]
        for n in range(4):
            message[l, 4 + n : 5 + n, :] = out_sum[:, n * 256 : (n + 1) * 256]
        here = y * 4 + z
        for y_ in range(4):
            for k in range(2):
                z_ = 2 * core + k
                own = jnp.logical_and(core == l, jnp.logical_and(y_ == y, z_ == z))
                push_or_keep(
                    own,
                    message.at[l],
                    messages.at[here],
                    msg_s.at[l, y_ * 2 + k],
                    msg_r.at[here],
                    device(l, y_, z_, x),
                )

    def after_first_layer(ck):
        rows = own_rows(ck)
        result = x_in[rows, :].astype(F32) + reduce_finish(0, ck) + out_row[0]
        low = result.astype(BF)
        y_mid[ck * QUARTER : (ck + 1) * QUARTER, :] = low
        xhat[1, rows, :] = standardize(low.astype(F32))[0].astype(BF)
        gather_send(0, ck, xhat.at[1])

    def after_second_layer(ck):
        mid = slice(ck * QUARTER, (ck + 1) * QUARTER)
        result = y_mid[mid, :].astype(F32) + reduce_finish(1, ck) + out_row[1]
        ends_low[0, mid, :] = result.astype(BF)

    def through_norm(stream, grad, e):
        scaled, inverse = standardize(stream)
        return grad + inverse * (
            e
            - jnp.mean(e, axis=-1, keepdims=True)
            - scaled * jnp.mean(e * scaled, axis=-1, keepdims=True)
        )

    def input_grad_middle(ck):
        mid = slice(ck * QUARTER, (ck + 1) * QUARTER)
        rows = own_rows(ck)
        e = reduce_finish(2, ck)
        moved = through_norm(y_mid[mid, :].astype(F32), grads_in[1, rows, :].astype(F32), e)
        grads_in[0, rows, :] = moved.astype(BF)
        gather_send(1, ck, grads_in.at[0])

    def input_grad_first(ck):
        mid = slice(ck * QUARTER, (ck + 1) * QUARTER)
        rows = own_rows(ck)
        e = reduce_finish(3, ck)
        moved = through_norm(x_in[rows, :].astype(F32), grads_in[0, rows, :].astype(F32), e)
        ends_low[1, mid, :] = moved.astype(BF)

    forward(0, 0)
    gather_rest(0, 1)
    reduce_send(0, 0, functools.partial(branch, 0))
    gather_second(1, 0)
    forward(0, 1)
    after_first_layer(0)
    reduce_send(0, 1, functools.partial(branch, 0))
    gather_pass(0, 0, xhat.at[1])
    after_first_layer(1)
    gather_finish(0, 0, xhat.at[1])
    gather_rest(1, 0)
    forward(1, 0)
    reduce_send(1, 0, functools.partial(branch, 1))
    gather_pass(0, 1, xhat.at[1])
    gather_finish(0, 1, xhat.at[1])
    forward(1, 1)
    reduce_send(1, 1, functools.partial(branch, 1))

    wait(x_in, swap_s)
    backward_first(1, 1)
    backward_second(1, 1)
    after_second_layer(0)
    after_second_layer(1)
    reduce_send(2, 1, functools.partial(norm_grad, 1))
    backward_first(1, 0)
    backward_second(1, 0)
    input_grad_middle(1)
    reduce_send(2, 0, functools.partial(norm_grad, 1))
    weight_grads(1, 0)
    plane_first(1, 0)
    gather_pass(1, 1, grads_in.at[0])
    input_grad_middle(0)
    give_out(0, 1)
    give_out(0, 0)
    weight_grads(1, 1)
    plane_first(1, 1)
    send_small(1)
    gather_finish(1, 1, grads_in.at[0])

    backward_first(0, 1)
    backward_second(0, 1)
    gather_pass(1, 0, grads_in.at[0])
    reduce_send(3, 1, functools.partial(norm_grad, 0))
    gather_finish(1, 0, grads_in.at[0])
    backward_first(0, 0)
    plane_second(1, 0)
    plane_second(1, 1)
    drain("grad")
    weight_grads(0, 0)
    plane_first(0, 0)
    across(0, 1)
    across(0, 0)
    backward_second(0, 0)
    input_grad_first(1)
    give_out(1, 1)
    reduce_send(3, 0, functools.partial(norm_grad, 0))
    weight_grads(0, 1)
    plane_first(0, 1)
    input_grad_first(0)
    direct_first(1, 0)
    give_out(1, 0)
    send_small(0)
    across(1, 1)
    plane_second(0, 0)
    direct_second(1, 0)
    plane_second(0, 1)

    for k in range(16):
        wait(messages.at[k], msg_r.at[k])
    summed = messages[0]
    for k in range(1, 16):
        summed = summed + messages[k]
    for n in range(4):
        bias_total[:, n * 256 : (n + 1) * 256] = summed[n : n + 1, :]
        g_out_b[:, n * 256 : (n + 1) * 256] = summed[4 + n : 5 + n, :]
    for k in range(4):
        for p, cols in enumerate(G_PARTS):
            wait(own_a.at[k, :, slice(*cols)], p2a_r.at[p, k])
            wait(own_b.at[k, :, slice(*cols)], p2b_r.at[p, k])
    total[0:64, :] = (
        own_a[0].astype(F32) + own_a[1].astype(F32) + own_a[2].astype(F32) + own_a[3].astype(F32)
    )
    total[64:128, :] = (
        own_b[0].astype(F32) + own_b[1].astype(F32) + own_b[2].astype(F32) + own_b[3].astype(F32)
    )
    by_gain = [jnp.zeros((128, 128), F32) for _ in range(2)]
    by_offset = [jnp.zeros((128, 128), F32) for _ in range(2)]
    for n in range(7):
        tile, k, _ = raw_tile(n)
        cols = slice(n * 128, (n + 1) * 128)
        raw = total[:, cols]
        bias = bias_total[:, cols]
        grad = raw * gain_cols[k] + offset_cols[k] * bias
        by_gain[k] = by_gain[k] + tile * raw
        by_offset[k] = by_offset[k] + tile * bias
        if n < 3:
            g_qkv[n] = grad
            g_qkv_b[n] = bias
        else:
            g_up[:, (n - 3) * 128 : (n - 2) * 128] = grad
            g_up_b[:, (n - 3) * 128 : (n - 2) * 128] = bias
    g_dense[...] = total[:, NIN : NIN + 128].T
    g_down[...] = total[:, NIN + 128 : NALL].T
    ln_own[...] = jnp.zeros_like(ln_own)
    for n, value in enumerate(by_gain + by_offset):
        ln_own[n : n + 1, :] = jnp.sum(value.T, axis=0, keepdims=True)
    for j in range(1, 4):
        push(
            ln_own,
            ln_ring.at[j - 1],
            ln1_s.at[j - 1],
            ln1_r.at[j - 1],
            device(core, y, z, (x + j) % 4),
        )
    for j in range(3):
        wait(ln_ring.at[j], ln1_r.at[j])
    here = y * 4 + z
    ln_plane[here] = ln_own[...] + ln_ring[0] + ln_ring[1] + ln_ring[2]
    for dy in range(4):
        for dz in range(4):
            if (dy, dz) != (0, 0):
                push(
                    ln_plane.at[here],
                    ln_plane.at[here],
                    ln2_s.at[dy * 4 + dz - 1],
                    ln2_r.at[here],
                    device(core, (y + dy) % 4, (z + dz) % 4, x),
                )
    for dy in range(4):
        for dz in range(4):
            if (dy, dz) != (0, 0):
                there = ((y + dy) % 4) * 4 + (z + dz) % 4
                wait(ln_plane.at[there], ln2_r.at[there])
    for dp_ in range(8):
        first = (dp_ // 2) * 4 + dp_ % 2
        both = ln_plane[first] + ln_plane[first + 2]
        cols = slice(dp_ * 128, (dp_ + 1) * 128)
        g_gains[:, cols] = both[0:2, :]
        g_offsets[:, cols] = both[2:4, :]

    across_end(0, 0)
    across_end(0, 1)
    across_end(1, 1)
    direct_end(1, 0)
    drain("grad")
    for ck in range(NCH):
        drain(("part", ck))
    drain("end")
    drain_first()
    drain_second()
    drain_extra()
    drain_plane()


def settle(*refs):
    count = (len(refs) - 1) // 2
    sources, targets, sem = refs[:count], refs[count : 2 * count], refs[-1]
    copies = []
    rows = sources[0].shape[0] // 8
    for k in range(8):
        piece = pl.ds(k * rows, rows)
        copies.append(
            pltpu.make_async_copy(sources[0].at[piece], targets[0].at[piece], sem.at[count + k])
        )
    for n in range(1, count):
        copies.append(pltpu.make_async_copy(sources[n], targets[n], sem.at[n]))
    for copy in copies:
        copy.start()
    for copy in copies:
        copy.wait()


def body(ends_in, ln_gains, ln_biases, qkv_w, qkv_bias, dense_w, up_w, up_bias, down_w, out_bias):
    cosine, sine = rotary_tables()
    vmem = pl.BlockSpec(memory_space=pltpu.VMEM)
    anywhere = pl.BlockSpec(memory_space=pl.ANY)

    def shape(*dims):
        return jax.ShapeDtypeStruct(dims, F32)

    def sems(*dims):
        return pltpu.SemaphoreType.DMA(dims)

    outs = pl.pallas_call(
        kernel,
        out_shape=[
            jax.ShapeDtypeStruct((2 * LEN, D), BF),
            shape(2, D),
            shape(2, D),
            shape(3, 128, 128),
            shape(3, 1, 128),
            shape(128, 128),
            shape(128, 512),
            shape(1, 512),
            shape(512, 128),
            shape(1, D),
        ],
        in_specs=[anywhere] + [vmem] * 11,
        out_specs=[anywhere] + [vmem] * 9,
        scratch_shapes=[
            pltpu.VMEM((128, NALL), BF),
            pltpu.VMEM((8, 256), F32),
            pltpu.VMEM((2, 8, 8, 256), F32),
            pltpu.VMEM((2, 1, 1024), F32),
            pltpu.VMEM((2, 1, 1024), F32),
            pltpu.VMEM((2, D, NALL), BF),
            pltpu.VMEM((LEN, D), BF),
            pltpu.VMEM((2, LEN, D), BF),
            pltpu.VMEM((2, LEN, D), BF),
            pltpu.VMEM((LEN // 8, D), BF),
            pltpu.VMEM((2, LEN, NOUT), BF),
            pltpu.VMEM((2, LEN, 512), BF),
            pltpu.VMEM((2, LEN, 128), BF),
            pltpu.VMEM((2, LEN, 128), BF),
            pltpu.VMEM((2, LEN, 128), BF),
            pltpu.VMEM((2, 128, LEN), BF),
            pltpu.VMEM((2, 128, LEN), BF),
            pltpu.VMEM((2, 10, BQ, 2 * BQ), BF),
            pltpu.VMEM((2, LEN // BQ, 2 * BQ), F32),
            pltpu.VMEM((2, 128, LEN), F32),
            pltpu.VMEM((LEN, 2 * BQ), F32),
            pltpu.VMEM((LEN, 128), BF),
            pltpu.VMEM((LEN, NIN), BF),
            pltpu.VMEM((LEN, 128), F32),
            pltpu.VMEM((LEN, 128), F32),
            pltpu.VMEM((LEN, D), BF),
            pltpu.VMEM((2, LEN // 2, D), BF),
            pltpu.VMEM((2, 3, LEN // 8, D), BF),
            pltpu.VMEM((2, LEN // 8, D), BF),
            pltpu.VMEM((4, 2, 2, 64, NALL), BF),
            pltpu.VMEM((2, 3, 4, 64, NALL), BF),
            pltpu.VMEM((2, 3, 2, 64, NALL), BF),
            pltpu.VMEM((2, 4, 64, NALL), BF),
            pltpu.VMEM((2, 2, 64, NALL), BF),
            pltpu.VMEM((4, 64, NALL), BF),
            pltpu.VMEM((4, 64, NALL), BF),
            pltpu.VMEM((128, NALL), F32),
            pltpu.VMEM((2, 8, 256), F32),
            pltpu.VMEM((16, 8, 256), F32),
            pltpu.VMEM((1, 1024), F32),
            pltpu.VMEM((8, 128), F32),
            pltpu.VMEM((3, 8, 128), F32),
            pltpu.VMEM((16, 8, 128), F32),
            pltpu.SemaphoreType.DMA,
            pltpu.SemaphoreType.DMA,
            pltpu.SemaphoreType.DMA,
            sems(2, 2, 4),
            sems(2, 2, 2, 8),
            sems(2, 2, 4, 3),
            sems(2, 2, 2, 3),
            sems(16),
            sems(2, 8),
            sems(4, NCH, NB),
            sems(4, NCH, NB),
            sems(4, NCH, 3),
            sems(4, NCH, 3),
            sems(2, NCH, 3),
            sems(2, NCH, 3),
            sems(2, NCH, 4),
            sems(2, NCH, 4),
            sems(2, NCH, 4),
            sems(NCH, 8),
            sems(NCH),
            sems(NCH),
            sems(1),
            sems(2),
            sems(2, 3),
            sems(2, 3),
            sems(2, 8),
            sems(16),
            sems(2, 2, 2),
            sems(2, 2, 3),
            sems(2, 2, 3),
            sems(2, 2, 3),
            sems(2, 2, 4),
            sems(2, 4),
            sems(2, 2, 2),
            sems(2, 4),
            sems(3),
            sems(3),
            sems(15),
            sems(16),
        ],
        compiler_params=pltpu.CompilerParams(
            collective_id=0, has_side_effects=True, vmem_limit_bytes=63 * 2**20
        ),
        cost_estimate=pl.CostEstimate(
            flops=22 * 10**9, bytes_accessed=20 * 10**6, transcendentals=4 * 10**6
        ),
    )(
        ends_in[0],
        qkv_w[0],
        dense_w[0],
        up_w[0],
        down_w[0],
        ln_gains[0],
        ln_biases[0],
        jnp.transpose(qkv_bias, (1, 0, 2)),
        up_bias,
        out_bias,
        jnp.asarray(cosine),
        jnp.asarray(sine),
    )
    outs = pl.pallas_call(
        settle,
        out_shape=[jax.ShapeDtypeStruct(out.shape, out.dtype) for out in outs],
        in_specs=[anywhere] * len(outs),
        out_specs=[anywhere] * len(outs),
        scratch_shapes=[sems(len(outs) + 8)],
        cost_estimate=pl.CostEstimate(flops=0, bytes_accessed=10 * 10**6, transcendentals=0),
    )(*outs)
    out, gains, offsets, d_qkv, d_qkv_b, d_dense, d_up, d_up_b, d_down, d_out_b = outs
    return (
        out[None],
        gains[None],
        offsets[None],
        d_qkv[None],
        jnp.transpose(d_qkv_b, (1, 0, 2)),
        d_dense[None],
        d_up[None],
        d_up_b,
        d_down[None],
        d_out_b,
    )


def solution(mesh):
    in_specs = (
        P("section", "dp", None),
        P("section", None, None),
        P("section", None, None),
        P("section", None, "dp", "tensor"),
        P("section", None, "tensor"),
        P("section", "tensor", "dp"),
        P("section", "dp", "tensor"),
        P("section", "tensor"),
        P("section", "tensor", "dp"),
        P("section", None),
    )
    out_specs = (
        P("section", "dp", None),
        P("section", None, None),
        P("section", None, None),
        P("section", None, "dp", "tensor"),
        P("section", None, "tensor"),
        P("section", "tensor", "dp"),
        P("section", "dp", "tensor"),
        P("section", "tensor"),
        P("section", "tensor", "dp"),
        P("section", None),
    )
    return jax.shard_map(body, mesh=mesh, in_specs=in_specs, out_specs=out_specs, check_vma=False)
```

```python
import functools

import jax
import jax.numpy as jnp
import numpy as np
from jax import lax
from jax.experimental import pallas as pl
from jax.experimental.pallas import tpu as pltpu
from jax.sharding import PartitionSpec as P

MESH = pl.DeviceIdType.MESH
BF = jnp.bfloat16
F32 = jnp.float32

D = 1024
LEN = 1024
HD = 64
ROT = 16
NIN = 896
NOUT = 640
NALL = NIN + NOUT
BQ = 256
NCH = 2
R = LEN // NCH
HALF = R // 2
QUARTER = R // 8
BM = min(256, HALF)
NB = HALF // BM
W_PARTS = (((0, NIN), (NIN, NALL)), ((0, NALL),))
G_PARTS = ((384, NALL), (0, 384))
ROWS_A = 32
ROWS_B = 128 - ROWS_A


def dot(a, b, ca, cb):
    return lax.dot_general(a, b, (((ca,), (cb,)), ((), ())), preferred_element_type=F32)


def rotary_tables():
    position = np.arange(LEN, dtype=np.float32)[:, None]
    exponent = np.arange(ROT // 2, dtype=np.float32) * np.float32(2.0) / np.float32(ROT)
    angles = (position * np.float32(10000.0) ** (-exponent)).astype(np.float32)
    cosine = np.ones((LEN, 2 * HD), np.float32)
    sine = np.zeros((LEN, 2 * HD), np.float32)
    for first in (0, 8, HD, HD + 8):
        cosine[:, first : first + 8] = np.cos(angles)
        sine[:, first : first + 8] = np.sin(angles)
    return cosine, sine


def lanes_of_head(shape):
    return lax.broadcasted_iota(jnp.int32, shape, 1) % HD


def turn(value, cosine, sine):
    lane = lanes_of_head(value.shape)
    partner = jnp.where(lane < 8, -pltpu.roll(value, 120, 1), pltpu.roll(value, 8, 1))
    return value * cosine + partner * sine


def turn_back(grad, cosine, sine):
    lane = lanes_of_head(grad.shape)
    moved = grad * sine
    partner = jnp.where(
        lane < 8, pltpu.roll(moved, 120, 1), jnp.where(lane < 16, -pltpu.roll(moved, 8, 1), 0.0)
    )
    return grad * cosine + partner


def gelu_and_slope(hidden):
    bell = jnp.exp(-0.5 * hidden * hidden)
    size = 1.0 + (0.3275911 * 0.7071067811865476) * jnp.abs(hidden)
    t = pltpu.reciprocal(size, approx=True)
    t = t * (2.0 - size * t)
    series = t * (
        0.254829592 * 0.5
        + t
        * (
            -0.284496736 * 0.5
            + t * (1.421413741 * 0.5 + t * (-1.453152027 * 0.5 + t * (1.061405429 * 0.5)))
        )
    )
    tail = series * bell
    below = jnp.where(hidden >= 0.0, 1.0 - tail, tail)
    return hidden * below, below + hidden * bell * 0.3989422804014327


def standardize(value):
    center = jnp.mean(value, axis=-1, keepdims=True)
    centred = value - center
    inverse = lax.rsqrt(jnp.mean(centred * centred, axis=-1, keepdims=True) + 1e-05)
    return centred * inverse, inverse


def stack_heads(value):
    lane = lax.broadcasted_iota(jnp.int32, value.shape, 1)
    wide = value.astype(F32)
    return jnp.concatenate(
        [jnp.where(lane < HD, wide, 0.0), jnp.where(lane >= HD, wide, 0.0)], axis=0
    ).astype(BF)


def split_heads(value):
    half = value.shape[1] // 2
    return jnp.concatenate([value[:HD, :half], value[HD:, half:]], axis=0)


def pair(i, j):
    return i * (i + 1) // 2 + j


def kernel(
    ends,
    qkv,
    dense,
    up,
    down,
    gains,
    offsets,
    qkv_b,
    up_b,
    out_b,
    cosine,
    sine,
    ends_out,
    g_gains,
    g_offsets,
    g_qkv,
    g_qkv_b,
    g_dense,
    g_up,
    g_up_b,
    g_down,
    g_out_b,
    shard,
    extra,
    extras,
    bias_row,
    out_row,
    weights,
    x_in,
    grads_in,
    xhat,
    y_mid,
    x_own,
    joined,
    slope,
    queries,
    keys,
    values,
    keys_t,
    values_t,
    soft,
    soft_scale,
    context_t,
    scores,
    d_context,
    d_joined,
    core_part,
    ring_part,
    ends_low,
    w_grad,
    plane_a,
    plane_b,
    sum_a,
    sum_b,
    own_a,
    own_b,
    total,
    message,
    messages,
    small,
    small_ring,
    small_sum,
    small_far,
    local_sem,
    swap_s,
    swap_r,
    w1_s,
    w_r,
    w2a_s,
    w2b_s,
    extra_s,
    extra_r,
    core_s,
    core_r,
    ring_s,
    ring_r,
    gx_s,
    gx_r,
    gc_s,
    gc_r,
    out_s,
    out_r,
    across_s,
    across_r,
    direct_s,
    direct_r,
    direct2_s,
    direct2_r,
    msg_s,
    msg_r,
    p1a_s,
    p1a_r,
    p1b_s,
    p1b_r,
    p2a_s,
    p2a_r,
    p2b_s,
    p2b_r,
    ln1_s,
    ln1_r,
    ln2_s,
    ln2_r,
):
    part = x_in
    core = lax.axis_index("section")
    dp = lax.axis_index("dp")
    t = lax.axis_index("tensor")
    y, z_lo = dp // 2, dp % 2
    z_hi, x = t // 4, t % 4
    z = 2 * z_hi + z_lo
    forwarder = core == z_hi

    def device(c_, y_, z_, x_):
        return {"section": c_, "dp": y_ * 2 + z_ % 2, "tensor": (z_ // 2) * 4 + x_}

    drains = {}

    def wait(ref, sem):
        pltpu.make_async_copy(ref, ref, sem).wait()

    def push(src, dst, send, recv, where, tag="end"):
        pltpu.make_async_remote_copy(
            src_ref=src, dst_ref=dst, send_sem=send, recv_sem=recv, device_id=where, device_id_type=MESH
        ).start()
        drains.setdefault(tag, []).append((None, src, send))

    def push_or_keep(own, src, dst, send, recv, where):
        other = jnp.logical_not(own)

        @pl.when(own)
        def _():
            pltpu.make_async_copy(src, dst, recv).start()

        @pl.when(other)
        def _():
            pltpu.make_async_remote_copy(
                src_ref=src,
                dst_ref=dst,
                send_sem=send,
                recv_sem=recv,
                device_id=where,
                device_id_type=MESH,
            ).start()

        drains.setdefault("end", []).append((other, src, send))

    def drain(tag):
        for condition, src, send in drains.pop(tag, []):
            if condition is None:
                wait(src, send)
            else:
                pl.when(condition)(functools.partial(wait, src, send))

    barrier = pltpu.get_barrier_semaphore()
    for dy in range(4):
        for dz in range(4):
            for c_ in range(2):
                if (dy, dz, c_) == (0, 0, 0):
                    continue
                pl.semaphore_signal(
                    barrier,
                    inc=1,
                    device_id=device((core + c_) % 2, (y + dy) % 4, (z + dz) % 4, x),
                    device_id_type=MESH,
                )
    for j in range(1, 4):
        pl.semaphore_signal(
            barrier, inc=1, device_id=device(core, y, z, (x + j) % 4), device_id_type=MESH
        )

    block = pl.ds(pl.multiple_of(dp * 128, 128), 128)

    def column(row):
        return jnp.broadcast_to(row, (128, 128)).T

    gain_cols = [column(gains[k : k + 1, block]) for k in range(2)]
    offset_cols = [column(offsets[k : k + 1, block]) for k in range(2)]

    def raw_tile(n):
        if n < 3:
            return qkv[n].astype(F32), 0, qkv_b[n]
        cols = slice((n - 3) * 128, (n - 2) * 128)
        return up[:, cols].astype(F32), 1, up_b[:, cols]

    extra[...] = jnp.zeros_like(extra)
    message[...] = jnp.zeros_like(message)
    for n in range(7):
        tile, k, bias = raw_tile(n)
        shard[:, n * 128 : (n + 1) * 128] = (tile * gain_cols[k]).astype(BF)
        added = jnp.sum(tile * offset_cols[k], axis=0, keepdims=True) + 0.125 * bias
        extra[n // 2 : n // 2 + 1, (n % 2) * 128 : (n % 2) * 128 + 128] = added
    for n in range(4):
        extra[4 + n : 5 + n, :] = 0.125 * out_b[:, n * 256 : (n + 1) * 256]
    shard[:, NIN : NIN + 128] = dense[...].T
    shard[:, NIN + 128 : NALL] = down[...].T

    pl.semaphore_wait(barrier, 34)

    mine = ends.at[pl.ds(pl.multiple_of(z_hi * LEN, LEN), LEN)]
    for c_, buffer in ((0, x_in), (1, grads_in.at[1])):

        @pl.when(core == c_)
        def _(buffer=buffer):
            pltpu.make_async_copy(mine, buffer, local_sem).start()
            pltpu.make_async_remote_copy(
                src_ref=mine,
                dst_ref=buffer,
                send_sem=swap_s,
                recv_sem=swap_r,
                device_id=device(1 - core, y, z, x),
                device_id_type=MESH,
            ).start()

    def w_rows(l, p, dp_, half):
        rows = pl.ds(pl.multiple_of(dp_ * 128 + half * 64, 64), 64)
        return weights.at[l, rows, slice(*W_PARTS[l][p])]

    def gather_first(l):
        @pl.when(core == l)
        def _():
            for p, cols in enumerate(W_PARTS[l]):
                for half in range(2):
                    src = shard.at[half * 64 : half * 64 + 64, slice(*cols)]
                    dst = w_rows(l, p, dp, half)
                    recv = w_r.at[half, l, p, dp]

                    @pl.when(forwarder)
                    def _(src=src, dst=dst, recv=recv):
                        pltpu.make_async_copy(src, dst, recv).start()

                    for j in range(4):
                        if half == 0:
                            where = device(z_hi, (y + j) % 4, z, x)
                        else:
                            where = device(z_hi, y, (z + j) % 4, x)
                        copy = pltpu.make_async_remote_copy(
                            src_ref=src,
                            dst_ref=dst,
                            send_sem=w1_s.at[p, half, j],
                            recv_sem=recv,
                            device_id=where,
                            device_id_type=MESH,
                        )
                        if j == 0:
                            pl.when(jnp.logical_not(forwarder))(copy.start)
                        else:
                            copy.start()

    def drain_first():
        for l in range(2):

            @pl.when(core == l)
            def _(l=l):
                for p, cols in enumerate(W_PARTS[l]):
                    src = shard.at[0:64, slice(*cols)]
                    for half in range(2):
                        for j in range(4):
                            ended = functools.partial(wait, src, w1_s.at[p, half, j])
                            if j == 0:
                                pl.when(jnp.logical_not(forwarder))(ended)
                            else:
                                ended()

    def gather_second(l, p):
        for k in range(2):
            block_b = w_rows(l, p, y * 2 + k, 1)
            wait(block_b, w_r.at[1, l, p, y * 2 + k])
            for j in range(1, 4):
                push(
                    block_b,
                    block_b,
                    w2b_s.at[l, p, k, j - 1],
                    w_r.at[1, l, p, y * 2 + k],
                    device(core, (y + j) % 4, z, x),
                )

        @pl.when(forwarder)
        def _():
            for y_ in range(4):
                dp_ = y_ * 2 + z_lo
                block_a = w_rows(l, p, dp_, 0)
                wait(block_a, w_r.at[0, l, p, dp_])
                for j in range(1, 4):
                    pltpu.make_async_remote_copy(
                        src_ref=block_a,
                        dst_ref=block_a,
                        send_sem=w2a_s.at[l, p, y_, j - 1],
                        recv_sem=w_r.at[0, l, p, dp_],
                        device_id=device(core, y, (z + j) % 4, x),
                        device_id_type=MESH,
                    ).start()

    def drain_second():
        @pl.when(forwarder)
        def _():
            for l in range(2):
                for p in range(len(W_PARTS[l])):
                    for y_ in range(4):
                        for j in range(3):
                            wait(w_rows(l, p, 0, 0), w2a_s.at[l, p, y_, j])

    def gather_rest(l, p):
        for j in range(1, 4):
            for k in range(2):
                dp_ = ((y + j) % 4) * 2 + k
                wait(w_rows(l, p, dp_, 1), w_r.at[1, l, p, dp_])
        for y_ in range(4):
            dp_ = y_ * 2 + 1 - z_lo
            wait(w_rows(l, p, dp_, 0), w_r.at[0, l, p, dp_])

            @pl.when(jnp.logical_not(forwarder))
            def _(dp_=y_ * 2 + z_lo):
                wait(w_rows(l, p, dp_, 0), w_r.at[0, l, p, dp_])

        if p > 0:
            return
        for dp_ in range(8):
            wait(extras.at[l, dp_], extra_r.at[l, dp_])
        summed = extras[l, 0]
        for dp_ in range(1, 8):
            summed = summed + extras[l, dp_]
        for n in range(4):
            bias_row[l, :, n * 256 : (n + 1) * 256] = summed[n : n + 1, :]
            out_row[l, :, n * 256 : (n + 1) * 256] = summed[4 + n : 5 + n, :]

    gather_first(0)
    for l in range(2):

        @pl.when(core == l)
        def _(l=l):
            for dy in range(4):
                for dz in range(4):
                    where = device(z_hi, (y + dy) % 4, (z + dz) % 4, x)
                    dst = extras.at[l, dp]
                    recv = extra_r.at[l, dp]
                    copy = pltpu.make_async_remote_copy(
                        src_ref=extra,
                        dst_ref=dst,
                        send_sem=extra_s.at[dy * 4 + dz],
                        recv_sem=recv,
                        device_id=where,
                        device_id_type=MESH,
                    )
                    if (dy, dz) == (0, 0):
                        pl.when(forwarder)(pltpu.make_async_copy(extra, dst, recv).start)
                        pl.when(jnp.logical_not(forwarder))(copy.start)
                    else:
                        copy.start()

    def drain_extra():
        for k in range(16):
            if k == 0:
                pl.when(jnp.logical_not(forwarder))(
                    functools.partial(wait, extra, extra_s.at[k])
                )
            else:
                wait(extra, extra_s.at[k])

    wait(x_in, local_sem)
    wait(x_in, swap_r)

    gather_second(0, 0)

    def normalize_rows(i, carry):
        rows = pl.ds(pl.multiple_of(i * 128, 128), 128)
        xhat[0, rows, :] = standardize(x_in[rows, :].astype(F32))[0].astype(BF)
        return carry

    lax.fori_loop(0, LEN // 128, normalize_rows, 0)
    for ck in range(NCH):
        first = ck * R + core * HALF + x * QUARTER
        x_own[ck * QUARTER : (ck + 1) * QUARTER, :] = x_in[
            pl.ds(pl.multiple_of(first, QUARTER), QUARTER), :
        ]
    gather_second(0, 1)
    gather_first(1)
    gather_rest(0, 0)

    def project(l, i):
        rows = pl.ds(pl.multiple_of(i * BQ, BQ), BQ)
        low = xhat[l, rows, :]
        raw = dot(low, weights[l, :, 0:384], 1, 0) + bias_row[l, :, 0:384]
        cos_rows, sin_rows = cosine[rows, :], sine[rows, :]
        q = turn(raw[:, 0:128], cos_rows, sin_rows) * HD**-0.5
        k = turn(raw[:, 128:256], cos_rows, sin_rows)
        v = raw[:, 256:384]
        queries[l, rows, :] = q.astype(BF)
        keys[l, rows, :] = k.astype(BF)
        values[l, rows, :] = v.astype(BF)
        keys_t[l, :, rows] = k.T.astype(BF)
        values_t[:, rows] = v.T.astype(BF)
        hidden = dot(low, weights[l, :, 384:NIN], 1, 0) + bias_row[l, :, 384:NIN]
        act, gradient = gelu_and_slope(hidden)
        joined[l, rows, 128:NOUT] = act.astype(BF)
        slope[l, rows, :] = gradient.astype(BF)

    def attend(l, i):
        rows = slice(i * BQ, (i + 1) * BQ)
        stacked = stack_heads(queries[l, rows, :])
        largest = None
        for j in range(i + 1):
            tile = dot(keys[l, j * BQ : (j + 1) * BQ, :], stacked, 1, 1)
            if j == i:
                key_at = lax.broadcasted_iota(jnp.int32, tile.shape, 0)
                query_at = lax.broadcasted_iota(jnp.int32, tile.shape, 1) % BQ
                tile = jnp.where(key_at <= query_at, tile, -1e30)
            scores[j * BQ : (j + 1) * BQ, :] = tile
            top = jnp.max(tile, axis=0, keepdims=True)
            largest = top if largest is None else jnp.maximum(largest, top)
        summed = jnp.zeros((1, 2 * BQ), F32)
        outcome = jnp.zeros((2 * HD, 2 * BQ), F32)
        for j in range(i + 1):
            terms = jnp.exp(scores[j * BQ : (j + 1) * BQ, :] - largest)
            summed = summed + jnp.sum(terms, axis=0, keepdims=True)
            low = terms.astype(BF)
            soft[l, pair(i, j)] = low
            outcome = outcome + dot(values_t[:, j * BQ : (j + 1) * BQ], low, 1, 0)
        scale = 1.0 / summed
        soft_scale[l, i : i + 1, :] = scale
        context = split_heads(outcome * scale)
        context_t[l, :, rows] = context
        joined[l, rows, 0:128] = context.T.astype(BF)

    def attend_back(l, i):
        rows = slice(i * BQ, (i + 1) * BQ)
        grad_t = d_context[rows, :].astype(F32).T
        scale = soft_scale[l, i : i + 1, :]
        top = grad_t[:HD] * scale[:, :BQ]
        bottom = grad_t[HD:] * scale[:, BQ:]
        context = context_t[l, :, rows]
        delta = jnp.concatenate(
            [
                jnp.sum(context[:HD] * top, axis=0, keepdims=True),
                jnp.sum(context[HD:] * bottom, axis=0, keepdims=True),
            ],
            axis=1,
        )
        blank = jnp.zeros_like(top)
        spread_wide = jnp.concatenate(
            [jnp.concatenate([top, blank], axis=1), jnp.concatenate([blank, bottom], axis=1)], axis=0
        )
        spread_t = spread_wide.astype(BF)
        spread = spread_wide.T.astype(BF)
        stacked = stack_heads(queries[l, rows, :])
        d_query_t = jnp.zeros((2 * HD, 2 * BQ), F32)
        for j in range(i + 1):
            cols = slice(j * BQ, (j + 1) * BQ)
            terms = soft[l, pair(i, j)]
            d_terms = dot(values[l, cols, :], spread_t, 1, 0)
            d_scores = (terms.astype(F32) * (d_terms - delta)).astype(BF)
            d_key = dot(d_scores, stacked, 1, 0)
            d_value = dot(terms, spread, 1, 0)
            if i == LEN // BQ - 1:
                scores[cols, 0:128] = d_key
                scores[cols, 128:256] = d_value
            else:
                scores[cols, 0:128] += d_key
                scores[cols, 128:256] += d_value
            d_query_t = d_query_t + dot(keys_t[l, :, cols], d_scores, 1, 0)
        d_query = split_heads(d_query_t).T * HD**-0.5
        d_joined[rows, 0:128] = turn_back(d_query, cosine[rows, :], sine[rows, :]).astype(BF)

    def finish_keys(i, carry):
        rows = pl.ds(pl.multiple_of(i * BQ, BQ), BQ)
        d_joined[rows, 128:256] = turn_back(scores[rows, 0:128], cosine[rows, :], sine[rows, :]).astype(
            BF
        )
        d_joined[rows, 256:384] = scores[rows, 128:256].astype(BF)
        return carry

    def blocks_of(ck):
        return range(ck * R // BQ, (ck + 1) * R // BQ)

    def forward(l, ck):
        def one(i, carry):
            project(l, i)
            return carry

        lax.fori_loop(ck * R // BQ, (ck + 1) * R // BQ, one, 0)
        for i in blocks_of(ck):
            attend(l, i)

    def backward_first(l, ck):
        def one(i, carry):
            rows = pl.ds(pl.multiple_of(i * BQ, BQ), BQ)
            both = dot(grads_in[l, rows, :], weights[l, :, NIN:NALL], 1, 0)
            d_context[rows, :] = both[:, 0:128].astype(BF)
            d_joined[rows, 384:NIN] = (both[:, 128:NOUT] * slope[l, rows, :].astype(F32)).astype(BF)
            return carry

        lax.fori_loop(ck * R // BQ, (ck + 1) * R // BQ, one, 0)

    def backward_second(l, ck):
        for i in reversed(blocks_of(ck)):
            attend_back(l, i)
        lax.fori_loop(ck * R // BQ, (ck + 1) * R // BQ, finish_keys, 0)

    def branch(l, rows):
        return dot(joined[l, rows, :], weights[l, :, NIN:NALL], 1, 1)

    def norm_grad(l, rows):
        shares = [
            dot(d_joined[rows, 0:384], weights[l, :, 0:384], 1, 1),
            dot(d_joined[rows, 384:NIN], weights[l, :, 384:NIN], 1, 1),
        ]
        scaled = xhat[l, rows, :].astype(F32)
        for k, e in enumerate(shares):
            message[l, 2 + k : 3 + k, :] += jnp.sum(scaled * e, axis=0, keepdims=True)
            message[l, 4 + k : 5 + k, :] += jnp.sum(e, axis=0, keepdims=True)
        return shares[0] + shares[1]

    def own_rows(ck, part_=None):
        first = ck * R + core * HALF + x * QUARTER
        return pl.ds(pl.multiple_of(first, QUARTER), QUARTER)

    def reduce_send(ph, ck, term):
        slot = ph % 2
        drain(("part", ck))
        for b in range(NB):
            rows = pl.ds(pl.multiple_of(ck * R + (1 - core) * HALF + b * BM, BM), BM)
            part[rows, :] = term(rows).astype(BF)
            push(
                part.at[rows],
                core_part.at[slot, ck * HALF + b * BM : ck * HALF + (b + 1) * BM],
                core_s.at[ph, ck, b],
                core_r.at[ph, ck, b],
                device(1 - core, y, z, x),
                ("part", ck),
            )
        for b in range(NB):
            rows = pl.ds(pl.multiple_of(ck * R + core * HALF + b * BM, BM), BM)
            value = term(rows)
            other = core_part.at[slot, ck * HALF + b * BM : ck * HALF + (b + 1) * BM]
            wait(other, core_r.at[ph, ck, b])
            part[rows, :] = (value + other[...].astype(F32)).astype(BF)
        for j in range(1, 4):
            to = (x + j) % 4
            first = ck * R + core * HALF + to * QUARTER
            push(
                part.at[pl.ds(pl.multiple_of(first, QUARTER), QUARTER)],
                ring_part.at[slot, j - 1, ck * QUARTER : (ck + 1) * QUARTER],
                ring_s.at[ph, ck, j - 1],
                ring_r.at[ph, ck, j - 1],
                device(core, y, z, to),
                ("part", ck),
            )

    def reduce_finish(ph, ck):
        slot = ph % 2
        summed = part[own_rows(ck), :].astype(F32)
        for j in range(3):
            piece = ring_part.at[slot, j, ck * QUARTER : (ck + 1) * QUARTER]
            wait(piece, ring_r.at[ph, ck, j])
            summed = summed + piece[...].astype(F32)
        return summed

    def gather_send(n, ck, buffer):
        rows = own_rows(ck)
        for j in range(1, 4):
            push(
                buffer.at[rows],
                buffer.at[rows],
                gx_s.at[n, ck, j - 1],
                gx_r.at[n, ck, j - 1],
                device(core, y, z, (x + j) % 4),
            )
        push(
            buffer.at[rows],
            buffer.at[rows],
            gc_s.at[n, ck, 0],
            gc_r.at[n, ck, 0],
            device(1 - core, y, z, x),
        )

    def gather_pass(n, ck, buffer):
        for j in range(1, 4):
            first = ck * R + core * HALF + ((x - j + 4) % 4) * QUARTER
            piece = buffer.at[pl.ds(pl.multiple_of(first, QUARTER), QUARTER)]
            wait(piece, gx_r.at[n, ck, j - 1])
            push(
                piece,
                piece,
                gc_s.at[n, ck, j],
                gc_r.at[n, ck, j],
                device(1 - core, y, z, x),
            )

    def gather_finish(n, ck, buffer):
        for j in range(4):
            wait(buffer.at[own_rows(ck)], gc_r.at[n, ck, j])

    def out_rows(seq, ck, c_, x_):
        first = seq * LEN + ck * R + c_ * HALF + x_ * QUARTER
        return ends_out.at[pl.ds(pl.multiple_of(first, QUARTER), QUARTER)]

    def give_out(n, ck):
        src = ends_low.at[n, ck * QUARTER : (ck + 1) * QUARTER]
        dst = out_rows(z_hi, ck, core, x)
        recv = out_r.at[ck, core * 4 + x]
        target = 1 - n
        for j in range(4):
            where, send = device(target, y, z, (x + j) % 4), out_s.at[n, ck, j]
            if j == 0:
                push_or_keep(core == target, src, dst, send, recv, where)
            else:
                push(src, dst, send, recv, where)

    def out_arrived(ck):
        for c_ in range(2):
            for x_ in range(4):
                wait(out_rows(z_hi, ck, c_, x_), out_r.at[ck, c_ * 4 + x_])

    def across_copy(n, ck):
        first = z_hi * LEN + ck * R
        rows = ends_out.at[pl.ds(pl.multiple_of(first, R), R)]
        return pltpu.make_async_remote_copy(
            src_ref=rows,
            dst_ref=rows,
            send_sem=across_s.at[ck],
            recv_sem=across_r.at[ck],
            device_id=device(1 - n, y, (z + 2) % 4, x),
            device_id_type=MESH,
        )

    def across(n, ck):
        @pl.when(core == 1 - n)
        def _():
            out_arrived(ck)
            across_copy(n, ck).start()

    def across_end(n, ck):
        @pl.when(core == 1 - n)
        def _():
            across_copy(n, ck).wait()

    def direct_first(n, ck):
        push(
            ends_low.at[n, ck * QUARTER : (ck + 1) * QUARTER],
            out_rows(z_hi, ck, core, x),
            direct_s.at[0],
            direct_r.at[core],
            device(1 - n, y, (z + 2) % 4, x),
        )

    def direct_copy(n, ck, c_, j):
        rows = out_rows(1 - z_hi, ck, c_, x)
        return pltpu.make_async_remote_copy(
            src_ref=rows,
            dst_ref=rows,
            send_sem=direct2_s.at[c_, j - 1],
            recv_sem=direct2_r.at[c_, j - 1],
            device_id=device(1 - n, y, z, (x + j) % 4),
            device_id_type=MESH,
        )

    def direct_second(n, ck):
        @pl.when(core == 1 - n)
        def _():
            for c_ in range(2):
                wait(out_rows(1 - z_hi, ck, c_, x), direct_r.at[c_])
                for j in range(1, 4):
                    direct_copy(n, ck, c_, j).start()

    def direct_end(n, ck):
        @pl.when(core == 1 - n)
        def _():
            out_arrived(ck)
            for c_ in range(2):
                for j in range(1, 4):
                    direct_copy(n, ck, c_, j).wait()

    def weight_grads(l, p):
        for i in range(4):
            cols = slice(i * BQ, (i + 1) * BQ)
            if p == 0:
                pieces = [
                    ((384, NIN), dot(xhat[l, :, cols], d_joined[:, 384:NIN], 0, 0)),
                    ((NIN, NALL), dot(grads_in[l, :, cols], joined[l], 0, 0)),
                ]
            else:
                pieces = [((0, 384), dot(xhat[l, :, cols], d_joined[:, 0:384], 0, 0))]
            for (first, last), piece in pieces:
                low = piece.astype(BF)
                for k in range(2):
                    w_grad[i, k, :, first:last] = low[k * 128 : (k + 1) * 128]

    def plane_first(l, p):
        cols = slice(*G_PARTS[p])
        for k in range(2):
            z_ = 2 * core + k
            slot = (z_ - z + 3) % 4
            src, send = w_grad.at[:, k, 0:ROWS_A, cols], p1a_s.at[l, p, k]
            other = z_ != z

            @pl.when(other)
            def _(src=src, send=send, z_=z_, slot=slot):
                pltpu.make_async_remote_copy(
                    src_ref=src,
                    dst_ref=plane_a.at[l, slot, :, :, cols],
                    send_sem=send,
                    recv_sem=p1a_r.at[l, p, slot],
                    device_id=device(core, y, z_, x),
                    device_id_type=MESH,
                ).start()

            drains.setdefault("grad", []).append((other, src, send))
        for j in range(1, 4):
            to = (y + j) % 4
            push(
                w_grad.at[to, :, ROWS_A:, cols],
                plane_b.at[l, j - 1, :, :, cols],
                p1b_s.at[l, p, j - 1],
                p1b_r.at[l, p, j - 1],
                device(core, to, z, x),
                "grad",
            )

    def plane_second(l, p):
        cols = slice(*G_PARTS[p])

        @pl.when(forwarder)
        def _():
            for j in range(3):
                wait(plane_a.at[l, j, :, :, cols], p1a_r.at[l, p, j])

            def one(y_, carry):
                summed = w_grad[y_, z_lo, 0:ROWS_A, cols].astype(F32)
                for j in range(3):
                    summed = summed + plane_a[l, j, y_, :, cols].astype(F32)
                sum_a[l, y_, :, cols] = summed.astype(BF)
                return carry

            lax.fori_loop(0, 4, one, 0)
            for j in range(4):
                to = (y + j) % 4
                src, dst = sum_a.at[l, to, :, cols], own_a.at[y, :, cols]
                copy = pltpu.make_async_remote_copy(
                    src_ref=src,
                    dst_ref=dst,
                    send_sem=p2a_s.at[l, p, j],
                    recv_sem=p2a_r.at[p, y],
                    device_id=device(l, to, z, x),
                    device_id_type=MESH,
                )
                if j == 0:
                    pl.when(core == l)(pltpu.make_async_copy(src, dst, p2a_r.at[p, y]).start)
                    pl.when(core != l)(copy.start)
                else:
                    copy.start()

        for j in range(3):
            wait(plane_b.at[l, j, :, :, cols], p1b_r.at[l, p, j])
        for k in range(2):
            summed = w_grad[y, k, ROWS_A:, cols].astype(F32)
            for j in range(3):
                summed = summed + plane_b[l, j, k, :, cols].astype(F32)
            sum_b[l, k, :, cols] = summed.astype(BF)
            z_ = 2 * core + k
            push_or_keep(
                jnp.logical_and(core == l, z_ == z),
                sum_b.at[l, k, :, cols],
                own_b.at[z, :, cols],
                p2b_s.at[l, p, k],
                p2b_r.at[p, z],
                device(l, y, z_, x),
            )

    def drain_plane():
        @pl.when(forwarder)
        def _():
            for l in range(2):
                for p, cols in enumerate(G_PARTS):
                    src = sum_a.at[l, 0, :, slice(*cols)]
                    for j in range(4):
                        ended = functools.partial(wait, src, p2a_s.at[l, p, j])
                        if j == 0:
                            pl.when(core != l)(ended)
                        else:
                            ended()

    def send_small(l):
        column_sum = jnp.zeros((1, NIN), F32)
        out_sum = jnp.zeros((1, D), F32)

        def one(i, carry):
            rows = pl.ds(pl.multiple_of(i * 128, 128), 128)
            a, b = carry
            a = a + jnp.sum(d_joined[rows, :].astype(F32), axis=0, keepdims=True)
            b = b + jnp.sum(grads_in[l, rows, :].astype(F32), axis=0, keepdims=True)
            return a, b

        column_sum, out_sum = lax.fori_loop(0, LEN // 128, one, (column_sum, out_sum))
        message[l, 0:1, 0:NIN] = column_sum
        message[l, 1:2, :] = out_sum
        here = y * 4 + z
        for y_ in range(4):
            for k in range(2):
                z_ = 2 * core + k
                own = jnp.logical_and(core == l, jnp.logical_and(y_ == y, z_ == z))
                push_or_keep(
                    own,
                    message.at[l],
                    messages.at[here],
                    msg_s.at[l, y_ * 2 + k],
                    msg_r.at[here],
                    device(l, y_, z_, x),
                )

    def small_first():
        for k in range(16):
            wait(messages.at[k], msg_r.at[k])
        summed = messages[0]
        for k in range(1, 16):
            summed = summed + messages[k]
        small[...] = summed
        for j in range(1, 4):
            push(
                small,
                small_ring.at[j - 1],
                ln1_s.at[j - 1],
                ln1_r.at[j - 1],
                device(core, y, z, (x + j) % 4),
            )
        for n in range(3):
            g_qkv_b[n] = summed[0:1, n * 128 : (n + 1) * 128]
        g_up_b[...] = summed[0:1, 384:NIN]
        g_out_b[...] = summed[1:2, :]

    def small_second():
        for j in range(3):
            wait(small_ring.at[j], ln1_r.at[j])
        small_sum[...] = small[...] + small_ring[0] + small_ring[1] + small_ring[2]
        push(small_sum, small_far, ln2_s, ln2_r, device(core, y, (z + 2) % 4, x))

    def small_third():
        wait(small_far, ln2_r)
        both = small_sum[...] + small_far[...]
        for k in range(2):
            g_gains[k : k + 1, :] = both[2 + k : 3 + k, :] / gains[k : k + 1, :]
            g_offsets[k : k + 1, :] = both[4 + k : 5 + k, :] / gains[k : k + 1, :]

    def after_first_layer(ck):
        rows = own_rows(ck)
        mid = slice(ck * QUARTER, (ck + 1) * QUARTER)
        result = x_own[mid, :].astype(F32) + reduce_finish(0, ck) + out_row[0]
        low = result.astype(BF)
        y_mid[ck * QUARTER : (ck + 1) * QUARTER, :] = low
        xhat[1, rows, :] = standardize(low.astype(F32))[0].astype(BF)
        gather_send(0, ck, xhat.at[1])

    def after_second_layer(ck):
        mid = slice(ck * QUARTER, (ck + 1) * QUARTER)
        result = y_mid[mid, :].astype(F32) + reduce_finish(1, ck) + out_row[1]
        ends_low[0, mid, :] = result.astype(BF)

    def through_norm(stream, grad, e):
        scaled, inverse = standardize(stream)
        return grad + inverse * (
            e
            - jnp.mean(e, axis=-1, keepdims=True)
            - scaled * jnp.mean(e * scaled, axis=-1, keepdims=True)
        )

    def input_grad_middle(ck):
        mid = slice(ck * QUARTER, (ck + 1) * QUARTER)
        rows = own_rows(ck)
        e = reduce_finish(2, ck)
        moved = through_norm(y_mid[mid, :].astype(F32), grads_in[1, rows, :].astype(F32), e)
        grads_in[0, rows, :] = moved.astype(BF)
        gather_send(1, ck, grads_in.at[0])

    def input_grad_first(ck):
        mid = slice(ck * QUARTER, (ck + 1) * QUARTER)
        rows = own_rows(ck)
        e = reduce_finish(3, ck)
        moved = through_norm(x_own[mid, :].astype(F32), grads_in[0, rows, :].astype(F32), e)
        ends_low[1, mid, :] = moved.astype(BF)

    forward(0, 0)
    gather_rest(0, 1)
    reduce_send(0, 0, functools.partial(branch, 0))
    gather_second(1, 0)
    forward(0, 1)
    reduce_send(0, 1, functools.partial(branch, 0))
    after_first_layer(0)
    after_first_layer(1)
    gather_pass(0, 0, xhat.at[1])
    gather_finish(0, 0, xhat.at[1])
    gather_rest(1, 0)
    forward(1, 0)
    reduce_send(1, 0, functools.partial(branch, 1))
    gather_pass(0, 1, xhat.at[1])
    gather_finish(0, 1, xhat.at[1])
    forward(1, 1)
    reduce_send(1, 1, functools.partial(branch, 1))

    wait(mine, swap_s)
    backward_first(1, 1)
    backward_first(1, 0)
    after_second_layer(0)
    give_out(0, 0)
    weight_grads(1, 0)
    plane_first(1, 0)
    after_second_layer(1)
    give_out(0, 1)
    backward_second(1, 1)
    reduce_send(2, 1, functools.partial(norm_grad, 1))
    backward_second(1, 0)
    reduce_send(2, 0, functools.partial(norm_grad, 1))
    input_grad_middle(1)
    weight_grads(1, 1)
    plane_first(1, 1)
    input_grad_middle(0)
    gather_pass(1, 1, grads_in.at[0])
    across(0, 0)
    across(0, 1)
    send_small(1)
    plane_second(1, 0)
    gather_finish(1, 1, grads_in.at[0])

    backward_first(0, 1)
    backward_second(0, 1)
    gather_pass(1, 0, grads_in.at[0])
    reduce_send(3, 1, functools.partial(norm_grad, 0))
    gather_finish(1, 0, grads_in.at[0])
    backward_first(0, 0)
    plane_second(1, 1)
    drain("grad")
    weight_grads(0, 0)
    plane_first(0, 0)
    backward_second(0, 0)
    reduce_send(3, 0, functools.partial(norm_grad, 0))
    input_grad_first(1)
    give_out(1, 1)
    weight_grads(0, 1)
    plane_first(0, 1)
    send_small(0)
    input_grad_first(0)
    direct_first(1, 0)
    give_out(1, 0)
    across(1, 1)
    plane_second(0, 0)
    small_first()
    direct_second(1, 0)
    plane_second(0, 1)
    small_second()

    for k in range(4):
        for p, cols in enumerate(G_PARTS):
            wait(own_a.at[k, :, slice(*cols)], p2a_r.at[p, k])
            wait(own_b.at[k, :, slice(*cols)], p2b_r.at[p, k])
    total[0:ROWS_A, :] = (
        own_a[0].astype(F32) + own_a[1].astype(F32) + own_a[2].astype(F32) + own_a[3].astype(F32)
    )
    total[ROWS_A:128, :] = (
        own_b[0].astype(F32) + own_b[1].astype(F32) + own_b[2].astype(F32) + own_b[3].astype(F32)
    )
    for n in range(7):
        k = 0 if n < 3 else 1
        cols = slice(n * 128, (n + 1) * 128)
        grad = total[:, cols] * gain_cols[k] + offset_cols[k] * small[0:1, cols]
        if n < 3:
            g_qkv[n] = grad
        else:
            g_up[:, (n - 3) * 128 : (n - 2) * 128] = grad
    g_dense[...] = total[:, NIN : NIN + 128].T
    g_down[...] = total[:, NIN + 128 : NALL].T
    small_third()
    across_end(0, 0)
    across_end(0, 1)
    across_end(1, 1)
    direct_end(1, 0)
    drain("grad")
    for ck in range(NCH):
        drain(("part", ck))
    drain("end")
    drain_first()
    drain_second()
    drain_extra()
    drain_plane()


def settle(*refs):
    count = (len(refs) - 2) // 3
    sources, targets, held = refs[:count], refs[count : 2 * count], refs[2 * count : 3 * count]
    sem_in, sem_out = refs[-2:]
    trips = []
    rows = sources[0].shape[0] // 8
    for k in range(8):
        piece = pl.ds(k * rows, rows)
        trips.append((sources[0].at[piece], held[0].at[piece], targets[0].at[piece]))
    for n in range(1, count):
        trips.append((sources[n], held[n], targets[n]))
    arrivals = []
    departures = []
    for n, (source, stop, target) in enumerate(trips):
        arrivals.append(pltpu.make_async_copy(source, stop, sem_in.at[n]))
        departures.append(pltpu.make_async_copy(stop, target, sem_out.at[n]))
    for copy in arrivals:
        copy.start()
    for arrival, departure in zip(arrivals, departures):
        arrival.wait()
        departure.start()
    for copy in departures:
        copy.wait()


def body(ends_in, ln_gains, ln_biases, qkv_w, qkv_bias, dense_w, up_w, up_bias, down_w, out_bias):
    cosine, sine = rotary_tables()
    vmem = pl.BlockSpec(memory_space=pltpu.VMEM)
    anywhere = pl.BlockSpec(memory_space=pl.ANY)

    def shape(*dims):
        return jax.ShapeDtypeStruct(dims, F32)

    def sems(*dims):
        return pltpu.SemaphoreType.DMA(dims)

    outs = pl.pallas_call(
        kernel,
        out_shape=[
            jax.ShapeDtypeStruct((2 * LEN, D), BF),
            shape(2, D),
            shape(2, D),
            shape(3, 128, 128),
            shape(3, 1, 128),
            shape(128, 128),
            shape(128, 512),
            shape(1, 512),
            shape(512, 128),
            shape(1, D),
        ],
        in_specs=[anywhere] + [vmem] * 11,
        out_specs=[vmem] * 10,
        scratch_shapes=[
            pltpu.VMEM((128, NALL), BF),
            pltpu.VMEM((8, 256), F32),
            pltpu.VMEM((2, 8, 8, 256), F32),
            pltpu.VMEM((2, 1, 1024), F32),
            pltpu.VMEM((2, 1, 1024), F32),
            pltpu.VMEM((2, D, NALL), BF),
            pltpu.VMEM((LEN, D), BF),
            pltpu.VMEM((2, LEN, D), BF),
            pltpu.VMEM((2, LEN, D), BF),
            pltpu.VMEM((LEN // 8, D), BF),
            pltpu.VMEM((LEN // 8, D), BF),
            pltpu.VMEM((2, LEN, NOUT), BF),
            pltpu.VMEM((2, LEN, 512), BF),
            pltpu.VMEM((2, LEN, 128), BF),
            pltpu.VMEM((2, LEN, 128), BF),
            pltpu.VMEM((2, LEN, 128), BF),
            pltpu.VMEM((2, 128, LEN), BF),
            pltpu.VMEM((128, LEN), BF),
            pltpu.VMEM((2, 10, BQ, 2 * BQ), BF),
            pltpu.VMEM((2, LEN // BQ, 2 * BQ), F32),
            pltpu.VMEM((2, 128, LEN), F32),
            pltpu.VMEM((LEN, 2 * BQ), F32),
            pltpu.VMEM((LEN, 128), BF),
            pltpu.VMEM((LEN, NIN), BF),
            pltpu.VMEM((2, LEN // 2, D), BF),
            pltpu.VMEM((2, 3, LEN // 8, D), BF),
            pltpu.VMEM((2, LEN // 8, D), BF),
            pltpu.VMEM((4, 2, 128, NALL), BF),
            pltpu.VMEM((2, 3, 4, ROWS_A, NALL), BF),
            pltpu.VMEM((2, 3, 2, ROWS_B, NALL), BF),
            pltpu.VMEM((2, 4, ROWS_A, NALL), BF),
            pltpu.VMEM((2, 2, ROWS_B, NALL), BF),
            pltpu.VMEM((4, ROWS_A, NALL), BF),
            pltpu.VMEM((4, ROWS_B, NALL), BF),
            pltpu.VMEM((128, NALL), F32),
            pltpu.VMEM((2, 8, D), F32),
            pltpu.VMEM((16, 8, D), F32),
            pltpu.VMEM((8, D), F32),
            pltpu.VMEM((3, 8, D), F32),
            pltpu.VMEM((8, D), F32),
            pltpu.VMEM((8, D), F32),
            pltpu.SemaphoreType.DMA,
            pltpu.SemaphoreType.DMA,
            pltpu.SemaphoreType.DMA,
            sems(2, 2, 4),
            sems(2, 2, 2, 8),
            sems(2, 2, 4, 3),
            sems(2, 2, 2, 3),
            sems(16),
            sems(2, 8),
            sems(4, NCH, NB),
            sems(4, NCH, NB),
            sems(4, NCH, 3),
            sems(4, NCH, 3),
            sems(2, NCH, 3),
            sems(2, NCH, 3),
            sems(2, NCH, 4),
            sems(2, NCH, 4),
            sems(2, NCH, 4),
            sems(NCH, 8),
            sems(NCH),
            sems(NCH),
            sems(1),
            sems(2),
            sems(2, 3),
            sems(2, 3),
            sems(2, 8),
            sems(16),
            sems(2, 2, 2),
            sems(2, 2, 3),
            sems(2, 2, 3),
            sems(2, 2, 3),
            sems(2, 2, 4),
            sems(2, 4),
            sems(2, 2, 2),
            sems(2, 4),
            sems(3),
            sems(3),
            pltpu.SemaphoreType.DMA,
            pltpu.SemaphoreType.DMA,
        ],
        compiler_params=pltpu.CompilerParams(
            collective_id=0, has_side_effects=True, vmem_limit_bytes=63 * 2**20
        ),
        cost_estimate=pl.CostEstimate(
            flops=22 * 10**9, bytes_accessed=20 * 10**6, transcendentals=4 * 10**6
        ),
    )(
        ends_in[0],
        qkv_w[0],
        dense_w[0],
        up_w[0],
        down_w[0],
        ln_gains[0],
        ln_biases[0],
        jnp.transpose(qkv_bias, (1, 0, 2)),
        up_bias,
        out_bias,
        jnp.asarray(cosine),
        jnp.asarray(sine),
    )
    outs = pl.pallas_call(
        settle,
        out_shape=[jax.ShapeDtypeStruct(out.shape, out.dtype) for out in outs],
        in_specs=[anywhere] * len(outs),
        out_specs=[anywhere] * len(outs),
        scratch_shapes=[pltpu.VMEM(out.shape, out.dtype) for out in outs]
        + [sems(len(outs) + 7), sems(len(outs) + 7)],
        compiler_params=pltpu.CompilerParams(vmem_limit_bytes=63 * 2**20),
        cost_estimate=pl.CostEstimate(flops=0, bytes_accessed=10 * 10**6, transcendentals=0),
    )(*outs)
    out, gains, offsets, d_qkv, d_qkv_b, d_dense, d_up, d_up_b, d_down, d_out_b = outs
    return (
        out[None],
        gains[None],
        offsets[None],
        d_qkv[None],
        jnp.transpose(d_qkv_b, (1, 0, 2)),
        d_dense[None],
        d_up[None],
        d_up_b,
        d_down[None],
        d_out_b,
    )


def solution(mesh):
    in_specs = (
        P("section", "dp", None),
        P("section", None, None),
        P("section", None, None),
        P("section", None, "dp", "tensor"),
        P("section", None, "tensor"),
        P("section", "tensor", "dp"),
        P("section", "dp", "tensor"),
        P("section", "tensor"),
        P("section", "tensor", "dp"),
        P("section", None),
    )
    out_specs = (
        P("section", "dp", None),
        P("section", None, None),
        P("section", None, None),
        P("section", None, "dp", "tensor"),
        P("section", None, "tensor"),
        P("section", "tensor", "dp"),
        P("section", "dp", "tensor"),
        P("section", "tensor"),
        P("section", "tensor", "dp"),
        P("section", None),
    )
    return jax.shard_map(body, mesh=mesh, in_specs=in_specs, out_specs=out_specs, check_vma=False)
```

```python
import functools

import jax
import jax.numpy as jnp
import numpy as np
from jax import lax
from jax.experimental import pallas as pl
from jax.experimental.pallas import tpu as pltpu
from jax.sharding import PartitionSpec as P

MESH = pl.DeviceIdType.MESH
BF = jnp.bfloat16
F32 = jnp.float32

D = 1024
LEN = 1024
HD = 64
ROT = 16
NIN = 896
NOUT = 640
NALL = NIN + NOUT
BQ = 256
NCH = 2
R = LEN // NCH
HALF = R // 2
QUARTER = R // 8
BM = min(256, HALF)
NB = HALF // BM
W_PARTS = (((0, NIN), (NIN, NALL)), ((0, NALL),))
G_PARTS = ((384, NALL), (0, 384))
ROWS_A = 48
ROWS_B = 128 - ROWS_A


def dot(a, b, ca, cb):
    return lax.dot_general(a, b, (((ca,), (cb,)), ((), ())), preferred_element_type=F32)


def rotary_tables():
    position = np.arange(LEN, dtype=np.float32)[:, None]
    exponent = np.arange(ROT // 2, dtype=np.float32) * np.float32(2.0) / np.float32(ROT)
    angles = (position * np.float32(10000.0) ** (-exponent)).astype(np.float32)
    cosine = np.ones((LEN, 2 * HD), np.float32)
    sine = np.zeros((LEN, 2 * HD), np.float32)
    for first in (0, 8, HD, HD + 8):
        cosine[:, first : first + 8] = np.cos(angles)
        sine[:, first : first + 8] = np.sin(angles)
    return cosine, sine


def lanes_of_head(shape):
    return lax.broadcasted_iota(jnp.int32, shape, 1) % HD


def turn(value, cosine, sine):
    lane = lanes_of_head(value.shape)
    partner = jnp.where(lane < 8, -pltpu.roll(value, 120, 1), pltpu.roll(value, 8, 1))
    return value * cosine + partner * sine


def turn_back(grad, cosine, sine):
    lane = lanes_of_head(grad.shape)
    moved = grad * sine
    partner = jnp.where(
        lane < 8, pltpu.roll(moved, 120, 1), jnp.where(lane < 16, -pltpu.roll(moved, 8, 1), 0.0)
    )
    return grad * cosine + partner


def gelu_and_slope(hidden):
    bell = jnp.exp(-0.5 * hidden * hidden)
    size = 1.0 + (0.3275911 * 0.7071067811865476) * jnp.abs(hidden)
    t = pltpu.reciprocal(size, approx=True)
    t = t * (2.0 - size * t)
    series = t * (
        0.254829592 * 0.5
        + t
        * (
            -0.284496736 * 0.5
            + t * (1.421413741 * 0.5 + t * (-1.453152027 * 0.5 + t * (1.061405429 * 0.5)))
        )
    )
    tail = series * bell
    below = jnp.where(hidden >= 0.0, 1.0 - tail, tail)
    return hidden * below, below + hidden * bell * 0.3989422804014327


def standardize(value):
    center = jnp.mean(value, axis=-1, keepdims=True)
    centred = value - center
    inverse = lax.rsqrt(jnp.mean(centred * centred, axis=-1, keepdims=True) + 1e-05)
    return centred * inverse, inverse


def stack_heads(value):
    lane = lax.broadcasted_iota(jnp.int32, value.shape, 1)
    wide = value.astype(F32)
    return jnp.concatenate(
        [jnp.where(lane < HD, wide, 0.0), jnp.where(lane >= HD, wide, 0.0)], axis=0
    ).astype(BF)


def split_heads(value):
    half = value.shape[1] // 2
    return jnp.concatenate([value[:HD, :half], value[HD:, half:]], axis=0)


def pair(i, j):
    return i * (i + 1) // 2 + j


def kernel(
    ends,
    qkv,
    dense,
    up,
    down,
    gains,
    offsets,
    qkv_b,
    up_b,
    out_b,
    cosine,
    sine,
    ends_out,
    g_gains,
    g_offsets,
    g_qkv,
    g_qkv_b,
    g_dense,
    g_up,
    g_up_b,
    g_down,
    g_out_b,
    shard,
    extra,
    extras,
    bias_row,
    out_row,
    weights,
    x_in,
    grads_in,
    xhat,
    y_mid,
    x_own,
    joined,
    slope,
    queries,
    keys,
    values,
    keys_t,
    values_t,
    soft,
    soft_scale,
    context_t,
    scores,
    d_context,
    d_joined,
    core_part,
    ring_part,
    ends_low,
    w_grad,
    plane_a,
    plane_b,
    sum_a,
    sum_b,
    own_a,
    own_b,
    total,
    message,
    messages,
    small,
    small_ring,
    small_sum,
    small_far,
    local_sem,
    swap_s,
    swap_r,
    w1_s,
    w_r,
    w2a_s,
    w2b_s,
    extra_s,
    extra_r,
    core_s,
    core_r,
    ring_s,
    ring_r,
    gx_s,
    gx_r,
    gc_s,
    gc_r,
    out_s,
    out_r,
    direct_s,
    direct_r,
    direct2_s,
    direct2_r,
    msg_s,
    msg_r,
    p1a_s,
    p1a_r,
    p1b_s,
    p1b_r,
    p2a_s,
    p2a_r,
    p2b_s,
    p2b_r,
    ln1_s,
    ln1_r,
    ln2_s,
    ln2_r,
):
    part = x_in
    core = lax.axis_index("section")
    dp = lax.axis_index("dp")
    t = lax.axis_index("tensor")
    y, z_lo = dp // 2, dp % 2
    z_hi, x = t // 4, t % 4
    z = 2 * z_hi + z_lo
    forwarder = core == z_hi

    def device(c_, y_, z_, x_):
        return {"section": c_, "dp": y_ * 2 + z_ % 2, "tensor": (z_ // 2) * 4 + x_}

    drains = {}

    def wait(ref, sem):
        pltpu.make_async_copy(ref, ref, sem).wait()

    def push(src, dst, send, recv, where, tag="end"):
        pltpu.make_async_remote_copy(
            src_ref=src, dst_ref=dst, send_sem=send, recv_sem=recv, device_id=where, device_id_type=MESH
        ).start()
        drains.setdefault(tag, []).append((None, src, send))

    def push_or_keep(own, src, dst, send, recv, where):
        other = jnp.logical_not(own)

        @pl.when(own)
        def _():
            pltpu.make_async_copy(src, dst, recv).start()

        @pl.when(other)
        def _():
            pltpu.make_async_remote_copy(
                src_ref=src,
                dst_ref=dst,
                send_sem=send,
                recv_sem=recv,
                device_id=where,
                device_id_type=MESH,
            ).start()

        drains.setdefault("end", []).append((other, src, send))

    def drain(tag):
        for condition, src, send in drains.pop(tag, []):
            if condition is None:
                wait(src, send)
            else:
                pl.when(condition)(functools.partial(wait, src, send))

    barrier = pltpu.get_barrier_semaphore()
    for dy in range(4):
        for dz in range(4):
            for c_ in range(2):
                if (dy, dz, c_) == (0, 0, 0):
                    continue
                pl.semaphore_signal(
                    barrier,
                    inc=1,
                    device_id=device((core + c_) % 2, (y + dy) % 4, (z + dz) % 4, x),
                    device_id_type=MESH,
                )
    for j in range(1, 4):
        pl.semaphore_signal(
            barrier, inc=1, device_id=device(core, y, z, (x + j) % 4), device_id_type=MESH
        )

    block = pl.ds(pl.multiple_of(dp * 128, 128), 128)

    def column(row):
        return jnp.broadcast_to(row, (128, 128)).T

    gain_cols = [column(gains[k : k + 1, block]) for k in range(2)]
    offset_cols = [column(offsets[k : k + 1, block]) for k in range(2)]

    def raw_tile(n):
        if n < 3:
            return qkv[n].astype(F32), 0, qkv_b[n]
        cols = slice((n - 3) * 128, (n - 2) * 128)
        return up[:, cols].astype(F32), 1, up_b[:, cols]

    extra[...] = jnp.zeros_like(extra)
    message[...] = jnp.zeros_like(message)
    for n in range(7):
        tile, k, bias = raw_tile(n)
        shard[:, n * 128 : (n + 1) * 128] = (tile * gain_cols[k]).astype(BF)
        added = jnp.sum(tile * offset_cols[k], axis=0, keepdims=True) + 0.125 * bias
        extra[n // 2 : n // 2 + 1, (n % 2) * 128 : (n % 2) * 128 + 128] = added
    for n in range(4):
        extra[4 + n : 5 + n, :] = 0.125 * out_b[:, n * 256 : (n + 1) * 256]
    shard[:, NIN : NIN + 128] = dense[...].T
    shard[:, NIN + 128 : NALL] = down[...].T

    pl.semaphore_wait(barrier, 34)

    mine = ends.at[pl.ds(pl.multiple_of(z_hi * LEN, LEN), LEN)]
    for c_, buffer in ((0, x_in), (1, grads_in.at[1])):

        @pl.when(core == c_)
        def _(buffer=buffer):
            pltpu.make_async_copy(mine, buffer, local_sem).start()
            pltpu.make_async_remote_copy(
                src_ref=mine,
                dst_ref=buffer,
                send_sem=swap_s,
                recv_sem=swap_r,
                device_id=device(1 - core, y, z, x),
                device_id_type=MESH,
            ).start()

    def w_rows(l, p, dp_, half):
        rows = pl.ds(pl.multiple_of(dp_ * 128 + half * 64, 64), 64)
        return weights.at[l, rows, slice(*W_PARTS[l][p])]

    def gather_first(l):
        @pl.when(core == l)
        def _():
            for p, cols in enumerate(W_PARTS[l]):
                for half in range(2):
                    src = shard.at[half * 64 : half * 64 + 64, slice(*cols)]
                    dst = w_rows(l, p, dp, half)
                    recv = w_r.at[half, l, p, dp]

                    @pl.when(forwarder)
                    def _(src=src, dst=dst, recv=recv):
                        pltpu.make_async_copy(src, dst, recv).start()

                    for j in range(4):
                        if half == 0:
                            where = device(z_hi, (y + j) % 4, z, x)
                        else:
                            where = device(z_hi, y, (z + j) % 4, x)
                        copy = pltpu.make_async_remote_copy(
                            src_ref=src,
                            dst_ref=dst,
                            send_sem=w1_s.at[p, half, j],
                            recv_sem=recv,
                            device_id=where,
                            device_id_type=MESH,
                        )
                        if j == 0:
                            pl.when(jnp.logical_not(forwarder))(copy.start)
                        else:
                            copy.start()

    def drain_first():
        for l in range(2):

            @pl.when(core == l)
            def _(l=l):
                for p, cols in enumerate(W_PARTS[l]):
                    src = shard.at[0:64, slice(*cols)]
                    for half in range(2):
                        for j in range(4):
                            ended = functools.partial(wait, src, w1_s.at[p, half, j])
                            if j == 0:
                                pl.when(jnp.logical_not(forwarder))(ended)
                            else:
                                ended()

    def gather_second(l, p):
        for k in range(2):
            block_b = w_rows(l, p, y * 2 + k, 1)
            wait(block_b, w_r.at[1, l, p, y * 2 + k])
            for j in range(1, 4):
                push(
                    block_b,
                    block_b,
                    w2b_s.at[l, p, k, j - 1],
                    w_r.at[1, l, p, y * 2 + k],
                    device(core, (y + j) % 4, z, x),
                )

        @pl.when(forwarder)
        def _():
            for y_ in range(4):
                dp_ = y_ * 2 + z_lo
                block_a = w_rows(l, p, dp_, 0)
                wait(block_a, w_r.at[0, l, p, dp_])
                for j in range(1, 4):
                    pltpu.make_async_remote_copy(
                        src_ref=block_a,
                        dst_ref=block_a,
                        send_sem=w2a_s.at[l, p, y_, j - 1],
                        recv_sem=w_r.at[0, l, p, dp_],
                        device_id=device(core, y, (z + j) % 4, x),
                        device_id_type=MESH,
                    ).start()

    def drain_second():
        @pl.when(forwarder)
        def _():
            for l in range(2):
                for p in range(len(W_PARTS[l])):
                    for y_ in range(4):
                        for j in range(3):
                            wait(w_rows(l, p, 0, 0), w2a_s.at[l, p, y_, j])

    def gather_rest(l, p):
        for j in range(1, 4):
            for k in range(2):
                dp_ = ((y + j) % 4) * 2 + k
                wait(w_rows(l, p, dp_, 1), w_r.at[1, l, p, dp_])
        for y_ in range(4):
            dp_ = y_ * 2 + 1 - z_lo
            wait(w_rows(l, p, dp_, 0), w_r.at[0, l, p, dp_])

            @pl.when(jnp.logical_not(forwarder))
            def _(dp_=y_ * 2 + z_lo):
                wait(w_rows(l, p, dp_, 0), w_r.at[0, l, p, dp_])

        if p > 0:
            return
        for dp_ in range(8):
            wait(extras.at[l, dp_], extra_r.at[l, dp_])
        summed = extras[l, 0]
        for dp_ in range(1, 8):
            summed = summed + extras[l, dp_]
        for n in range(4):
            bias_row[l, :, n * 256 : (n + 1) * 256] = summed[n : n + 1, :]
            out_row[l, :, n * 256 : (n + 1) * 256] = summed[4 + n : 5 + n, :]

    gather_first(0)
    for l in range(2):

        @pl.when(core == l)
        def _(l=l):
            for dy in range(4):
                for dz in range(4):
                    where = device(z_hi, (y + dy) % 4, (z + dz) % 4, x)
                    dst = extras.at[l, dp]
                    recv = extra_r.at[l, dp]
                    copy = pltpu.make_async_remote_copy(
                        src_ref=extra,
                        dst_ref=dst,
                        send_sem=extra_s.at[dy * 4 + dz],
                        recv_sem=recv,
                        device_id=where,
                        device_id_type=MESH,
                    )
                    if (dy, dz) == (0, 0):
                        pl.when(forwarder)(pltpu.make_async_copy(extra, dst, recv).start)
                        pl.when(jnp.logical_not(forwarder))(copy.start)
                    else:
                        copy.start()

    def drain_extra():
        for k in range(16):
            if k == 0:
                pl.when(jnp.logical_not(forwarder))(
                    functools.partial(wait, extra, extra_s.at[k])
                )
            else:
                wait(extra, extra_s.at[k])

    wait(x_in, local_sem)
    wait(x_in, swap_r)

    gather_second(0, 0)

    def normalize_rows(i, carry):
        rows = pl.ds(pl.multiple_of(i * 128, 128), 128)
        xhat[0, rows, :] = standardize(x_in[rows, :].astype(F32))[0].astype(BF)
        return carry

    lax.fori_loop(0, LEN // 128, normalize_rows, 0)
    for ck in range(NCH):
        first = ck * R + core * HALF + x * QUARTER
        x_own[ck * QUARTER : (ck + 1) * QUARTER, :] = x_in[
            pl.ds(pl.multiple_of(first, QUARTER), QUARTER), :
        ]
    gather_second(0, 1)
    gather_first(1)
    gather_rest(0, 0)

    def project(l, i):
        rows = pl.ds(pl.multiple_of(i * BQ, BQ), BQ)
        low = xhat[l, rows, :]
        raw = dot(low, weights[l, :, 0:384], 1, 0) + bias_row[l, :, 0:384]
        cos_rows, sin_rows = cosine[rows, :], sine[rows, :]
        q = turn(raw[:, 0:128], cos_rows, sin_rows) * HD**-0.5
        k = turn(raw[:, 128:256], cos_rows, sin_rows)
        v = raw[:, 256:384]
        queries[l, rows, :] = q.astype(BF)
        keys[l, rows, :] = k.astype(BF)
        values[l, rows, :] = v.astype(BF)
        keys_t[l, :, rows] = k.T.astype(BF)
        values_t[:, rows] = v.T.astype(BF)
        hidden = dot(low, weights[l, :, 384:NIN], 1, 0) + bias_row[l, :, 384:NIN]
        act, gradient = gelu_and_slope(hidden)
        joined[l, rows, 128:NOUT] = act.astype(BF)
        slope[l, rows, :] = gradient.astype(BF)

    def attend(l, i):
        rows = slice(i * BQ, (i + 1) * BQ)
        stacked = stack_heads(queries[l, rows, :])
        largest = None
        for j in range(i + 1):
            tile = dot(keys[l, j * BQ : (j + 1) * BQ, :], stacked, 1, 1)
            if j == i:
                key_at = lax.broadcasted_iota(jnp.int32, tile.shape, 0)
                query_at = lax.broadcasted_iota(jnp.int32, tile.shape, 1) % BQ
                tile = jnp.where(key_at <= query_at, tile, -1e30)
            scores[j * BQ : (j + 1) * BQ, :] = tile
            top = jnp.max(tile, axis=0, keepdims=True)
            largest = top if largest is None else jnp.maximum(largest, top)
        summed = jnp.zeros((1, 2 * BQ), F32)
        outcome = jnp.zeros((2 * HD, 2 * BQ), F32)
        for j in range(i + 1):
            terms = jnp.exp(scores[j * BQ : (j + 1) * BQ, :] - largest)
            summed = summed + jnp.sum(terms, axis=0, keepdims=True)
            low = terms.astype(BF)
            soft[l, pair(i, j)] = low
            outcome = outcome + dot(values_t[:, j * BQ : (j + 1) * BQ], low, 1, 0)
        scale = 1.0 / summed
        soft_scale[l, i : i + 1, :] = scale
        context = split_heads(outcome * scale)
        context_t[l, :, rows] = context
        joined[l, rows, 0:128] = context.T.astype(BF)

    def attend_back(l, i):
        rows = slice(i * BQ, (i + 1) * BQ)
        grad_t = d_context[rows, :].astype(F32).T
        scale = soft_scale[l, i : i + 1, :]
        top = grad_t[:HD] * scale[:, :BQ]
        bottom = grad_t[HD:] * scale[:, BQ:]
        context = context_t[l, :, rows]
        delta = jnp.concatenate(
            [
                jnp.sum(context[:HD] * top, axis=0, keepdims=True),
                jnp.sum(context[HD:] * bottom, axis=0, keepdims=True),
            ],
            axis=1,
        )
        blank = jnp.zeros_like(top)
        spread_wide = jnp.concatenate(
            [jnp.concatenate([top, blank], axis=1), jnp.concatenate([blank, bottom], axis=1)], axis=0
        )
        spread_t = spread_wide.astype(BF)
        spread = spread_wide.T.astype(BF)
        stacked = stack_heads(queries[l, rows, :])
        d_query_t = jnp.zeros((2 * HD, 2 * BQ), F32)
        for j in range(i + 1):
            cols = slice(j * BQ, (j + 1) * BQ)
            terms = soft[l, pair(i, j)]
            d_terms = dot(values[l, cols, :], spread_t, 1, 0)
            d_scores = (terms.astype(F32) * (d_terms - delta)).astype(BF)
            d_key = dot(d_scores, stacked, 1, 0)
            d_value = dot(terms, spread, 1, 0)
            if i == LEN // BQ - 1:
                scores[cols, 0:128] = d_key
                scores[cols, 128:256] = d_value
            else:
                scores[cols, 0:128] += d_key
                scores[cols, 128:256] += d_value
            d_query_t = d_query_t + dot(keys_t[l, :, cols], d_scores, 1, 0)
        d_query = split_heads(d_query_t).T * HD**-0.5
        d_joined[rows, 0:128] = turn_back(d_query, cosine[rows, :], sine[rows, :]).astype(BF)

    def finish_keys(i, carry):
        rows = pl.ds(pl.multiple_of(i * BQ, BQ), BQ)
        d_joined[rows, 128:256] = turn_back(scores[rows, 0:128], cosine[rows, :], sine[rows, :]).astype(
            BF
        )
        d_joined[rows, 256:384] = scores[rows, 128:256].astype(BF)
        return carry

    def blocks_of(ck):
        return range(ck * R // BQ, (ck + 1) * R // BQ)

    def project_all(l, ck):
        def one(i, carry):
            project(l, i)
            return carry

        lax.fori_loop(ck * R // BQ, (ck + 1) * R // BQ, one, 0)

    def attend_all(l, ck):
        for i in blocks_of(ck):
            attend(l, i)

    def backward_first(l, ck):
        def one(i, carry):
            rows = pl.ds(pl.multiple_of(i * BQ, BQ), BQ)
            both = dot(grads_in[l, rows, :], weights[l, :, NIN:NALL], 1, 0)
            d_context[rows, :] = both[:, 0:128].astype(BF)
            d_joined[rows, 384:NIN] = (both[:, 128:NOUT] * slope[l, rows, :].astype(F32)).astype(BF)
            return carry

        lax.fori_loop(ck * R // BQ, (ck + 1) * R // BQ, one, 0)

    def backward_second(l, ck):
        for i in reversed(blocks_of(ck)):
            attend_back(l, i)
        lax.fori_loop(ck * R // BQ, (ck + 1) * R // BQ, finish_keys, 0)

    def branch(l, rows):
        return dot(joined[l, rows, :], weights[l, :, NIN:NALL], 1, 1)

    def norm_grad(l, rows):
        shares = [
            dot(d_joined[rows, 0:384], weights[l, :, 0:384], 1, 1),
            dot(d_joined[rows, 384:NIN], weights[l, :, 384:NIN], 1, 1),
        ]
        scaled = xhat[l, rows, :].astype(F32)
        for k, e in enumerate(shares):
            message[l, 2 + k : 3 + k, :] += jnp.sum(scaled * e, axis=0, keepdims=True)
            message[l, 4 + k : 5 + k, :] += jnp.sum(e, axis=0, keepdims=True)
        return shares[0] + shares[1]

    def own_rows(ck, part_=None):
        first = ck * R + core * HALF + x * QUARTER
        return pl.ds(pl.multiple_of(first, QUARTER), QUARTER)

    def reduce_send(ph, ck, term):
        slot = ph % 2
        drain(("part", ck))
        for b in range(NB):
            rows = pl.ds(pl.multiple_of(ck * R + (1 - core) * HALF + b * BM, BM), BM)
            part[rows, :] = term(rows).astype(BF)
            push(
                part.at[rows],
                core_part.at[slot, ck * HALF + b * BM : ck * HALF + (b + 1) * BM],
                core_s.at[ph, ck, b],
                core_r.at[ph, ck, b],
                device(1 - core, y, z, x),
                ("part", ck),
            )
        for b in range(NB):
            rows = pl.ds(pl.multiple_of(ck * R + core * HALF + b * BM, BM), BM)
            value = term(rows)
            other = core_part.at[slot, ck * HALF + b * BM : ck * HALF + (b + 1) * BM]
            wait(other, core_r.at[ph, ck, b])
            part[rows, :] = (value + other[...].astype(F32)).astype(BF)
        for j in range(1, 4):
            to = (x + j) % 4
            first = ck * R + core * HALF + to * QUARTER
            push(
                part.at[pl.ds(pl.multiple_of(first, QUARTER), QUARTER)],
                ring_part.at[slot, j - 1, ck * QUARTER : (ck + 1) * QUARTER],
                ring_s.at[ph, ck, j - 1],
                ring_r.at[ph, ck, j - 1],
                device(core, y, z, to),
                ("part", ck),
            )

    def reduce_finish(ph, ck):
        slot = ph % 2
        summed = part[own_rows(ck), :].astype(F32)
        for j in range(3):
            piece = ring_part.at[slot, j, ck * QUARTER : (ck + 1) * QUARTER]
            wait(piece, ring_r.at[ph, ck, j])
            summed = summed + piece[...].astype(F32)
        return summed

    def gather_send(n, ck, buffer):
        rows = own_rows(ck)
        for j in range(1, 4):
            push(
                buffer.at[rows],
                buffer.at[rows],
                gx_s.at[n, ck, j - 1],
                gx_r.at[n, ck, j - 1],
                device(core, y, z, (x + j) % 4),
            )
        push(
            buffer.at[rows],
            buffer.at[rows],
            gc_s.at[n, ck, 0],
            gc_r.at[n, ck, 0],
            device(1 - core, y, z, x),
        )

    def gather_pass(n, ck, buffer):
        for j in range(1, 4):
            first = ck * R + core * HALF + ((x - j + 4) % 4) * QUARTER
            piece = buffer.at[pl.ds(pl.multiple_of(first, QUARTER), QUARTER)]
            wait(piece, gx_r.at[n, ck, j - 1])
            push(
                piece,
                piece,
                gc_s.at[n, ck, j],
                gc_r.at[n, ck, j],
                device(1 - core, y, z, x),
            )

    def gather_finish(n, ck, buffer):
        for j in range(4):
            wait(buffer.at[own_rows(ck)], gc_r.at[n, ck, j])

    def out_rows(seq, ck, c_, x_):
        first = seq * LEN + ck * R + c_ * HALF + x_ * QUARTER
        return ends_out.at[pl.ds(pl.multiple_of(first, QUARTER), QUARTER)]

    def give_out(n, ck):
        src = ends_low.at[n, ck * QUARTER : (ck + 1) * QUARTER]
        dst = out_rows(z_hi, ck, core, x)
        recv = out_r.at[ck, core * 4 + x]
        target = 1 - n
        for j in range(4):
            where, send = device(target, y, z, (x + j) % 4), out_s.at[n, ck, j]
            if j == 0:
                push_or_keep(core == target, src, dst, send, recv, where)
            else:
                push(src, dst, send, recv, where)

    def out_arrived(ck):
        for c_ in range(2):
            for x_ in range(4):
                wait(out_rows(z_hi, ck, c_, x_), out_r.at[ck, c_ * 4 + x_])

    def direct_first(n, ck):
        push(
            ends_low.at[n, ck * QUARTER : (ck + 1) * QUARTER],
            out_rows(z_hi, ck, core, x),
            direct_s.at[n, ck],
            direct_r.at[ck, core],
            device(1 - n, y, (z + 2) % 4, x),
        )

    def direct_copy(n, ck, c_, j):
        rows = out_rows(1 - z_hi, ck, c_, x)
        return pltpu.make_async_remote_copy(
            src_ref=rows,
            dst_ref=rows,
            send_sem=direct2_s.at[ck, c_, j - 1],
            recv_sem=direct2_r.at[ck, c_, j - 1],
            device_id=device(1 - n, y, z, (x + j) % 4),
            device_id_type=MESH,
        )

    def direct_second(n, ck):
        @pl.when(core == 1 - n)
        def _():
            for c_ in range(2):
                wait(out_rows(1 - z_hi, ck, c_, x), direct_r.at[ck, c_])
                for j in range(1, 4):
                    direct_copy(n, ck, c_, j).start()

    def direct_end(n, ck):
        @pl.when(core == 1 - n)
        def _():
            out_arrived(ck)
            for c_ in range(2):
                for j in range(1, 4):
                    direct_copy(n, ck, c_, j).wait()

    def weight_grads(l, p):
        for i in range(4):
            cols = slice(i * BQ, (i + 1) * BQ)
            if p == 0:
                pieces = [
                    ((384, NIN), dot(xhat[l, :, cols], d_joined[:, 384:NIN], 0, 0)),
                    ((NIN, NALL), dot(grads_in[l, :, cols], joined[l], 0, 0)),
                ]
            else:
                pieces = [((0, 384), dot(xhat[l, :, cols], d_joined[:, 0:384], 0, 0))]
            for (first, last), piece in pieces:
                low = piece.astype(BF)
                for k in range(2):
                    w_grad[i, k, :, first:last] = low[k * 128 : (k + 1) * 128]

    def plane_first(l, p):
        cols = slice(*G_PARTS[p])
        for k in range(2):
            z_ = 2 * core + k
            slot = (z_ - z + 3) % 4
            src, send = w_grad.at[:, k, 0:ROWS_A, cols], p1a_s.at[l, p, k]
            other = z_ != z

            @pl.when(other)
            def _(src=src, send=send, z_=z_, slot=slot):
                pltpu.make_async_remote_copy(
                    src_ref=src,
                    dst_ref=plane_a.at[l, slot, :, :, cols],
                    send_sem=send,
                    recv_sem=p1a_r.at[l, p, slot],
                    device_id=device(core, y, z_, x),
                    device_id_type=MESH,
                ).start()

            drains.setdefault("grad", []).append((other, src, send))
        for j in range(1, 4):
            to = (y + j) % 4
            push(
                w_grad.at[to, :, ROWS_A:, cols],
                plane_b.at[l, j - 1, :, :, cols],
                p1b_s.at[l, p, j - 1],
                p1b_r.at[l, p, j - 1],
                device(core, to, z, x),
                "grad",
            )

    def plane_second(l, p):
        cols = slice(*G_PARTS[p])

        @pl.when(forwarder)
        def _():
            for j in range(3):
                wait(plane_a.at[l, j, :, :, cols], p1a_r.at[l, p, j])

            def one(y_, carry):
                summed = w_grad[y_, z_lo, 0:ROWS_A, cols].astype(F32)
                for j in range(3):
                    summed = summed + plane_a[l, j, y_, :, cols].astype(F32)
                sum_a[l, y_, :, cols] = summed.astype(BF)
                return carry

            lax.fori_loop(0, 4, one, 0)
            for j in range(4):
                to = (y + j) % 4
                src, dst = sum_a.at[l, to, :, cols], own_a.at[y, :, cols]
                copy = pltpu.make_async_remote_copy(
                    src_ref=src,
                    dst_ref=dst,
                    send_sem=p2a_s.at[l, p, j],
                    recv_sem=p2a_r.at[p, y],
                    device_id=device(l, to, z, x),
                    device_id_type=MESH,
                )
                if j == 0:
                    pl.when(core == l)(pltpu.make_async_copy(src, dst, p2a_r.at[p, y]).start)
                    pl.when(core != l)(copy.start)
                else:
                    copy.start()

        for j in range(3):
            wait(plane_b.at[l, j, :, :, cols], p1b_r.at[l, p, j])
        for k in range(2):
            summed = w_grad[y, k, ROWS_A:, cols].astype(F32)
            for j in range(3):
                summed = summed + plane_b[l, j, k, :, cols].astype(F32)
            sum_b[l, k, :, cols] = summed.astype(BF)
            z_ = 2 * core + k
            push_or_keep(
                jnp.logical_and(core == l, z_ == z),
                sum_b.at[l, k, :, cols],
                own_b.at[z, :, cols],
                p2b_s.at[l, p, k],
                p2b_r.at[p, z],
                device(l, y, z_, x),
            )

    def drain_plane():
        @pl.when(forwarder)
        def _():
            for l in range(2):
                for p, cols in enumerate(G_PARTS):
                    src = sum_a.at[l, 0, :, slice(*cols)]
                    for j in range(4):
                        ended = functools.partial(wait, src, p2a_s.at[l, p, j])
                        if j == 0:
                            pl.when(core != l)(ended)
                        else:
                            ended()

    def send_small(l):
        column_sum = jnp.zeros((1, NIN), F32)
        out_sum = jnp.zeros((1, D), F32)

        def one(i, carry):
            rows = pl.ds(pl.multiple_of(i * 128, 128), 128)
            a, b = carry
            a = a + jnp.sum(d_joined[rows, :].astype(F32), axis=0, keepdims=True)
            b = b + jnp.sum(grads_in[l, rows, :].astype(F32), axis=0, keepdims=True)
            return a, b

        column_sum, out_sum = lax.fori_loop(0, LEN // 128, one, (column_sum, out_sum))
        message[l, 0:1, 0:NIN] = column_sum
        message[l, 1:2, :] = out_sum
        here = y * 4 + z
        for y_ in range(4):
            for k in range(2):
                z_ = 2 * core + k
                own = jnp.logical_and(core == l, jnp.logical_and(y_ == y, z_ == z))
                push_or_keep(
                    own,
                    message.at[l],
                    messages.at[here],
                    msg_s.at[l, y_ * 2 + k],
                    msg_r.at[here],
                    device(l, y_, z_, x),
                )

    def small_first():
        for k in range(16):
            wait(messages.at[k], msg_r.at[k])
        summed = messages[0]
        for k in range(1, 16):
            summed = summed + messages[k]
        small[...] = summed
        for j in range(1, 4):
            push(
                small,
                small_ring.at[j - 1],
                ln1_s.at[j - 1],
                ln1_r.at[j - 1],
                device(core, y, z, (x + j) % 4),
            )
        for n in range(3):
            g_qkv_b[n] = summed[0:1, n * 128 : (n + 1) * 128]
        g_up_b[...] = summed[0:1, 384:NIN]
        g_out_b[...] = summed[1:2, :]

    def small_second():
        for j in range(3):
            wait(small_ring.at[j], ln1_r.at[j])
        small_sum[...] = small[...] + small_ring[0] + small_ring[1] + small_ring[2]
        push(small_sum, small_far, ln2_s, ln2_r, device(core, y, (z + 2) % 4, x))

    def small_third():
        wait(small_far, ln2_r)
        both = small_sum[...] + small_far[...]
        for k in range(2):
            g_gains[k : k + 1, :] = both[2 + k : 3 + k, :] / gains[k : k + 1, :]
            g_offsets[k : k + 1, :] = both[4 + k : 5 + k, :] / gains[k : k + 1, :]

    def after_first_layer(ck):
        rows = own_rows(ck)
        mid = slice(ck * QUARTER, (ck + 1) * QUARTER)
        result = x_own[mid, :].astype(F32) + reduce_finish(0, ck) + out_row[0]
        low = result.astype(BF)
        y_mid[ck * QUARTER : (ck + 1) * QUARTER, :] = low
        xhat[1, rows, :] = standardize(low.astype(F32))[0].astype(BF)
        gather_send(0, ck, xhat.at[1])

    def after_second_layer(ck):
        mid = slice(ck * QUARTER, (ck + 1) * QUARTER)
        result = y_mid[mid, :].astype(F32) + reduce_finish(1, ck) + out_row[1]
        ends_low[0, mid, :] = result.astype(BF)

    def through_norm(stream, grad, e):
        scaled, inverse = standardize(stream)
        return grad + inverse * (
            e
            - jnp.mean(e, axis=-1, keepdims=True)
            - scaled * jnp.mean(e * scaled, axis=-1, keepdims=True)
        )

    def input_grad_middle(ck):
        mid = slice(ck * QUARTER, (ck + 1) * QUARTER)
        rows = own_rows(ck)
        e = reduce_finish(2, ck)
        moved = through_norm(y_mid[mid, :].astype(F32), grads_in[1, rows, :].astype(F32), e)
        grads_in[0, rows, :] = moved.astype(BF)
        gather_send(1, ck, grads_in.at[0])

    def input_grad_first(ck):
        mid = slice(ck * QUARTER, (ck + 1) * QUARTER)
        rows = own_rows(ck)
        e = reduce_finish(3, ck)
        moved = through_norm(x_own[mid, :].astype(F32), grads_in[0, rows, :].astype(F32), e)
        ends_low[1, mid, :] = moved.astype(BF)

    project_all(0, 0)
    attend_all(0, 0)
    gather_rest(0, 1)
    reduce_send(0, 0, functools.partial(branch, 0))
    gather_second(1, 0)
    project_all(0, 1)
    attend_all(0, 1)
    reduce_send(0, 1, functools.partial(branch, 0))
    after_first_layer(0)
    after_first_layer(1)
    gather_pass(0, 0, xhat.at[1])
    gather_rest(1, 0)
    gather_finish(0, 0, xhat.at[1])
    project_all(1, 0)
    gather_pass(0, 1, xhat.at[1])
    attend_all(1, 0)
    reduce_send(1, 0, functools.partial(branch, 1))
    gather_finish(0, 1, xhat.at[1])
    project_all(1, 1)
    attend_all(1, 1)
    reduce_send(1, 1, functools.partial(branch, 1))

    wait(mine, swap_s)
    backward_first(1, 1)
    backward_first(1, 0)
    after_second_layer(0)
    direct_first(0, 0)
    give_out(0, 0)
    weight_grads(1, 0)
    plane_first(1, 0)
    after_second_layer(1)
    direct_first(0, 1)
    give_out(0, 1)
    backward_second(1, 1)
    reduce_send(2, 1, functools.partial(norm_grad, 1))
    backward_second(1, 0)
    reduce_send(2, 0, functools.partial(norm_grad, 1))
    input_grad_middle(1)
    weight_grads(1, 1)
    plane_first(1, 1)
    input_grad_middle(0)
    gather_pass(1, 1, grads_in.at[0])
    direct_second(0, 0)
    direct_second(0, 1)
    send_small(1)
    plane_second(1, 0)
    gather_finish(1, 1, grads_in.at[0])

    backward_first(0, 1)
    gather_pass(1, 0, grads_in.at[0])
    backward_second(0, 1)
    reduce_send(3, 1, functools.partial(norm_grad, 0))
    gather_finish(1, 0, grads_in.at[0])
    backward_first(0, 0)
    plane_second(1, 1)
    drain("grad")
    weight_grads(0, 0)
    plane_first(0, 0)
    backward_second(0, 0)
    reduce_send(3, 0, functools.partial(norm_grad, 0))
    input_grad_first(1)
    direct_first(1, 1)
    give_out(1, 1)
    weight_grads(0, 1)
    plane_first(0, 1)
    send_small(0)
    input_grad_first(0)
    direct_first(1, 0)
    give_out(1, 0)
    direct_second(1, 1)
    plane_second(0, 0)
    small_first()
    direct_second(1, 0)
    plane_second(0, 1)
    small_second()

    for k in range(4):
        for p, cols in enumerate(G_PARTS):
            wait(own_a.at[k, :, slice(*cols)], p2a_r.at[p, k])
            wait(own_b.at[k, :, slice(*cols)], p2b_r.at[p, k])
    total[0:ROWS_A, :] = (
        own_a[0].astype(F32) + own_a[1].astype(F32) + own_a[2].astype(F32) + own_a[3].astype(F32)
    )
    total[ROWS_A:128, :] = (
        own_b[0].astype(F32) + own_b[1].astype(F32) + own_b[2].astype(F32) + own_b[3].astype(F32)
    )
    for n in range(7):
        k = 0 if n < 3 else 1
        cols = slice(n * 128, (n + 1) * 128)
        grad = total[:, cols] * gain_cols[k] + offset_cols[k] * small[0:1, cols]
        if n < 3:
            g_qkv[n] = grad
        else:
            g_up[:, (n - 3) * 128 : (n - 2) * 128] = grad
    g_dense[...] = total[:, NIN : NIN + 128].T
    g_down[...] = total[:, NIN + 128 : NALL].T
    small_third()
    direct_end(0, 0)
    direct_end(0, 1)
    direct_end(1, 1)
    direct_end(1, 0)
    drain("grad")
    for ck in range(NCH):
        drain(("part", ck))
    drain("end")
    drain_first()
    drain_second()
    drain_extra()
    drain_plane()


def settle(*refs):
    count = (len(refs) - 2) // 3
    sources, targets, held = refs[:count], refs[count : 2 * count], refs[2 * count : 3 * count]
    sem_in, sem_out = refs[-2:]
    trips = []
    rows = sources[0].shape[0] // 8
    for k in range(8):
        piece = pl.ds(k * rows, rows)
        trips.append((sources[0].at[piece], held[0].at[piece], targets[0].at[piece]))
    for n in range(1, count):
        trips.append((sources[n], held[n], targets[n]))
    arrivals = []
    departures = []
    for n, (source, stop, target) in enumerate(trips):
        arrivals.append(pltpu.make_async_copy(source, stop, sem_in.at[n]))
        departures.append(pltpu.make_async_copy(stop, target, sem_out.at[n]))
    for copy in arrivals:
        copy.start()
    for arrival, departure in zip(arrivals, departures):
        arrival.wait()
        departure.start()
    for copy in departures:
        copy.wait()


def body(ends_in, ln_gains, ln_biases, qkv_w, qkv_bias, dense_w, up_w, up_bias, down_w, out_bias):
    cosine, sine = rotary_tables()
    vmem = pl.BlockSpec(memory_space=pltpu.VMEM)
    anywhere = pl.BlockSpec(memory_space=pl.ANY)

    def shape(*dims):
        return jax.ShapeDtypeStruct(dims, F32)

    def sems(*dims):
        return pltpu.SemaphoreType.DMA(dims)

    outs = pl.pallas_call(
        kernel,
        out_shape=[
            jax.ShapeDtypeStruct((2 * LEN, D), BF),
            shape(2, D),
            shape(2, D),
            shape(3, 128, 128),
            shape(3, 1, 128),
            shape(128, 128),
            shape(128, 512),
            shape(1, 512),
            shape(512, 128),
            shape(1, D),
        ],
        in_specs=[anywhere] + [vmem] * 11,
        out_specs=[vmem] * 10,
        scratch_shapes=[
            pltpu.VMEM((128, NALL), BF),
            pltpu.VMEM((8, 256), F32),
            pltpu.VMEM((2, 8, 8, 256), F32),
            pltpu.VMEM((2, 1, 1024), F32),
            pltpu.VMEM((2, 1, 1024), F32),
            pltpu.VMEM((2, D, NALL), BF),
            pltpu.VMEM((LEN, D), BF),
            pltpu.VMEM((2, LEN, D), BF),
            pltpu.VMEM((2, LEN, D), BF),
            pltpu.VMEM((LEN // 8, D), BF),
            pltpu.VMEM((LEN // 8, D), BF),
            pltpu.VMEM((2, LEN, NOUT), BF),
            pltpu.VMEM((2, LEN, 512), BF),
            pltpu.VMEM((2, LEN, 128), BF),
            pltpu.VMEM((2, LEN, 128), BF),
            pltpu.VMEM((2, LEN, 128), BF),
            pltpu.VMEM((2, 128, LEN), BF),
            pltpu.VMEM((128, LEN), BF),
            pltpu.VMEM((2, 10, BQ, 2 * BQ), BF),
            pltpu.VMEM((2, LEN // BQ, 2 * BQ), F32),
            pltpu.VMEM((2, 128, LEN), F32),
            pltpu.VMEM((LEN, 2 * BQ), F32),
            pltpu.VMEM((LEN, 128), BF),
            pltpu.VMEM((LEN, NIN), BF),
            pltpu.VMEM((2, LEN // 2, D), BF),
            pltpu.VMEM((2, 3, LEN // 8, D), BF),
            pltpu.VMEM((2, LEN // 8, D), BF),
            pltpu.VMEM((4, 2, 128, NALL), BF),
            pltpu.VMEM((2, 3, 4, ROWS_A, NALL), BF),
            pltpu.VMEM((2, 3, 2, ROWS_B, NALL), BF),
            pltpu.VMEM((2, 4, ROWS_A, NALL), BF),
            pltpu.VMEM((2, 2, ROWS_B, NALL), BF),
            pltpu.VMEM((4, ROWS_A, NALL), BF),
            pltpu.VMEM((4, ROWS_B, NALL), BF),
            pltpu.VMEM((128, NALL), F32),
            pltpu.VMEM((2, 8, D), F32),
            pltpu.VMEM((16, 8, D), F32),
            pltpu.VMEM((8, D), F32),
            pltpu.VMEM((3, 8, D), F32),
            pltpu.VMEM((8, D), F32),
            pltpu.VMEM((8, D), F32),
            pltpu.SemaphoreType.DMA,
            pltpu.SemaphoreType.DMA,
            pltpu.SemaphoreType.DMA,
            sems(2, 2, 4),
            sems(2, 2, 2, 8),
            sems(2, 2, 4, 3),
            sems(2, 2, 2, 3),
            sems(16),
            sems(2, 8),
            sems(4, NCH, NB),
            sems(4, NCH, NB),
            sems(4, NCH, 3),
            sems(4, NCH, 3),
            sems(2, NCH, 3),
            sems(2, NCH, 3),
            sems(2, NCH, 4),
            sems(2, NCH, 4),
            sems(2, NCH, 4),
            sems(NCH, 8),
            sems(2, NCH),
            sems(NCH, 2),
            sems(NCH, 2, 3),
            sems(NCH, 2, 3),
            sems(2, 8),
            sems(16),
            sems(2, 2, 2),
            sems(2, 2, 3),
            sems(2, 2, 3),
            sems(2, 2, 3),
            sems(2, 2, 4),
            sems(2, 4),
            sems(2, 2, 2),
            sems(2, 4),
            sems(3),
            sems(3),
            pltpu.SemaphoreType.DMA,
            pltpu.SemaphoreType.DMA,
        ],
        compiler_params=pltpu.CompilerParams(
            collective_id=0, has_side_effects=True, vmem_limit_bytes=63 * 2**20
        ),
        cost_estimate=pl.CostEstimate(
            flops=22 * 10**9, bytes_accessed=20 * 10**6, transcendentals=4 * 10**6
        ),
    )(
        ends_in[0],
        qkv_w[0],
        dense_w[0],
        up_w[0],
        down_w[0],
        ln_gains[0],
        ln_biases[0],
        jnp.transpose(qkv_bias, (1, 0, 2)),
        up_bias,
        out_bias,
        jnp.asarray(cosine),
        jnp.asarray(sine),
    )
    outs = pl.pallas_call(
        settle,
        out_shape=[jax.ShapeDtypeStruct(out.shape, out.dtype) for out in outs],
        in_specs=[anywhere] * len(outs),
        out_specs=[anywhere] * len(outs),
        scratch_shapes=[pltpu.VMEM(out.shape, out.dtype) for out in outs]
        + [sems(len(outs) + 7), sems(len(outs) + 7)],
        compiler_params=pltpu.CompilerParams(vmem_limit_bytes=63 * 2**20),
        cost_estimate=pl.CostEstimate(flops=0, bytes_accessed=10 * 10**6, transcendentals=0),
    )(*outs)
    out, gains, offsets, d_qkv, d_qkv_b, d_dense, d_up, d_up_b, d_down, d_out_b = outs
    return (
        out[None],
        gains[None],
        offsets[None],
        d_qkv[None],
        jnp.transpose(d_qkv_b, (1, 0, 2)),
        d_dense[None],
        d_up[None],
        d_up_b,
        d_down[None],
        d_out_b,
    )


def solution(mesh):
    in_specs = (
        P("section", "dp", None),
        P("section", None, None),
        P("section", None, None),
        P("section", None, "dp", "tensor"),
        P("section", None, "tensor"),
        P("section", "tensor", "dp"),
        P("section", "dp", "tensor"),
        P("section", "tensor"),
        P("section", "tensor", "dp"),
        P("section", None),
    )
    out_specs = (
        P("section", "dp", None),
        P("section", None, None),
        P("section", None, None),
        P("section", None, "dp", "tensor"),
        P("section", None, "tensor"),
        P("section", "tensor", "dp"),
        P("section", "dp", "tensor"),
        P("section", "tensor"),
        P("section", "tensor", "dp"),
        P("section", None),
    )
    return jax.shard_map(body, mesh=mesh, in_specs=in_specs, out_specs=out_specs, check_vma=False)
```

```python
import functools

import jax
import jax.numpy as jnp
import numpy as np
from jax import lax
from jax.experimental import pallas as pl
from jax.experimental.pallas import tpu as pltpu
from jax.sharding import PartitionSpec as P

MESH = pl.DeviceIdType.MESH
BF = jnp.bfloat16
F32 = jnp.float32

D = 1024
LEN = 1024
HD = 64
ROT = 16
NIN = 896
NOUT = 640
NALL = NIN + NOUT
BQ = 256
NCH = 2
R = LEN // NCH
HALF = R // 2
QUARTER = R // 8
BM = min(256, HALF)
NB = HALF // BM
W_PARTS = (((0, NIN), (NIN, NALL)), ((0, NALL),))
G_PARTS = ((384, NALL), (0, 384))
ROWS_A = 48
ROWS_B = 128 - ROWS_A


def dot(a, b, ca, cb):
    return lax.dot_general(a, b, (((ca,), (cb,)), ((), ())), preferred_element_type=F32)


def rotary_tables():
    position = np.arange(LEN, dtype=np.float32)[:, None]
    exponent = np.arange(ROT // 2, dtype=np.float32) * np.float32(2.0) / np.float32(ROT)
    angles = (position * np.float32(10000.0) ** (-exponent)).astype(np.float32)
    cosine = np.ones((LEN, 2 * HD), np.float32)
    sine = np.zeros((LEN, 2 * HD), np.float32)
    for first in (0, 8, HD, HD + 8):
        cosine[:, first : first + 8] = np.cos(angles)
        sine[:, first : first + 8] = np.sin(angles)
    return cosine, sine


def lanes_of_head(shape):
    return lax.broadcasted_iota(jnp.int32, shape, 1) % HD


def turn(value, cosine, sine):
    lane = lanes_of_head(value.shape)
    partner = jnp.where(lane < 8, -pltpu.roll(value, 120, 1), pltpu.roll(value, 8, 1))
    return value * cosine + partner * sine


def turn_back(grad, cosine, sine):
    lane = lanes_of_head(grad.shape)
    moved = grad * sine
    partner = jnp.where(
        lane < 8, pltpu.roll(moved, 120, 1), jnp.where(lane < 16, -pltpu.roll(moved, 8, 1), 0.0)
    )
    return grad * cosine + partner


def gelu_and_slope(hidden):
    bell = jnp.exp(-0.5 * hidden * hidden)
    size = 1.0 + (0.3275911 * 0.7071067811865476) * jnp.abs(hidden)
    t = pltpu.reciprocal(size, approx=True)
    t = t * (2.0 - size * t)
    series = t * (
        0.254829592 * 0.5
        + t
        * (
            -0.284496736 * 0.5
            + t * (1.421413741 * 0.5 + t * (-1.453152027 * 0.5 + t * (1.061405429 * 0.5)))
        )
    )
    tail = series * bell
    below = jnp.where(hidden >= 0.0, 1.0 - tail, tail)
    return hidden * below, below + hidden * bell * 0.3989422804014327


def standardize(value):
    center = jnp.mean(value, axis=-1, keepdims=True)
    centred = value - center
    inverse = lax.rsqrt(jnp.mean(centred * centred, axis=-1, keepdims=True) + 1e-05)
    return centred * inverse, inverse


def stack_heads(value):
    lane = lax.broadcasted_iota(jnp.int32, value.shape, 1)
    wide = value.astype(F32)
    return jnp.concatenate(
        [jnp.where(lane < HD, wide, 0.0), jnp.where(lane >= HD, wide, 0.0)], axis=0
    ).astype(BF)


def split_heads(value):
    half = value.shape[1] // 2
    return jnp.concatenate([value[:HD, :half], value[HD:, half:]], axis=0)


def pair(i, j):
    return i * (i + 1) // 2 + j


def kernel(
    ends,
    qkv,
    dense,
    up,
    down,
    gains,
    offsets,
    qkv_b,
    up_b,
    out_b,
    cosine,
    sine,
    ends_out,
    g_gains,
    g_offsets,
    g_qkv,
    g_qkv_b,
    g_dense,
    g_up,
    g_up_b,
    g_down,
    g_out_b,
    shard,
    extra,
    extras,
    bias_row,
    out_row,
    weights,
    x_in,
    grads_in,
    xhat,
    y_mid,
    x_own,
    joined,
    slope,
    queries,
    keys,
    values,
    keys_t,
    values_t,
    soft,
    soft_scale,
    context_t,
    scores,
    d_context,
    d_joined,
    core_part,
    ring_part,
    ends_low,
    w_grad,
    plane_a,
    plane_b,
    sum_a,
    sum_b,
    own_a,
    own_b,
    total,
    message,
    messages,
    small,
    small_ring,
    small_sum,
    small_far,
    local_sem,
    swap_s,
    swap_r,
    w1_s,
    w_r,
    w2a_s,
    w2b_s,
    extra_s,
    extra_r,
    core_s,
    core_r,
    ring_s,
    ring_r,
    gx_s,
    gx_r,
    gc_s,
    gc_r,
    out_s,
    out_r,
    direct_s,
    direct_r,
    direct2_s,
    direct2_r,
    msg_s,
    msg_r,
    p1a_s,
    p1a_r,
    p1b_s,
    p1b_r,
    p2a_s,
    p2a_r,
    p2b_s,
    p2b_r,
    ln1_s,
    ln1_r,
    ln2_s,
    ln2_r,
):
    part = x_in
    core = lax.axis_index("section")
    dp = lax.axis_index("dp")
    t = lax.axis_index("tensor")
    y, z_lo = dp // 2, dp % 2
    z_hi, x = t // 4, t % 4
    z = 2 * z_hi + z_lo
    forwarder = core == z_hi

    def device(c_, y_, z_, x_):
        return {"section": c_, "dp": y_ * 2 + z_ % 2, "tensor": (z_ // 2) * 4 + x_}

    drains = {}

    def wait(ref, sem):
        pltpu.make_async_copy(ref, ref, sem).wait()

    def push(src, dst, send, recv, where, tag="end"):
        pltpu.make_async_remote_copy(
            src_ref=src, dst_ref=dst, send_sem=send, recv_sem=recv, device_id=where, device_id_type=MESH
        ).start()
        drains.setdefault(tag, []).append((None, src, send))

    def push_or_keep(own, src, dst, send, recv, where):
        other = jnp.logical_not(own)

        @pl.when(own)
        def _():
            pltpu.make_async_copy(src, dst, recv).start()

        @pl.when(other)
        def _():
            pltpu.make_async_remote_copy(
                src_ref=src,
                dst_ref=dst,
                send_sem=send,
                recv_sem=recv,
                device_id=where,
                device_id_type=MESH,
            ).start()

        drains.setdefault("end", []).append((other, src, send))

    def drain(tag):
        for condition, src, send in drains.pop(tag, []):
            if condition is None:
                wait(src, send)
            else:
                pl.when(condition)(functools.partial(wait, src, send))

    barrier = pltpu.get_barrier_semaphore()
    for dy in range(4):
        for dz in range(4):
            for c_ in range(2):
                if (dy, dz, c_) == (0, 0, 0):
                    continue
                pl.semaphore_signal(
                    barrier,
                    inc=1,
                    device_id=device((core + c_) % 2, (y + dy) % 4, (z + dz) % 4, x),
                    device_id_type=MESH,
                )
    for j in range(1, 4):
        pl.semaphore_signal(
            barrier, inc=1, device_id=device(core, y, z, (x + j) % 4), device_id_type=MESH
        )

    block = pl.ds(pl.multiple_of(dp * 128, 128), 128)

    def column(row):
        return jnp.broadcast_to(row, (128, 128)).T

    gain_cols = [column(gains[k : k + 1, block]) for k in range(2)]
    offset_cols = [column(offsets[k : k + 1, block]) for k in range(2)]

    def raw_tile(n):
        if n < 3:
            return qkv[n].astype(F32), 0, qkv_b[n]
        cols = slice((n - 3) * 128, (n - 2) * 128)
        return up[:, cols].astype(F32), 1, up_b[:, cols]

    extra[...] = jnp.zeros_like(extra)
    message[...] = jnp.zeros_like(message)
    for n in range(7):
        tile, k, bias = raw_tile(n)
        shard[:, n * 128 : (n + 1) * 128] = (tile * gain_cols[k]).astype(BF)
        added = jnp.sum(tile * offset_cols[k], axis=0, keepdims=True) + 0.125 * bias
        extra[n // 2 : n // 2 + 1, (n % 2) * 128 : (n % 2) * 128 + 128] = added
    for n in range(4):
        extra[4 + n : 5 + n, :] = 0.125 * out_b[:, n * 256 : (n + 1) * 256]
    shard[:, NIN : NIN + 128] = dense[...].T
    shard[:, NIN + 128 : NALL] = down[...].T

    pl.semaphore_wait(barrier, 34)

    mine = ends.at[pl.ds(pl.multiple_of(z_hi * LEN, LEN), LEN)]
    for c_, buffer in ((0, x_in), (1, grads_in.at[1])):

        @pl.when(core == c_)
        def _(buffer=buffer):
            pltpu.make_async_copy(mine, buffer, local_sem).start()
            pltpu.make_async_remote_copy(
                src_ref=mine,
                dst_ref=buffer,
                send_sem=swap_s,
                recv_sem=swap_r,
                device_id=device(1 - core, y, z, x),
                device_id_type=MESH,
            ).start()

    def w_rows(l, p, dp_, half):
        rows = pl.ds(pl.multiple_of(dp_ * 128 + half * 64, 64), 64)
        return weights.at[l, rows, slice(*W_PARTS[l][p])]

    def gather_first(l):
        @pl.when(core == l)
        def _():
            for p, cols in enumerate(W_PARTS[l]):
                for half in range(2):
                    src = shard.at[half * 64 : half * 64 + 64, slice(*cols)]
                    dst = w_rows(l, p, dp, half)
                    recv = w_r.at[half, l, p, dp]

                    @pl.when(forwarder)
                    def _(src=src, dst=dst, recv=recv):
                        pltpu.make_async_copy(src, dst, recv).start()

                    for j in range(4):
                        if half == 0:
                            where = device(z_hi, (y + j) % 4, z, x)
                        else:
                            where = device(z_hi, y, (z + j) % 4, x)
                        copy = pltpu.make_async_remote_copy(
                            src_ref=src,
                            dst_ref=dst,
                            send_sem=w1_s.at[p, half, j],
                            recv_sem=recv,
                            device_id=where,
                            device_id_type=MESH,
                        )
                        if j == 0:
                            pl.when(jnp.logical_not(forwarder))(copy.start)
                        else:
                            copy.start()

    def drain_first():
        for l in range(2):

            @pl.when(core == l)
            def _(l=l):
                for p, cols in enumerate(W_PARTS[l]):
                    src = shard.at[0:64, slice(*cols)]
                    for half in range(2):
                        for j in range(4):
                            ended = functools.partial(wait, src, w1_s.at[p, half, j])
                            if j == 0:
                                pl.when(jnp.logical_not(forwarder))(ended)
                            else:
                                ended()

    def gather_second(l, p):
        for k in range(2):
            block_b = w_rows(l, p, y * 2 + k, 1)
            wait(block_b, w_r.at[1, l, p, y * 2 + k])
            for j in range(1, 4):
                push(
                    block_b,
                    block_b,
                    w2b_s.at[l, p, k, j - 1],
                    w_r.at[1, l, p, y * 2 + k],
                    device(core, (y + j) % 4, z, x),
                    ("w", l, p),
                )

        @pl.when(forwarder)
        def _():
            for y_ in range(4):
                dp_ = y_ * 2 + z_lo
                block_a = w_rows(l, p, dp_, 0)
                wait(block_a, w_r.at[0, l, p, dp_])
                for j in range(1, 4):
                    pltpu.make_async_remote_copy(
                        src_ref=block_a,
                        dst_ref=block_a,
                        send_sem=w2a_s.at[l, p, y_, j - 1],
                        recv_sem=w_r.at[0, l, p, dp_],
                        device_id=device(core, y, (z + j) % 4, x),
                        device_id_type=MESH,
                    ).start()

    def drain_second(l, p):
        drain(("w", l, p))

        @pl.when(forwarder)
        def _():
            for y_ in range(4):
                for j in range(3):
                    wait(w_rows(l, p, 0, 0), w2a_s.at[l, p, y_, j])

    def gather_rest(l, p):
        for j in range(1, 4):
            for k in range(2):
                dp_ = ((y + j) % 4) * 2 + k
                wait(w_rows(l, p, dp_, 1), w_r.at[1, l, p, dp_])
        for y_ in range(4):
            dp_ = y_ * 2 + 1 - z_lo
            wait(w_rows(l, p, dp_, 0), w_r.at[0, l, p, dp_])

            @pl.when(jnp.logical_not(forwarder))
            def _(dp_=y_ * 2 + z_lo):
                wait(w_rows(l, p, dp_, 0), w_r.at[0, l, p, dp_])

        if p > 0:
            return
        for dp_ in range(8):
            wait(extras.at[l, dp_], extra_r.at[l, dp_])
        summed = extras[l, 0]
        for dp_ in range(1, 8):
            summed = summed + extras[l, dp_]
        for n in range(4):
            bias_row[l, :, n * 256 : (n + 1) * 256] = summed[n : n + 1, :]
            out_row[l, :, n * 256 : (n + 1) * 256] = summed[4 + n : 5 + n, :]

    gather_first(0)
    for l in range(2):

        @pl.when(core == l)
        def _(l=l):
            for dy in range(4):
                for dz in range(4):
                    where = device(z_hi, (y + dy) % 4, (z + dz) % 4, x)
                    dst = extras.at[l, dp]
                    recv = extra_r.at[l, dp]
                    copy = pltpu.make_async_remote_copy(
                        src_ref=extra,
                        dst_ref=dst,
                        send_sem=extra_s.at[dy * 4 + dz],
                        recv_sem=recv,
                        device_id=where,
                        device_id_type=MESH,
                    )
                    if (dy, dz) == (0, 0):
                        pl.when(forwarder)(pltpu.make_async_copy(extra, dst, recv).start)
                        pl.when(jnp.logical_not(forwarder))(copy.start)
                    else:
                        copy.start()

    def drain_extra():
        for k in range(16):
            if k == 0:
                pl.when(jnp.logical_not(forwarder))(
                    functools.partial(wait, extra, extra_s.at[k])
                )
            else:
                wait(extra, extra_s.at[k])

    wait(x_in, local_sem)
    wait(x_in, swap_r)

    gather_second(0, 0)

    def normalize_rows(i, carry):
        rows = pl.ds(pl.multiple_of(i * 128, 128), 128)
        xhat[0, rows, :] = standardize(x_in[rows, :].astype(F32))[0].astype(BF)
        return carry

    lax.fori_loop(0, LEN // 128, normalize_rows, 0)
    for ck in range(NCH):
        first = ck * R + core * HALF + x * QUARTER
        x_own[ck * QUARTER : (ck + 1) * QUARTER, :] = x_in[
            pl.ds(pl.multiple_of(first, QUARTER), QUARTER), :
        ]
    drain_second(0, 0)
    gather_second(0, 1)
    gather_first(1)
    gather_rest(0, 0)

    def project(l, i):
        rows = pl.ds(pl.multiple_of(i * BQ, BQ), BQ)
        low = xhat[l, rows, :]
        raw = dot(low, weights[l, :, 0:384], 1, 0) + bias_row[l, :, 0:384]
        cos_rows, sin_rows = cosine[rows, :], sine[rows, :]
        q = turn(raw[:, 0:128], cos_rows, sin_rows) * HD**-0.5
        k = turn(raw[:, 128:256], cos_rows, sin_rows)
        v = raw[:, 256:384]
        queries[l, rows, :] = q.astype(BF)
        keys[l, rows, :] = k.astype(BF)
        values[l, rows, :] = v.astype(BF)
        keys_t[l, :, rows] = k.T.astype(BF)
        values_t[:, rows] = v.T.astype(BF)
        hidden = dot(low, weights[l, :, 384:NIN], 1, 0) + bias_row[l, :, 384:NIN]
        act, gradient = gelu_and_slope(hidden)
        joined[l, rows, 128:NOUT] = act.astype(BF)
        slope[l, rows, :] = gradient.astype(BF)

    def attend(l, i):
        rows = slice(i * BQ, (i + 1) * BQ)
        stacked = stack_heads(queries[l, rows, :])
        largest = None
        for j in range(i + 1):
            tile = dot(keys[l, j * BQ : (j + 1) * BQ, :], stacked, 1, 1)
            if j == i:
                key_at = lax.broadcasted_iota(jnp.int32, tile.shape, 0)
                query_at = lax.broadcasted_iota(jnp.int32, tile.shape, 1) % BQ
                tile = jnp.where(key_at <= query_at, tile, -1e30)
            scores[j * BQ : (j + 1) * BQ, :] = tile
            top = jnp.max(tile, axis=0, keepdims=True)
            largest = top if largest is None else jnp.maximum(largest, top)
        summed = jnp.zeros((1, 2 * BQ), F32)
        outcome = jnp.zeros((2 * HD, 2 * BQ), F32)
        for j in range(i + 1):
            terms = jnp.exp(scores[j * BQ : (j + 1) * BQ, :] - largest)
            summed = summed + jnp.sum(terms, axis=0, keepdims=True)
            low = terms.astype(BF)
            soft[l, pair(i, j)] = low
            outcome = outcome + dot(values_t[:, j * BQ : (j + 1) * BQ], low, 1, 0)
        scale = 1.0 / summed
        soft_scale[l, i : i + 1, :] = scale
        context = split_heads(outcome * scale)
        context_t[l, :, rows] = context
        joined[l, rows, 0:128] = context.T.astype(BF)

    def attend_back(l, i):
        rows = slice(i * BQ, (i + 1) * BQ)
        grad_t = d_context[rows, :].astype(F32).T
        scale = soft_scale[l, i : i + 1, :]
        top = grad_t[:HD] * scale[:, :BQ]
        bottom = grad_t[HD:] * scale[:, BQ:]
        context = context_t[l, :, rows]
        delta = jnp.concatenate(
            [
                jnp.sum(context[:HD] * top, axis=0, keepdims=True),
                jnp.sum(context[HD:] * bottom, axis=0, keepdims=True),
            ],
            axis=1,
        )
        blank = jnp.zeros_like(top)
        spread_wide = jnp.concatenate(
            [jnp.concatenate([top, blank], axis=1), jnp.concatenate([blank, bottom], axis=1)], axis=0
        )
        spread_t = spread_wide.astype(BF)
        spread = spread_wide.T.astype(BF)
        stacked = stack_heads(queries[l, rows, :])
        d_query_t = jnp.zeros((2 * HD, 2 * BQ), F32)
        for j in range(i + 1):
            cols = slice(j * BQ, (j + 1) * BQ)
            terms = soft[l, pair(i, j)]
            d_terms = dot(values[l, cols, :], spread_t, 1, 0)
            d_scores = (terms.astype(F32) * (d_terms - delta)).astype(BF)
            d_key = dot(d_scores, stacked, 1, 0)
            d_value = dot(terms, spread, 1, 0)
            if i == LEN // BQ - 1:
                scores[cols, 0:128] = d_key
                scores[cols, 128:256] = d_value
            else:
                scores[cols, 0:128] += d_key
                scores[cols, 128:256] += d_value
            d_query_t = d_query_t + dot(keys_t[l, :, cols], d_scores, 1, 0)
        d_query = split_heads(d_query_t).T * HD**-0.5
        d_joined[rows, 0:128] = turn_back(d_query, cosine[rows, :], sine[rows, :]).astype(BF)

    def finish_keys(i, carry):
        rows = pl.ds(pl.multiple_of(i * BQ, BQ), BQ)
        d_joined[rows, 128:256] = turn_back(scores[rows, 0:128], cosine[rows, :], sine[rows, :]).astype(
            BF
        )
        d_joined[rows, 256:384] = scores[rows, 128:256].astype(BF)
        return carry

    def blocks_of(ck):
        return range(ck * R // BQ, (ck + 1) * R // BQ)

    def project_all(l, ck):
        def one(i, carry):
            project(l, i)
            return carry

        lax.fori_loop(ck * R // BQ, (ck + 1) * R // BQ, one, 0)

    def attend_all(l, ck):
        for i in blocks_of(ck):
            attend(l, i)

    def backward_first(l, ck):
        def one(i, carry):
            rows = pl.ds(pl.multiple_of(i * BQ, BQ), BQ)
            both = dot(grads_in[l, rows, :], weights[l, :, NIN:NALL], 1, 0)
            d_context[rows, :] = both[:, 0:128].astype(BF)
            d_joined[rows, 384:NIN] = (both[:, 128:NOUT] * slope[l, rows, :].astype(F32)).astype(BF)
            return carry

        lax.fori_loop(ck * R // BQ, (ck + 1) * R // BQ, one, 0)

    def backward_second(l, ck):
        for i in reversed(blocks_of(ck)):
            attend_back(l, i)
        lax.fori_loop(ck * R // BQ, (ck + 1) * R // BQ, finish_keys, 0)

    def branch(l, rows):
        return dot(joined[l, rows, :], weights[l, :, NIN:NALL], 1, 1)

    def norm_grad(l, rows):
        shares = [
            dot(d_joined[rows, 0:384], weights[l, :, 0:384], 1, 1),
            dot(d_joined[rows, 384:NIN], weights[l, :, 384:NIN], 1, 1),
        ]
        scaled = xhat[l, rows, :].astype(F32)
        for k, e in enumerate(shares):
            message[l, 2 + k : 3 + k, :] += jnp.sum(scaled * e, axis=0, keepdims=True)
            message[l, 4 + k : 5 + k, :] += jnp.sum(e, axis=0, keepdims=True)
        return shares[0] + shares[1]

    def own_rows(ck, part_=None):
        first = ck * R + core * HALF + x * QUARTER
        return pl.ds(pl.multiple_of(first, QUARTER), QUARTER)

    def reduce_send(ph, ck, term):
        slot = ph % 2
        drain(("part", ck))
        for b in range(NB):
            rows = pl.ds(pl.multiple_of(ck * R + (1 - core) * HALF + b * BM, BM), BM)
            part[rows, :] = term(rows).astype(BF)
            push(
                part.at[rows],
                core_part.at[slot, ck * HALF + b * BM : ck * HALF + (b + 1) * BM],
                core_s.at[ph, ck, b],
                core_r.at[ph, ck, b],
                device(1 - core, y, z, x),
                ("part", ck),
            )
        for b in range(NB):
            rows = pl.ds(pl.multiple_of(ck * R + core * HALF + b * BM, BM), BM)
            value = term(rows)
            other = core_part.at[slot, ck * HALF + b * BM : ck * HALF + (b + 1) * BM]
            wait(other, core_r.at[ph, ck, b])
            part[rows, :] = (value + other[...].astype(F32)).astype(BF)
        for j in range(1, 4):
            to = (x + j) % 4
            first = ck * R + core * HALF + to * QUARTER
            push(
                part.at[pl.ds(pl.multiple_of(first, QUARTER), QUARTER)],
                ring_part.at[slot, j - 1, ck * QUARTER : (ck + 1) * QUARTER],
                ring_s.at[ph, ck, j - 1],
                ring_r.at[ph, ck, j - 1],
                device(core, y, z, to),
                ("part", ck),
            )

    def reduce_finish(ph, ck):
        slot = ph % 2
        summed = part[own_rows(ck), :].astype(F32)
        for j in range(3):
            piece = ring_part.at[slot, j, ck * QUARTER : (ck + 1) * QUARTER]
            wait(piece, ring_r.at[ph, ck, j])
            summed = summed + piece[...].astype(F32)
        return summed

    def gather_send(n, ck, buffer):
        rows = own_rows(ck)
        for j in range(1, 4):
            push(
                buffer.at[rows],
                buffer.at[rows],
                gx_s.at[n, ck, j - 1],
                gx_r.at[n, ck, j - 1],
                device(core, y, z, (x + j) % 4),
            )
        push(
            buffer.at[rows],
            buffer.at[rows],
            gc_s.at[n, ck, 0],
            gc_r.at[n, ck, 0],
            device(1 - core, y, z, x),
        )

    def gather_pass(n, ck, buffer):
        for j in range(1, 4):
            first = ck * R + core * HALF + ((x - j + 4) % 4) * QUARTER
            piece = buffer.at[pl.ds(pl.multiple_of(first, QUARTER), QUARTER)]
            wait(piece, gx_r.at[n, ck, j - 1])
            push(
                piece,
                piece,
                gc_s.at[n, ck, j],
                gc_r.at[n, ck, j],
                device(1 - core, y, z, x),
            )

    def gather_finish(n, ck, buffer):
        for j in range(4):
            wait(buffer.at[own_rows(ck)], gc_r.at[n, ck, j])

    def out_rows(seq, ck, c_, x_):
        first = seq * LEN + ck * R + c_ * HALF + x_ * QUARTER
        return ends_out.at[pl.ds(pl.multiple_of(first, QUARTER), QUARTER)]

    def give_out(n, ck):
        src = ends_low.at[n, ck * QUARTER : (ck + 1) * QUARTER]
        dst = out_rows(z_hi, ck, core, x)
        recv = out_r.at[ck, core * 4 + x]
        target = 1 - n
        for j in range(4):
            where, send = device(target, y, z, (x + j) % 4), out_s.at[n, ck, j]
            if j == 0:
                push_or_keep(core == target, src, dst, send, recv, where)
            else:
                push(src, dst, send, recv, where)

    def out_arrived(ck):
        for c_ in range(2):
            for x_ in range(4):
                wait(out_rows(z_hi, ck, c_, x_), out_r.at[ck, c_ * 4 + x_])

    def direct_first(n, ck):
        push(
            ends_low.at[n, ck * QUARTER : (ck + 1) * QUARTER],
            out_rows(z_hi, ck, core, x),
            direct_s.at[n, ck],
            direct_r.at[ck, core],
            device(1 - n, y, (z + 2) % 4, x),
        )

    def direct_copy(n, ck, c_, j):
        rows = out_rows(1 - z_hi, ck, c_, x)
        return pltpu.make_async_remote_copy(
            src_ref=rows,
            dst_ref=rows,
            send_sem=direct2_s.at[ck, c_, j - 1],
            recv_sem=direct2_r.at[ck, c_, j - 1],
            device_id=device(1 - n, y, z, (x + j) % 4),
            device_id_type=MESH,
        )

    def direct_second(n, ck):
        @pl.when(core == 1 - n)
        def _():
            for c_ in range(2):
                wait(out_rows(1 - z_hi, ck, c_, x), direct_r.at[ck, c_])
                for j in range(1, 4):
                    direct_copy(n, ck, c_, j).start()

    def direct_end(n, ck):
        @pl.when(core == 1 - n)
        def _():
            out_arrived(ck)
            for c_ in range(2):
                for j in range(1, 4):
                    direct_copy(n, ck, c_, j).wait()

    def weight_grads(l, p):
        for i in range(4):
            cols = slice(i * BQ, (i + 1) * BQ)
            if p == 0:
                pieces = [
                    ((384, NIN), dot(xhat[l, :, cols], d_joined[:, 384:NIN], 0, 0)),
                    ((NIN, NALL), dot(grads_in[l, :, cols], joined[l], 0, 0)),
                ]
            else:
                pieces = [((0, 384), dot(xhat[l, :, cols], d_joined[:, 0:384], 0, 0))]
            for (first, last), piece in pieces:
                low = piece.astype(BF)
                for k in range(2):
                    w_grad[i, k, :, first:last] = low[k * 128 : (k + 1) * 128]

    def plane_first(l, p):
        cols = slice(*G_PARTS[p])
        for k in range(2):
            z_ = 2 * core + k
            slot = (z_ - z + 3) % 4
            src, send = w_grad.at[:, k, 0:ROWS_A, cols], p1a_s.at[l, p, k]
            other = z_ != z

            @pl.when(other)
            def _(src=src, send=send, z_=z_, slot=slot):
                pltpu.make_async_remote_copy(
                    src_ref=src,
                    dst_ref=plane_a.at[l, slot, :, :, cols],
                    send_sem=send,
                    recv_sem=p1a_r.at[l, p, slot],
                    device_id=device(core, y, z_, x),
                    device_id_type=MESH,
                ).start()

            drains.setdefault("grad", []).append((other, src, send))
        for j in range(1, 4):
            to = (y + j) % 4
            push(
                w_grad.at[to, :, ROWS_A:, cols],
                plane_b.at[l, j - 1, :, :, cols],
                p1b_s.at[l, p, j - 1],
                p1b_r.at[l, p, j - 1],
                device(core, to, z, x),
                "grad",
            )

    def plane_second(l, p):
        cols = slice(*G_PARTS[p])

        @pl.when(forwarder)
        def _():
            for j in range(3):
                wait(plane_a.at[l, j, :, :, cols], p1a_r.at[l, p, j])

            def one(y_, carry):
                summed = w_grad[y_, z_lo, 0:ROWS_A, cols].astype(F32)
                for j in range(3):
                    summed = summed + plane_a[l, j, y_, :, cols].astype(F32)
                sum_a[l, y_, :, cols] = summed.astype(BF)
                return carry

            lax.fori_loop(0, 4, one, 0)
            for j in range(4):
                to = (y + j) % 4
                src, dst = sum_a.at[l, to, :, cols], own_a.at[y, :, cols]
                copy = pltpu.make_async_remote_copy(
                    src_ref=src,
                    dst_ref=dst,
                    send_sem=p2a_s.at[l, p, j],
                    recv_sem=p2a_r.at[p, y],
                    device_id=device(l, to, z, x),
                    device_id_type=MESH,
                )
                if j == 0:
                    pl.when(core == l)(pltpu.make_async_copy(src, dst, p2a_r.at[p, y]).start)
                    pl.when(core != l)(copy.start)
                else:
                    copy.start()

        for j in range(3):
            wait(plane_b.at[l, j, :, :, cols], p1b_r.at[l, p, j])
        for k in range(2):
            summed = w_grad[y, k, ROWS_A:, cols].astype(F32)
            for j in range(3):
                summed = summed + plane_b[l, j, k, :, cols].astype(F32)
            sum_b[l, k, :, cols] = summed.astype(BF)
            z_ = 2 * core + k
            push_or_keep(
                jnp.logical_and(core == l, z_ == z),
                sum_b.at[l, k, :, cols],
                own_b.at[z, :, cols],
                p2b_s.at[l, p, k],
                p2b_r.at[p, z],
                device(l, y, z_, x),
            )

    def drain_plane():
        @pl.when(forwarder)
        def _():
            for l in range(2):
                for p, cols in enumerate(G_PARTS):
                    src = sum_a.at[l, 0, :, slice(*cols)]
                    for j in range(4):
                        ended = functools.partial(wait, src, p2a_s.at[l, p, j])
                        if j == 0:
                            pl.when(core != l)(ended)
                        else:
                            ended()

    def send_small(l):
        column_sum = jnp.zeros((1, NIN), F32)
        out_sum = jnp.zeros((1, D), F32)

        def one(i, carry):
            rows = pl.ds(pl.multiple_of(i * 128, 128), 128)
            a, b = carry
            a = a + jnp.sum(d_joined[rows, :].astype(F32), axis=0, keepdims=True)
            b = b + jnp.sum(grads_in[l, rows, :].astype(F32), axis=0, keepdims=True)
            return a, b

        column_sum, out_sum = lax.fori_loop(0, LEN // 128, one, (column_sum, out_sum))
        message[l, 0:1, 0:NIN] = column_sum
        message[l, 1:2, :] = out_sum
        here = y * 4 + z
        for y_ in range(4):
            for k in range(2):
                z_ = 2 * core + k
                own = jnp.logical_and(core == l, jnp.logical_and(y_ == y, z_ == z))
                push_or_keep(
                    own,
                    message.at[l],
                    messages.at[here],
                    msg_s.at[l, y_ * 2 + k],
                    msg_r.at[here],
                    device(l, y_, z_, x),
                )

    def small_first():
        for k in range(16):
            wait(messages.at[k], msg_r.at[k])
        summed = messages[0]
        for k in range(1, 16):
            summed = summed + messages[k]
        small[...] = summed
        for j in range(1, 4):
            push(
                small,
                small_ring.at[j - 1],
                ln1_s.at[j - 1],
                ln1_r.at[j - 1],
                device(core, y, z, (x + j) % 4),
            )
        for n in range(3):
            g_qkv_b[n] = summed[0:1, n * 128 : (n + 1) * 128]
        g_up_b[...] = summed[0:1, 384:NIN]
        g_out_b[...] = summed[1:2, :]

    def small_second():
        for j in range(3):
            wait(small_ring.at[j], ln1_r.at[j])
        small_sum[...] = small[...] + small_ring[0] + small_ring[1] + small_ring[2]
        push(small_sum, small_far, ln2_s, ln2_r, device(core, y, (z + 2) % 4, x))

    def small_third():
        wait(small_far, ln2_r)
        both = small_sum[...] + small_far[...]
        for k in range(2):
            g_gains[k : k + 1, :] = both[2 + k : 3 + k, :] / gains[k : k + 1, :]
            g_offsets[k : k + 1, :] = both[4 + k : 5 + k, :] / gains[k : k + 1, :]

    def after_first_layer(ck):
        rows = own_rows(ck)
        mid = slice(ck * QUARTER, (ck + 1) * QUARTER)
        result = x_own[mid, :].astype(F32) + reduce_finish(0, ck) + out_row[0]
        low = result.astype(BF)
        y_mid[ck * QUARTER : (ck + 1) * QUARTER, :] = low
        xhat[1, rows, :] = standardize(low.astype(F32))[0].astype(BF)
        gather_send(0, ck, xhat.at[1])

    def after_second_layer(ck):
        mid = slice(ck * QUARTER, (ck + 1) * QUARTER)
        result = y_mid[mid, :].astype(F32) + reduce_finish(1, ck) + out_row[1]
        ends_low[0, mid, :] = result.astype(BF)

    def through_norm(stream, grad, e):
        scaled, inverse = standardize(stream)
        return grad + inverse * (
            e
            - jnp.mean(e, axis=-1, keepdims=True)
            - scaled * jnp.mean(e * scaled, axis=-1, keepdims=True)
        )

    def input_grad_middle(ck):
        mid = slice(ck * QUARTER, (ck + 1) * QUARTER)
        rows = own_rows(ck)
        e = reduce_finish(2, ck)
        moved = through_norm(y_mid[mid, :].astype(F32), grads_in[1, rows, :].astype(F32), e)
        grads_in[0, rows, :] = moved.astype(BF)
        gather_send(1, ck, grads_in.at[0])

    def input_grad_first(ck):
        mid = slice(ck * QUARTER, (ck + 1) * QUARTER)
        rows = own_rows(ck)
        e = reduce_finish(3, ck)
        moved = through_norm(x_own[mid, :].astype(F32), grads_in[0, rows, :].astype(F32), e)
        ends_low[1, mid, :] = moved.astype(BF)

    project_all(0, 0)
    attend_all(0, 0)
    gather_rest(0, 1)
    reduce_send(0, 0, functools.partial(branch, 0))
    gather_second(1, 0)
    project_all(0, 1)
    attend_all(0, 1)
    reduce_send(0, 1, functools.partial(branch, 0))
    after_first_layer(0)
    after_first_layer(1)
    gather_pass(0, 0, xhat.at[1])
    gather_rest(1, 0)
    gather_finish(0, 0, xhat.at[1])
    project_all(1, 0)
    gather_pass(0, 1, xhat.at[1])
    attend_all(1, 0)
    reduce_send(1, 0, functools.partial(branch, 1))
    gather_finish(0, 1, xhat.at[1])
    project_all(1, 1)
    attend_all(1, 1)
    reduce_send(1, 1, functools.partial(branch, 1))

    wait(mine, swap_s)
    backward_first(1, 1)
    backward_first(1, 0)
    after_second_layer(0)
    direct_first(0, 0)
    give_out(0, 0)
    weight_grads(1, 0)
    plane_first(1, 0)
    after_second_layer(1)
    direct_first(0, 1)
    give_out(0, 1)
    backward_second(1, 1)
    reduce_send(2, 1, functools.partial(norm_grad, 1))
    backward_second(1, 0)
    reduce_send(2, 0, functools.partial(norm_grad, 1))
    input_grad_middle(1)
    weight_grads(1, 1)
    plane_first(1, 1)
    input_grad_middle(0)
    gather_pass(1, 1, grads_in.at[0])
    direct_second(0, 0)
    direct_second(0, 1)
    send_small(1)
    plane_second(1, 0)
    gather_finish(1, 1, grads_in.at[0])

    backward_first(0, 1)
    gather_pass(1, 0, grads_in.at[0])
    backward_second(0, 1)
    reduce_send(3, 1, functools.partial(norm_grad, 0))
    gather_finish(1, 0, grads_in.at[0])
    backward_first(0, 0)
    plane_second(1, 1)
    drain("grad")
    weight_grads(0, 0)
    plane_first(0, 0)
    backward_second(0, 0)
    reduce_send(3, 0, functools.partial(norm_grad, 0))
    input_grad_first(1)
    direct_first(1, 1)
    give_out(1, 1)
    weight_grads(0, 1)
    plane_first(0, 1)
    send_small(0)
    input_grad_first(0)
    direct_first(1, 0)
    give_out(1, 0)
    direct_second(1, 1)
    plane_second(0, 0)
    small_first()
    direct_second(1, 0)
    plane_second(0, 1)
    small_second()

    for k in range(4):
        for p, cols in enumerate(G_PARTS):
            wait(own_a.at[k, :, slice(*cols)], p2a_r.at[p, k])
            wait(own_b.at[k, :, slice(*cols)], p2b_r.at[p, k])
    total[0:ROWS_A, :] = (
        own_a[0].astype(F32) + own_a[1].astype(F32) + own_a[2].astype(F32) + own_a[3].astype(F32)
    )
    total[ROWS_A:128, :] = (
        own_b[0].astype(F32) + own_b[1].astype(F32) + own_b[2].astype(F32) + own_b[3].astype(F32)
    )
    for n in range(7):
        k = 0 if n < 3 else 1
        cols = slice(n * 128, (n + 1) * 128)
        grad = total[:, cols] * gain_cols[k] + offset_cols[k] * small[0:1, cols]
        if n < 3:
            g_qkv[n] = grad
        else:
            g_up[:, (n - 3) * 128 : (n - 2) * 128] = grad
    g_dense[...] = total[:, NIN : NIN + 128].T
    g_down[...] = total[:, NIN + 128 : NALL].T
    small_third()
    direct_end(0, 0)
    direct_end(0, 1)
    direct_end(1, 1)
    direct_end(1, 0)
    drain("grad")
    for ck in range(NCH):
        drain(("part", ck))
    drain("end")
    drain_first()
    drain_second(0, 1)
    drain_second(1, 0)
    drain_extra()
    drain_plane()


def settle(*refs):
    count = (len(refs) - 2) // 3
    sources, targets, held = refs[:count], refs[count : 2 * count], refs[2 * count : 3 * count]
    sem_in, sem_out = refs[-2:]
    trips = []
    rows = sources[0].shape[0] // 4
    for k in range(4):
        piece = pl.ds(k * rows, rows)
        trips.append((sources[0].at[piece], held[0].at[piece], targets[0].at[piece]))
    for n in range(1, count):
        trips.append((sources[n], held[n], targets[n]))
    arrivals = []
    departures = []
    for n, (source, stop, target) in enumerate(trips):
        arrivals.append(pltpu.make_async_copy(source, stop, sem_in.at[n]))
        departures.append(pltpu.make_async_copy(stop, target, sem_out.at[n]))
    for copy in arrivals:
        copy.start()
    for arrival, departure in zip(arrivals, departures):
        arrival.wait()
        departure.start()
    for copy in departures:
        copy.wait()


def body(ends_in, ln_gains, ln_biases, qkv_w, qkv_bias, dense_w, up_w, up_bias, down_w, out_bias):
    cosine, sine = rotary_tables()
    vmem = pl.BlockSpec(memory_space=pltpu.VMEM)
    anywhere = pl.BlockSpec(memory_space=pl.ANY)

    def shape(*dims):
        return jax.ShapeDtypeStruct(dims, F32)

    def sems(*dims):
        return pltpu.SemaphoreType.DMA(dims)

    outs = pl.pallas_call(
        kernel,
        out_shape=[
            jax.ShapeDtypeStruct((2 * LEN, D), BF),
            shape(2, D),
            shape(2, D),
            shape(3, 128, 128),
            shape(3, 1, 128),
            shape(128, 128),
            shape(128, 512),
            shape(1, 512),
            shape(512, 128),
            shape(1, D),
        ],
        in_specs=[anywhere] + [vmem] * 11,
        out_specs=[vmem] * 10,
        scratch_shapes=[
            pltpu.VMEM((128, NALL), BF),
            pltpu.VMEM((8, 256), F32),
            pltpu.VMEM((2, 8, 8, 256), F32),
            pltpu.VMEM((2, 1, 1024), F32),
            pltpu.VMEM((2, 1, 1024), F32),
            pltpu.VMEM((2, D, NALL), BF),
            pltpu.VMEM((LEN, D), BF),
            pltpu.VMEM((2, LEN, D), BF),
            pltpu.VMEM((2, LEN, D), BF),
            pltpu.VMEM((LEN // 8, D), BF),
            pltpu.VMEM((LEN // 8, D), BF),
            pltpu.VMEM((2, LEN, NOUT), BF),
            pltpu.VMEM((2, LEN, 512), BF),
            pltpu.VMEM((2, LEN, 128), BF),
            pltpu.VMEM((2, LEN, 128), BF),
            pltpu.VMEM((2, LEN, 128), BF),
            pltpu.VMEM((2, 128, LEN), BF),
            pltpu.VMEM((128, LEN), BF),
            pltpu.VMEM((2, 10, BQ, 2 * BQ), BF),
            pltpu.VMEM((2, LEN // BQ, 2 * BQ), F32),
            pltpu.VMEM((2, 128, LEN), F32),
            pltpu.VMEM((LEN, 2 * BQ), F32),
            pltpu.VMEM((LEN, 128), BF),
            pltpu.VMEM((LEN, NIN), BF),
            pltpu.VMEM((2, LEN // 2, D), BF),
            pltpu.VMEM((2, 3, LEN // 8, D), BF),
            pltpu.VMEM((2, LEN // 8, D), BF),
            pltpu.VMEM((4, 2, 128, NALL), BF),
            pltpu.VMEM((2, 3, 4, ROWS_A, NALL), BF),
            pltpu.VMEM((2, 3, 2, ROWS_B, NALL), BF),
            pltpu.VMEM((2, 4, ROWS_A, NALL), BF),
            pltpu.VMEM((2, 2, ROWS_B, NALL), BF),
            pltpu.VMEM((4, ROWS_A, NALL), BF),
            pltpu.VMEM((4, ROWS_B, NALL), BF),
            pltpu.VMEM((128, NALL), F32),
            pltpu.VMEM((2, 8, D), F32),
            pltpu.VMEM((16, 8, D), F32),
            pltpu.VMEM((8, D), F32),
            pltpu.VMEM((3, 8, D), F32),
            pltpu.VMEM((8, D), F32),
            pltpu.VMEM((8, D), F32),
            pltpu.SemaphoreType.DMA,
            pltpu.SemaphoreType.DMA,
            pltpu.SemaphoreType.DMA,
            sems(2, 2, 4),
            sems(2, 2, 2, 8),
            sems(2, 2, 4, 3),
            sems(2, 2, 2, 3),
            sems(16),
            sems(2, 8),
            sems(4, NCH, NB),
            sems(4, NCH, NB),
            sems(4, NCH, 3),
            sems(4, NCH, 3),
            sems(2, NCH, 3),
            sems(2, NCH, 3),
            sems(2, NCH, 4),
            sems(2, NCH, 4),
            sems(2, NCH, 4),
            sems(NCH, 8),
            sems(2, NCH),
            sems(NCH, 2),
            sems(NCH, 2, 3),
            sems(NCH, 2, 3),
            sems(2, 8),
            sems(16),
            sems(2, 2, 2),
            sems(2, 2, 3),
            sems(2, 2, 3),
            sems(2, 2, 3),
            sems(2, 2, 4),
            sems(2, 4),
            sems(2, 2, 2),
            sems(2, 4),
            sems(3),
            sems(3),
            pltpu.SemaphoreType.DMA,
            pltpu.SemaphoreType.DMA,
        ],
        compiler_params=pltpu.CompilerParams(
            collective_id=0, has_side_effects=True, vmem_limit_bytes=63 * 2**20
        ),
        cost_estimate=pl.CostEstimate(
            flops=22 * 10**9, bytes_accessed=20 * 10**6, transcendentals=4 * 10**6
        ),
    )(
        ends_in[0],
        qkv_w[0],
        dense_w[0],
        up_w[0],
        down_w[0],
        ln_gains[0],
        ln_biases[0],
        jnp.transpose(qkv_bias, (1, 0, 2)),
        up_bias,
        out_bias,
        jnp.asarray(cosine),
        jnp.asarray(sine),
    )
    outs = pl.pallas_call(
        settle,
        out_shape=[jax.ShapeDtypeStruct(out.shape, out.dtype) for out in outs],
        in_specs=[anywhere] * len(outs),
        out_specs=[anywhere] * len(outs),
        scratch_shapes=[pltpu.VMEM(out.shape, out.dtype) for out in outs]
        + [sems(len(outs) + 3), sems(len(outs) + 3)],
        compiler_params=pltpu.CompilerParams(vmem_limit_bytes=63 * 2**20),
        cost_estimate=pl.CostEstimate(flops=0, bytes_accessed=10 * 10**6, transcendentals=0),
    )(*outs)
    out, gains, offsets, d_qkv, d_qkv_b, d_dense, d_up, d_up_b, d_down, d_out_b = outs
    return (
        out[None],
        gains[None],
        offsets[None],
        d_qkv[None],
        jnp.transpose(d_qkv_b, (1, 0, 2)),
        d_dense[None],
        d_up[None],
        d_up_b,
        d_down[None],
        d_out_b,
    )


def solution(mesh):
    in_specs = (
        P("section", "dp", None),
        P("section", None, None),
        P("section", None, None),
        P("section", None, "dp", "tensor"),
        P("section", None, "tensor"),
        P("section", "tensor", "dp"),
        P("section", "dp", "tensor"),
        P("section", "tensor"),
        P("section", "tensor", "dp"),
        P("section", None),
    )
    out_specs = (
        P("section", "dp", None),
        P("section", None, None),
        P("section", None, None),
        P("section", None, "dp", "tensor"),
        P("section", None, "tensor"),
        P("section", "tensor", "dp"),
        P("section", "dp", "tensor"),
        P("section", "tensor"),
        P("section", "tensor", "dp"),
        P("section", None),
    )
    return jax.shard_map(body, mesh=mesh, in_specs=in_specs, out_specs=out_specs, check_vma=False)
```

```python
import functools

import jax
import jax.numpy as jnp
import numpy as np
from jax import lax
from jax.experimental import pallas as pl
from jax.experimental.pallas import tpu as pltpu
from jax.sharding import PartitionSpec as P

MESH = pl.DeviceIdType.MESH
BF = jnp.bfloat16
F32 = jnp.float32

D = 1024
LEN = 1024
HD = 64
ROT = 16
NIN = 896
NOUT = 640
NALL = NIN + NOUT
BQ = 256
NCH = 2
R = LEN // NCH
HALF = R // 2
QUARTER = R // 8
BM = min(256, HALF)
NB = HALF // BM
W_PARTS = (((0, NIN), (NIN, NALL)), ((0, NALL),))
G_PARTS = ((384, NALL), (0, 384))
ROWS_A = 48
ROWS_B = 128 - ROWS_A


def dot(a, b, ca, cb):
    return lax.dot_general(a, b, (((ca,), (cb,)), ((), ())), preferred_element_type=F32)


def rotary_tables():
    position = np.arange(LEN, dtype=np.float32)[:, None]
    exponent = np.arange(ROT // 2, dtype=np.float32) * np.float32(2.0) / np.float32(ROT)
    angles = (position * np.float32(10000.0) ** (-exponent)).astype(np.float32)
    cosine = np.ones((LEN, 2 * HD), np.float32)
    sine = np.zeros((LEN, 2 * HD), np.float32)
    for first in (0, 8, HD, HD + 8):
        cosine[:, first : first + 8] = np.cos(angles)
        sine[:, first : first + 8] = np.sin(angles)
    return cosine, sine


def lanes_of_head(shape):
    return lax.broadcasted_iota(jnp.int32, shape, 1) % HD


def turn(value, cosine, sine):
    lane = lanes_of_head(value.shape)
    partner = jnp.where(lane < 8, -pltpu.roll(value, 120, 1), pltpu.roll(value, 8, 1))
    return value * cosine + partner * sine


def turn_back(grad, cosine, sine):
    lane = lanes_of_head(grad.shape)
    moved = grad * sine
    partner = jnp.where(
        lane < 8, pltpu.roll(moved, 120, 1), jnp.where(lane < 16, -pltpu.roll(moved, 8, 1), 0.0)
    )
    return grad * cosine + partner


def gelu_and_slope(hidden):
    bell = jnp.exp(-0.5 * hidden * hidden)
    size = 1.0 + (0.3275911 * 0.7071067811865476) * jnp.abs(hidden)
    t = pltpu.reciprocal(size, approx=True)
    t = t * (2.0 - size * t)
    series = t * (
        0.254829592 * 0.5
        + t
        * (
            -0.284496736 * 0.5
            + t * (1.421413741 * 0.5 + t * (-1.453152027 * 0.5 + t * (1.061405429 * 0.5)))
        )
    )
    tail = series * bell
    below = jnp.where(hidden >= 0.0, 1.0 - tail, tail)
    return hidden * below, below + hidden * bell * 0.3989422804014327


def standardize(value):
    center = jnp.mean(value, axis=-1, keepdims=True)
    centred = value - center
    inverse = lax.rsqrt(jnp.mean(centred * centred, axis=-1, keepdims=True) + 1e-05)
    return centred * inverse, inverse


def stack_heads(value):
    lane = lax.broadcasted_iota(jnp.int32, value.shape, 1)
    wide = value.astype(F32)
    return jnp.concatenate(
        [jnp.where(lane < HD, wide, 0.0), jnp.where(lane >= HD, wide, 0.0)], axis=0
    ).astype(BF)


def split_heads(value):
    half = value.shape[1] // 2
    return jnp.concatenate([value[:HD, :half], value[HD:, half:]], axis=0)


def pair(i, j):
    return i * (i + 1) // 2 + j


def kernel(
    ends,
    qkv,
    dense,
    up,
    down,
    gains,
    offsets,
    qkv_b,
    up_b,
    out_b,
    cosine_in,
    sine_in,
    ends_hbm,
    g_gains,
    g_offsets,
    g_qkv,
    g_qkv_b,
    g_dense,
    g_up,
    g_up_b,
    g_down,
    g_out_b,
    cosine,
    sine,
    ends_out,
    shard,
    extra,
    extras,
    bias_row,
    out_row,
    weights,
    x_in,
    grads_in,
    xhat,
    y_mid,
    x_own,
    joined,
    slope,
    queries,
    keys,
    values,
    keys_t,
    values_t,
    soft,
    soft_scale,
    context_t,
    scores,
    d_context,
    d_joined,
    core_part,
    ring_part,
    ends_low,
    w_grad,
    plane_a,
    plane_b,
    sum_a,
    sum_b,
    own_a,
    own_b,
    total,
    message,
    messages,
    small,
    small_ring,
    small_sum,
    small_far,
    table_sem,
    done_sem,
    local_sem,
    swap_s,
    swap_r,
    w1_s,
    w_r,
    w2a_s,
    w2b_s,
    extra_s,
    extra_r,
    core_s,
    core_r,
    ring_s,
    ring_r,
    gx_s,
    gx_r,
    gc_s,
    gc_r,
    out_s,
    out_r,
    direct_s,
    direct_r,
    direct2_s,
    direct2_r,
    msg_s,
    msg_r,
    p1a_s,
    p1a_r,
    p1b_s,
    p1b_r,
    p2a_s,
    p2a_r,
    p2b_s,
    p2b_r,
    ln1_s,
    ln1_r,
    ln2_s,
    ln2_r,
):
    part = x_in
    core = lax.axis_index("section")
    dp = lax.axis_index("dp")
    t = lax.axis_index("tensor")
    y, z_lo = dp // 2, dp % 2
    z_hi, x = t // 4, t % 4
    z = 2 * z_hi + z_lo
    forwarder = core == z_hi

    def device(c_, y_, z_, x_):
        return {"section": c_, "dp": y_ * 2 + z_ % 2, "tensor": (z_ // 2) * 4 + x_}

    drains = {}

    def wait(ref, sem):
        pltpu.make_async_copy(ref, ref, sem).wait()

    def push(src, dst, send, recv, where, tag="end"):
        pltpu.make_async_remote_copy(
            src_ref=src, dst_ref=dst, send_sem=send, recv_sem=recv, device_id=where, device_id_type=MESH
        ).start()
        drains.setdefault(tag, []).append((None, src, send))

    def push_or_keep(own, src, dst, send, recv, where):
        other = jnp.logical_not(own)

        @pl.when(own)
        def _():
            pltpu.make_async_copy(src, dst, recv).start()

        @pl.when(other)
        def _():
            pltpu.make_async_remote_copy(
                src_ref=src,
                dst_ref=dst,
                send_sem=send,
                recv_sem=recv,
                device_id=where,
                device_id_type=MESH,
            ).start()

        drains.setdefault("end", []).append((other, src, send))

    def drain(tag):
        for condition, src, send in drains.pop(tag, []):
            if condition is None:
                wait(src, send)
            else:
                pl.when(condition)(functools.partial(wait, src, send))

    mine = ends.at[pl.ds(pl.multiple_of(z_hi * LEN, LEN), LEN)]
    table_copies = [
        pltpu.make_async_copy(cosine_in, cosine, table_sem.at[0]),
        pltpu.make_async_copy(sine_in, sine, table_sem.at[1]),
    ]
    for c_, buffer in ((0, x_in), (1, grads_in.at[1])):
        pl.when(core == c_)(pltpu.make_async_copy(mine, buffer, local_sem).start)

    barrier = pltpu.get_barrier_semaphore()
    for dy in range(4):
        for dz in range(4):
            for c_ in range(2):
                if (dy, dz, c_) == (0, 0, 0):
                    continue
                pl.semaphore_signal(
                    barrier,
                    inc=1,
                    device_id=device((core + c_) % 2, (y + dy) % 4, (z + dz) % 4, x),
                    device_id_type=MESH,
                )
    for j in range(1, 4):
        pl.semaphore_signal(
            barrier, inc=1, device_id=device(core, y, z, (x + j) % 4), device_id_type=MESH
        )

    for copy in table_copies:
        copy.start()

    block = pl.ds(pl.multiple_of(dp * 128, 128), 128)

    def column(row):
        return jnp.broadcast_to(row, (128, 128)).T

    gain_cols = [column(gains[k : k + 1, block]) for k in range(2)]
    offset_cols = [column(offsets[k : k + 1, block]) for k in range(2)]

    def raw_tile(n):
        if n < 3:
            return qkv[n].astype(F32), 0, qkv_b[n]
        cols = slice((n - 3) * 128, (n - 2) * 128)
        return up[:, cols].astype(F32), 1, up_b[:, cols]

    extra[...] = jnp.zeros_like(extra)
    message[...] = jnp.zeros_like(message)
    for n in range(7):
        tile, k, bias = raw_tile(n)
        shard[:, n * 128 : (n + 1) * 128] = (tile * gain_cols[k]).astype(BF)
        added = jnp.sum(tile * offset_cols[k], axis=0, keepdims=True) + 0.125 * bias
        extra[n // 2 : n // 2 + 1, (n % 2) * 128 : (n % 2) * 128 + 128] = added
    for n in range(4):
        extra[4 + n : 5 + n, :] = 0.125 * out_b[:, n * 256 : (n + 1) * 256]
    shard[:, NIN : NIN + 128] = dense[...].T
    shard[:, NIN + 128 : NALL] = down[...].T

    pl.semaphore_wait(barrier, 34)

    for c_, buffer in ((0, x_in), (1, grads_in.at[1])):

        @pl.when(core == c_)
        def _(buffer=buffer):
            pltpu.make_async_remote_copy(
                src_ref=mine,
                dst_ref=buffer,
                send_sem=swap_s,
                recv_sem=swap_r,
                device_id=device(1 - core, y, z, x),
                device_id_type=MESH,
            ).start()

    def w_rows(l, p, dp_, half):
        rows = pl.ds(pl.multiple_of(dp_ * 128 + half * 64, 64), 64)
        return weights.at[l, rows, slice(*W_PARTS[l][p])]

    def gather_first(l):
        @pl.when(core == l)
        def _():
            for p, cols in enumerate(W_PARTS[l]):
                for half in range(2):
                    src = shard.at[half * 64 : half * 64 + 64, slice(*cols)]
                    dst = w_rows(l, p, dp, half)
                    recv = w_r.at[half, l, p, dp]

                    @pl.when(forwarder)
                    def _(src=src, dst=dst, recv=recv):
                        pltpu.make_async_copy(src, dst, recv).start()

                    for j in range(4):
                        if half == 0:
                            where = device(z_hi, (y + j) % 4, z, x)
                        else:
                            where = device(z_hi, y, (z + j) % 4, x)
                        copy = pltpu.make_async_remote_copy(
                            src_ref=src,
                            dst_ref=dst,
                            send_sem=w1_s.at[p, half, j],
                            recv_sem=recv,
                            device_id=where,
                            device_id_type=MESH,
                        )
                        if j == 0:
                            pl.when(jnp.logical_not(forwarder))(copy.start)
                        else:
                            copy.start()

    def drain_first():
        for l in range(2):

            @pl.when(core == l)
            def _(l=l):
                for p, cols in enumerate(W_PARTS[l]):
                    src = shard.at[0:64, slice(*cols)]
                    for half in range(2):
                        for j in range(4):
                            ended = functools.partial(wait, src, w1_s.at[p, half, j])
                            if j == 0:
                                pl.when(jnp.logical_not(forwarder))(ended)
                            else:
                                ended()

    def gather_second(l, p):
        for k in range(2):
            block_b = w_rows(l, p, y * 2 + k, 1)
            wait(block_b, w_r.at[1, l, p, y * 2 + k])
            for j in range(1, 4):
                push(
                    block_b,
                    block_b,
                    w2b_s.at[l, p, k, j - 1],
                    w_r.at[1, l, p, y * 2 + k],
                    device(core, (y + j) % 4, z, x),
                    ("w", l, p),
                )

        @pl.when(forwarder)
        def _():
            for y_ in range(4):
                dp_ = y_ * 2 + z_lo
                block_a = w_rows(l, p, dp_, 0)
                wait(block_a, w_r.at[0, l, p, dp_])
                for j in range(1, 4):
                    pltpu.make_async_remote_copy(
                        src_ref=block_a,
                        dst_ref=block_a,
                        send_sem=w2a_s.at[l, p, y_, j - 1],
                        recv_sem=w_r.at[0, l, p, dp_],
                        device_id=device(core, y, (z + j) % 4, x),
                        device_id_type=MESH,
                    ).start()

    def drain_second(l, p):
        drain(("w", l, p))

        @pl.when(forwarder)
        def _():
            for y_ in range(4):
                for j in range(3):
                    wait(w_rows(l, p, 0, 0), w2a_s.at[l, p, y_, j])

    def gather_rest(l, p):
        for j in range(1, 4):
            for k in range(2):
                dp_ = ((y + j) % 4) * 2 + k
                wait(w_rows(l, p, dp_, 1), w_r.at[1, l, p, dp_])
        for y_ in range(4):
            dp_ = y_ * 2 + 1 - z_lo
            wait(w_rows(l, p, dp_, 0), w_r.at[0, l, p, dp_])

            @pl.when(jnp.logical_not(forwarder))
            def _(dp_=y_ * 2 + z_lo):
                wait(w_rows(l, p, dp_, 0), w_r.at[0, l, p, dp_])

        if p > 0:
            return
        for dp_ in range(8):
            wait(extras.at[l, dp_], extra_r.at[l, dp_])
        summed = extras[l, 0]
        for dp_ in range(1, 8):
            summed = summed + extras[l, dp_]
        for n in range(4):
            bias_row[l, :, n * 256 : (n + 1) * 256] = summed[n : n + 1, :]
            out_row[l, :, n * 256 : (n + 1) * 256] = summed[4 + n : 5 + n, :]

    gather_first(0)
    for l in range(2):

        @pl.when(core == l)
        def _(l=l):
            for dy in range(4):
                for dz in range(4):
                    where = device(z_hi, (y + dy) % 4, (z + dz) % 4, x)
                    dst = extras.at[l, dp]
                    recv = extra_r.at[l, dp]
                    copy = pltpu.make_async_remote_copy(
                        src_ref=extra,
                        dst_ref=dst,
                        send_sem=extra_s.at[dy * 4 + dz],
                        recv_sem=recv,
                        device_id=where,
                        device_id_type=MESH,
                    )
                    if (dy, dz) == (0, 0):
                        pl.when(forwarder)(pltpu.make_async_copy(extra, dst, recv).start)
                        pl.when(jnp.logical_not(forwarder))(copy.start)
                    else:
                        copy.start()

    def drain_extra():
        for k in range(16):
            if k == 0:
                pl.when(jnp.logical_not(forwarder))(
                    functools.partial(wait, extra, extra_s.at[k])
                )
            else:
                wait(extra, extra_s.at[k])

    wait(x_in, local_sem)
    wait(x_in, swap_r)

    gather_second(0, 0)

    def normalize_rows(i, carry):
        rows = pl.ds(pl.multiple_of(i * 128, 128), 128)
        xhat[0, rows, :] = standardize(x_in[rows, :].astype(F32))[0].astype(BF)
        return carry

    lax.fori_loop(0, LEN // 128, normalize_rows, 0)
    for ck in range(NCH):
        first = ck * R + core * HALF + x * QUARTER
        x_own[ck * QUARTER : (ck + 1) * QUARTER, :] = x_in[
            pl.ds(pl.multiple_of(first, QUARTER), QUARTER), :
        ]
    drain_second(0, 0)
    gather_second(0, 1)
    gather_first(1)
    gather_rest(0, 0)
    for copy in table_copies:
        copy.wait()

    def project(l, i):
        rows = pl.ds(pl.multiple_of(i * BQ, BQ), BQ)
        low = xhat[l, rows, :]
        raw = dot(low, weights[l, :, 0:384], 1, 0) + bias_row[l, :, 0:384]
        cos_rows, sin_rows = cosine[rows, :], sine[rows, :]
        q = turn(raw[:, 0:128], cos_rows, sin_rows) * HD**-0.5
        k = turn(raw[:, 128:256], cos_rows, sin_rows)
        v = raw[:, 256:384]
        queries[l, rows, :] = q.astype(BF)
        keys[l, rows, :] = k.astype(BF)
        values[l, rows, :] = v.astype(BF)
        keys_t[l, :, rows] = k.T.astype(BF)
        values_t[:, rows] = v.T.astype(BF)
        hidden = dot(low, weights[l, :, 384:NIN], 1, 0) + bias_row[l, :, 384:NIN]
        act, gradient = gelu_and_slope(hidden)
        joined[l, rows, 128:NOUT] = act.astype(BF)
        slope[l, rows, :] = gradient.astype(BF)

    def attend(l, i):
        rows = slice(i * BQ, (i + 1) * BQ)
        stacked = stack_heads(queries[l, rows, :])
        largest = None
        for j in range(i + 1):
            tile = dot(keys[l, j * BQ : (j + 1) * BQ, :], stacked, 1, 1)
            if j == i:
                key_at = lax.broadcasted_iota(jnp.int32, tile.shape, 0)
                query_at = lax.broadcasted_iota(jnp.int32, tile.shape, 1) % BQ
                tile = jnp.where(key_at <= query_at, tile, -1e30)
            scores[j * BQ : (j + 1) * BQ, :] = tile
            top = jnp.max(tile, axis=0, keepdims=True)
            largest = top if largest is None else jnp.maximum(largest, top)
        summed = jnp.zeros((1, 2 * BQ), F32)
        outcome = jnp.zeros((2 * HD, 2 * BQ), F32)
        for j in range(i + 1):
            terms = jnp.exp(scores[j * BQ : (j + 1) * BQ, :] - largest)
            summed = summed + jnp.sum(terms, axis=0, keepdims=True)
            low = terms.astype(BF)
            soft[l, pair(i, j)] = low
            outcome = outcome + dot(values_t[:, j * BQ : (j + 1) * BQ], low, 1, 0)
        scale = 1.0 / summed
        soft_scale[l, i : i + 1, :] = scale
        context = split_heads(outcome * scale)
        context_t[l, :, rows] = context
        joined[l, rows, 0:128] = context.T.astype(BF)

    def attend_back(l, i):
        rows = slice(i * BQ, (i + 1) * BQ)
        grad_t = d_context[rows, :].astype(F32).T
        scale = soft_scale[l, i : i + 1, :]
        top = grad_t[:HD] * scale[:, :BQ]
        bottom = grad_t[HD:] * scale[:, BQ:]
        context = context_t[l, :, rows]
        delta = jnp.concatenate(
            [
                jnp.sum(context[:HD] * top, axis=0, keepdims=True),
                jnp.sum(context[HD:] * bottom, axis=0, keepdims=True),
            ],
            axis=1,
        )
        blank = jnp.zeros_like(top)
        spread_wide = jnp.concatenate(
            [jnp.concatenate([top, blank], axis=1), jnp.concatenate([blank, bottom], axis=1)], axis=0
        )
        spread_t = spread_wide.astype(BF)
        spread = spread_wide.T.astype(BF)
        stacked = stack_heads(queries[l, rows, :])
        d_query_t = jnp.zeros((2 * HD, 2 * BQ), F32)
        for j in range(i + 1):
            cols = slice(j * BQ, (j + 1) * BQ)
            terms = soft[l, pair(i, j)]
            d_terms = dot(values[l, cols, :], spread_t, 1, 0)
            d_scores = (terms.astype(F32) * (d_terms - delta)).astype(BF)
            d_key = dot(d_scores, stacked, 1, 0)
            d_value = dot(terms, spread, 1, 0)
            if i == LEN // BQ - 1:
                scores[cols, 0:128] = d_key
                scores[cols, 128:256] = d_value
            else:
                scores[cols, 0:128] += d_key
                scores[cols, 128:256] += d_value
            d_query_t = d_query_t + dot(keys_t[l, :, cols], d_scores, 1, 0)
        d_query = split_heads(d_query_t).T * HD**-0.5
        d_joined[rows, 0:128] = turn_back(d_query, cosine[rows, :], sine[rows, :]).astype(BF)

    def finish_keys(i, carry):
        rows = pl.ds(pl.multiple_of(i * BQ, BQ), BQ)
        d_joined[rows, 128:256] = turn_back(scores[rows, 0:128], cosine[rows, :], sine[rows, :]).astype(
            BF
        )
        d_joined[rows, 256:384] = scores[rows, 128:256].astype(BF)
        return carry

    def blocks_of(ck):
        return range(ck * R // BQ, (ck + 1) * R // BQ)

    def project_all(l, ck):
        def one(i, carry):
            project(l, i)
            return carry

        lax.fori_loop(ck * R // BQ, (ck + 1) * R // BQ, one, 0)

    def attend_all(l, ck):
        for i in blocks_of(ck):
            attend(l, i)

    def backward_first(l, ck):
        def one(i, carry):
            rows = pl.ds(pl.multiple_of(i * BQ, BQ), BQ)
            both = dot(grads_in[l, rows, :], weights[l, :, NIN:NALL], 1, 0)
            d_context[rows, :] = both[:, 0:128].astype(BF)
            d_joined[rows, 384:NIN] = (both[:, 128:NOUT] * slope[l, rows, :].astype(F32)).astype(BF)
            return carry

        lax.fori_loop(ck * R // BQ, (ck + 1) * R // BQ, one, 0)

    def backward_second(l, ck):
        for i in reversed(blocks_of(ck)):
            attend_back(l, i)
        lax.fori_loop(ck * R // BQ, (ck + 1) * R // BQ, finish_keys, 0)

    def branch(l, rows):
        return dot(joined[l, rows, :], weights[l, :, NIN:NALL], 1, 1)

    def norm_grad(l, rows):
        shares = [
            dot(d_joined[rows, 0:384], weights[l, :, 0:384], 1, 1),
            dot(d_joined[rows, 384:NIN], weights[l, :, 384:NIN], 1, 1),
        ]
        scaled = xhat[l, rows, :].astype(F32)
        for k, e in enumerate(shares):
            message[l, 2 + k : 3 + k, :] += jnp.sum(scaled * e, axis=0, keepdims=True)
            message[l, 4 + k : 5 + k, :] += jnp.sum(e, axis=0, keepdims=True)
        return shares[0] + shares[1]

    def own_rows(ck, part_=None):
        first = ck * R + core * HALF + x * QUARTER
        return pl.ds(pl.multiple_of(first, QUARTER), QUARTER)

    def reduce_send(ph, ck, term):
        slot = ph % 2
        drain(("part", ck))
        for b in range(NB):
            rows = pl.ds(pl.multiple_of(ck * R + (1 - core) * HALF + b * BM, BM), BM)
            part[rows, :] = term(rows).astype(BF)
            push(
                part.at[rows],
                core_part.at[slot, ck * HALF + b * BM : ck * HALF + (b + 1) * BM],
                core_s.at[ph, ck, b],
                core_r.at[ph, ck, b],
                device(1 - core, y, z, x),
                ("part", ck),
            )
        for b in range(NB):
            rows = pl.ds(pl.multiple_of(ck * R + core * HALF + b * BM, BM), BM)
            value = term(rows)
            other = core_part.at[slot, ck * HALF + b * BM : ck * HALF + (b + 1) * BM]
            wait(other, core_r.at[ph, ck, b])
            part[rows, :] = (value + other[...].astype(F32)).astype(BF)
        for j in range(1, 4):
            to = (x + j) % 4
            first = ck * R + core * HALF + to * QUARTER
            push(
                part.at[pl.ds(pl.multiple_of(first, QUARTER), QUARTER)],
                ring_part.at[slot, j - 1, ck * QUARTER : (ck + 1) * QUARTER],
                ring_s.at[ph, ck, j - 1],
                ring_r.at[ph, ck, j - 1],
                device(core, y, z, to),
                ("part", ck),
            )

    def reduce_finish(ph, ck):
        slot = ph % 2
        summed = part[own_rows(ck), :].astype(F32)
        for j in range(3):
            piece = ring_part.at[slot, j, ck * QUARTER : (ck + 1) * QUARTER]
            wait(piece, ring_r.at[ph, ck, j])
            summed = summed + piece[...].astype(F32)
        return summed

    def gather_send(n, ck, buffer):
        rows = own_rows(ck)
        for j in range(1, 4):
            push(
                buffer.at[rows],
                buffer.at[rows],
                gx_s.at[n, ck, j - 1],
                gx_r.at[n, ck, j - 1],
                device(core, y, z, (x + j) % 4),
            )
        push(
            buffer.at[rows],
            buffer.at[rows],
            gc_s.at[n, ck, 0],
            gc_r.at[n, ck, 0],
            device(1 - core, y, z, x),
        )

    def gather_pass(n, ck, buffer):
        for j in range(1, 4):
            first = ck * R + core * HALF + ((x - j + 4) % 4) * QUARTER
            piece = buffer.at[pl.ds(pl.multiple_of(first, QUARTER), QUARTER)]
            wait(piece, gx_r.at[n, ck, j - 1])
            push(
                piece,
                piece,
                gc_s.at[n, ck, j],
                gc_r.at[n, ck, j],
                device(1 - core, y, z, x),
            )

    def gather_finish(n, ck, buffer):
        for j in range(4):
            wait(buffer.at[own_rows(ck)], gc_r.at[n, ck, j])

    def out_rows(seq, ck, c_, x_):
        first = seq * LEN + ck * R + c_ * HALF + x_ * QUARTER
        return ends_out.at[pl.ds(pl.multiple_of(first, QUARTER), QUARTER)]

    def give_out(n, ck):
        src = ends_low.at[n, ck * QUARTER : (ck + 1) * QUARTER]
        dst = out_rows(z_hi, ck, core, x)
        recv = out_r.at[ck, core * 4 + x]
        target = 1 - n
        for j in range(4):
            where, send = device(target, y, z, (x + j) % 4), out_s.at[n, ck, j]
            if j == 0:
                push_or_keep(core == target, src, dst, send, recv, where)
            else:
                push(src, dst, send, recv, where)

    def out_arrived(ck):
        for c_ in range(2):
            for x_ in range(4):
                wait(out_rows(z_hi, ck, c_, x_), out_r.at[ck, c_ * 4 + x_])

    def direct_first(n, ck):
        push(
            ends_low.at[n, ck * QUARTER : (ck + 1) * QUARTER],
            out_rows(z_hi, ck, core, x),
            direct_s.at[n, ck],
            direct_r.at[ck, core],
            device(1 - n, y, (z + 2) % 4, x),
        )

    def direct_copy(n, ck, c_, j):
        rows = out_rows(1 - z_hi, ck, c_, x)
        return pltpu.make_async_remote_copy(
            src_ref=rows,
            dst_ref=rows,
            send_sem=direct2_s.at[ck, c_, j - 1],
            recv_sem=direct2_r.at[ck, c_, j - 1],
            device_id=device(1 - n, y, z, (x + j) % 4),
            device_id_type=MESH,
        )

    def direct_second(n, ck):
        @pl.when(core == 1 - n)
        def _():
            for c_ in range(2):
                wait(out_rows(1 - z_hi, ck, c_, x), direct_r.at[ck, c_])
                for j in range(1, 4):
                    direct_copy(n, ck, c_, j).start()

    def direct_end(n, ck):
        @pl.when(core == 1 - n)
        def _():
            out_arrived(ck)
            for c_ in range(2):
                for j in range(1, 4):
                    direct_copy(n, ck, c_, j).wait()

    def done_copy(ck, seq):
        rows = slice(seq * LEN + ck * R, seq * LEN + (ck + 1) * R)
        return pltpu.make_async_copy(ends_out.at[rows], ends_hbm.at[rows], done_sem.at[ck, seq])

    def leave(ck):
        for n in range(2):
            direct_end(n, ck)
        for seq in range(2):
            done_copy(ck, seq).start()

    def weight_grads(l, p):
        for i in range(4):
            cols = slice(i * BQ, (i + 1) * BQ)
            if p == 0:
                pieces = [
                    ((384, NIN), dot(xhat[l, :, cols], d_joined[:, 384:NIN], 0, 0)),
                    ((NIN, NALL), dot(grads_in[l, :, cols], joined[l], 0, 0)),
                ]
            else:
                pieces = [((0, 384), dot(xhat[l, :, cols], d_joined[:, 0:384], 0, 0))]
            for (first, last), piece in pieces:
                low = piece.astype(BF)
                for k in range(2):
                    w_grad[i, k, :, first:last] = low[k * 128 : (k + 1) * 128]

    def plane_first(l, p):
        cols = slice(*G_PARTS[p])
        for k in range(2):
            z_ = 2 * core + k
            slot = (z_ - z + 3) % 4
            src, send = w_grad.at[:, k, 0:ROWS_A, cols], p1a_s.at[l, p, k]
            other = z_ != z

            @pl.when(other)
            def _(src=src, send=send, z_=z_, slot=slot):
                pltpu.make_async_remote_copy(
                    src_ref=src,
                    dst_ref=plane_a.at[l, slot, :, :, cols],
                    send_sem=send,
                    recv_sem=p1a_r.at[l, p, slot],
                    device_id=device(core, y, z_, x),
                    device_id_type=MESH,
                ).start()

            drains.setdefault("grad", []).append((other, src, send))
        for j in range(1, 4):
            to = (y + j) % 4
            push(
                w_grad.at[to, :, ROWS_A:, cols],
                plane_b.at[l, j - 1, :, :, cols],
                p1b_s.at[l, p, j - 1],
                p1b_r.at[l, p, j - 1],
                device(core, to, z, x),
                "grad",
            )

    def plane_second(l, p):
        cols = slice(*G_PARTS[p])

        @pl.when(forwarder)
        def _():
            for j in range(3):
                wait(plane_a.at[l, j, :, :, cols], p1a_r.at[l, p, j])

            def one(y_, carry):
                summed = w_grad[y_, z_lo, 0:ROWS_A, cols].astype(F32)
                for j in range(3):
                    summed = summed + plane_a[l, j, y_, :, cols].astype(F32)
                sum_a[l, y_, :, cols] = summed.astype(BF)
                return carry

            lax.fori_loop(0, 4, one, 0)
            for j in range(4):
                to = (y + j) % 4
                src, dst = sum_a.at[l, to, :, cols], own_a.at[y, :, cols]
                copy = pltpu.make_async_remote_copy(
                    src_ref=src,
                    dst_ref=dst,
                    send_sem=p2a_s.at[l, p, j],
                    recv_sem=p2a_r.at[p, y],
                    device_id=device(l, to, z, x),
                    device_id_type=MESH,
                )
                if j == 0:
                    pl.when(core == l)(pltpu.make_async_copy(src, dst, p2a_r.at[p, y]).start)
                    pl.when(core != l)(copy.start)
                else:
                    copy.start()

        for j in range(3):
            wait(plane_b.at[l, j, :, :, cols], p1b_r.at[l, p, j])
        for k in range(2):
            summed = w_grad[y, k, ROWS_A:, cols].astype(F32)
            for j in range(3):
                summed = summed + plane_b[l, j, k, :, cols].astype(F32)
            sum_b[l, k, :, cols] = summed.astype(BF)
            z_ = 2 * core + k
            push_or_keep(
                jnp.logical_and(core == l, z_ == z),
                sum_b.at[l, k, :, cols],
                own_b.at[z, :, cols],
                p2b_s.at[l, p, k],
                p2b_r.at[p, z],
                device(l, y, z_, x),
            )

    def drain_plane():
        @pl.when(forwarder)
        def _():
            for l in range(2):
                for p, cols in enumerate(G_PARTS):
                    src = sum_a.at[l, 0, :, slice(*cols)]
                    for j in range(4):
                        ended = functools.partial(wait, src, p2a_s.at[l, p, j])
                        if j == 0:
                            pl.when(core != l)(ended)
                        else:
                            ended()

    def send_small(l):
        column_sum = jnp.zeros((1, NIN), F32)
        out_sum = jnp.zeros((1, D), F32)

        def one(i, carry):
            rows = pl.ds(pl.multiple_of(i * 128, 128), 128)
            a, b = carry
            a = a + jnp.sum(d_joined[rows, :].astype(F32), axis=0, keepdims=True)
            b = b + jnp.sum(grads_in[l, rows, :].astype(F32), axis=0, keepdims=True)
            return a, b

        column_sum, out_sum = lax.fori_loop(0, LEN // 128, one, (column_sum, out_sum))
        message[l, 0:1, 0:NIN] = column_sum
        message[l, 1:2, :] = out_sum
        here = y * 4 + z
        for y_ in range(4):
            for k in range(2):
                z_ = 2 * core + k
                own = jnp.logical_and(core == l, jnp.logical_and(y_ == y, z_ == z))
                push_or_keep(
                    own,
                    message.at[l],
                    messages.at[here],
                    msg_s.at[l, y_ * 2 + k],
                    msg_r.at[here],
                    device(l, y_, z_, x),
                )

    def small_first():
        for k in range(16):
            wait(messages.at[k], msg_r.at[k])
        summed = messages[0]
        for k in range(1, 16):
            summed = summed + messages[k]
        small[...] = summed
        for j in range(1, 4):
            push(
                small,
                small_ring.at[j - 1],
                ln1_s.at[j - 1],
                ln1_r.at[j - 1],
                device(core, y, z, (x + j) % 4),
            )
        for n in range(3):
            g_qkv_b[n] = summed[0:1, n * 128 : (n + 1) * 128]
        g_up_b[...] = summed[0:1, 384:NIN]
        g_out_b[...] = summed[1:2, :]

    def small_second():
        for j in range(3):
            wait(small_ring.at[j], ln1_r.at[j])
        small_sum[...] = small[...] + small_ring[0] + small_ring[1] + small_ring[2]
        push(small_sum, small_far, ln2_s, ln2_r, device(core, y, (z + 2) % 4, x))

    def small_third():
        wait(small_far, ln2_r)
        both = small_sum[...] + small_far[...]
        for k in range(2):
            g_gains[k : k + 1, :] = both[2 + k : 3 + k, :] / gains[k : k + 1, :]
            g_offsets[k : k + 1, :] = both[4 + k : 5 + k, :] / gains[k : k + 1, :]

    def after_first_layer(ck):
        rows = own_rows(ck)
        mid = slice(ck * QUARTER, (ck + 1) * QUARTER)
        result = x_own[mid, :].astype(F32) + reduce_finish(0, ck) + out_row[0]
        low = result.astype(BF)
        y_mid[ck * QUARTER : (ck + 1) * QUARTER, :] = low
        xhat[1, rows, :] = standardize(low.astype(F32))[0].astype(BF)
        gather_send(0, ck, xhat.at[1])

    def after_second_layer(ck):
        mid = slice(ck * QUARTER, (ck + 1) * QUARTER)
        result = y_mid[mid, :].astype(F32) + reduce_finish(1, ck) + out_row[1]
        ends_low[0, mid, :] = result.astype(BF)

    def through_norm(stream, grad, e):
        scaled, inverse = standardize(stream)
        return grad + inverse * (
            e
            - jnp.mean(e, axis=-1, keepdims=True)
            - scaled * jnp.mean(e * scaled, axis=-1, keepdims=True)
        )

    def input_grad_middle(ck):
        mid = slice(ck * QUARTER, (ck + 1) * QUARTER)
        rows = own_rows(ck)
        e = reduce_finish(2, ck)
        moved = through_norm(y_mid[mid, :].astype(F32), grads_in[1, rows, :].astype(F32), e)
        grads_in[0, rows, :] = moved.astype(BF)
        gather_send(1, ck, grads_in.at[0])

    def input_grad_first(ck):
        mid = slice(ck * QUARTER, (ck + 1) * QUARTER)
        rows = own_rows(ck)
        e = reduce_finish(3, ck)
        moved = through_norm(x_own[mid, :].astype(F32), grads_in[0, rows, :].astype(F32), e)
        ends_low[1, mid, :] = moved.astype(BF)

    project_all(0, 0)
    attend_all(0, 0)
    gather_rest(0, 1)
    reduce_send(0, 0, functools.partial(branch, 0))
    gather_second(1, 0)
    project_all(0, 1)
    attend_all(0, 1)
    reduce_send(0, 1, functools.partial(branch, 0))
    after_first_layer(0)
    after_first_layer(1)
    gather_pass(0, 0, xhat.at[1])
    gather_rest(1, 0)
    gather_finish(0, 0, xhat.at[1])
    project_all(1, 0)
    gather_pass(0, 1, xhat.at[1])
    attend_all(1, 0)
    reduce_send(1, 0, functools.partial(branch, 1))
    gather_finish(0, 1, xhat.at[1])
    project_all(1, 1)
    attend_all(1, 1)
    reduce_send(1, 1, functools.partial(branch, 1))

    wait(mine, swap_s)
    backward_first(1, 1)
    backward_first(1, 0)
    after_second_layer(0)
    direct_first(0, 0)
    give_out(0, 0)
    weight_grads(1, 0)
    plane_first(1, 0)
    after_second_layer(1)
    direct_first(0, 1)
    give_out(0, 1)
    backward_second(1, 1)
    reduce_send(2, 1, functools.partial(norm_grad, 1))
    backward_second(1, 0)
    reduce_send(2, 0, functools.partial(norm_grad, 1))
    input_grad_middle(1)
    weight_grads(1, 1)
    plane_first(1, 1)
    input_grad_middle(0)
    gather_pass(1, 1, grads_in.at[0])
    direct_second(0, 0)
    direct_second(0, 1)
    send_small(1)
    plane_second(1, 0)
    gather_finish(1, 1, grads_in.at[0])

    backward_first(0, 1)
    gather_pass(1, 0, grads_in.at[0])
    backward_second(0, 1)
    reduce_send(3, 1, functools.partial(norm_grad, 0))
    gather_finish(1, 0, grads_in.at[0])
    backward_first(0, 0)
    plane_second(1, 1)
    drain("grad")
    weight_grads(0, 0)
    plane_first(0, 0)
    backward_second(0, 0)
    reduce_send(3, 0, functools.partial(norm_grad, 0))
    input_grad_first(1)
    direct_first(1, 1)
    give_out(1, 1)
    weight_grads(0, 1)
    plane_first(0, 1)
    send_small(0)
    input_grad_first(0)
    direct_first(1, 0)
    give_out(1, 0)
    direct_second(1, 1)
    plane_second(0, 0)
    small_first()
    direct_second(1, 0)
    plane_second(0, 1)
    small_second()

    leave(1)
    for k in range(4):
        for p, cols in enumerate(G_PARTS):
            wait(own_a.at[k, :, slice(*cols)], p2a_r.at[p, k])
            wait(own_b.at[k, :, slice(*cols)], p2b_r.at[p, k])
    total[0:ROWS_A, :] = (
        own_a[0].astype(F32) + own_a[1].astype(F32) + own_a[2].astype(F32) + own_a[3].astype(F32)
    )
    total[ROWS_A:128, :] = (
        own_b[0].astype(F32) + own_b[1].astype(F32) + own_b[2].astype(F32) + own_b[3].astype(F32)
    )
    for n in range(7):
        k = 0 if n < 3 else 1
        cols = slice(n * 128, (n + 1) * 128)
        grad = total[:, cols] * gain_cols[k] + offset_cols[k] * small[0:1, cols]
        if n < 3:
            g_qkv[n] = grad
        else:
            g_up[:, (n - 3) * 128 : (n - 2) * 128] = grad
    g_dense[...] = total[:, NIN : NIN + 128].T
    g_down[...] = total[:, NIN + 128 : NALL].T
    small_third()
    leave(0)
    for ck in range(NCH):
        for seq in range(2):
            done_copy(ck, seq).wait()
    drain("grad")
    for ck in range(NCH):
        drain(("part", ck))
    drain("end")
    drain_first()
    drain_second(0, 1)
    drain_second(1, 0)
    drain_extra()
    drain_plane()


def settle(*refs):
    count = (len(refs) - 2) // 3
    sources, targets, held = refs[:count], refs[count : 2 * count], refs[2 * count : 3 * count]
    sem_in, sem_out = refs[-2:]
    trips = []
    rows = sources[0].shape[0] // 4
    for k in range(4):
        piece = pl.ds(k * rows, rows)
        trips.append((sources[0].at[piece], held[0].at[piece], targets[0].at[piece]))
    for n in range(1, count):
        trips.append((sources[n], held[n], targets[n]))
    arrivals = []
    departures = []
    for n, (source, stop, target) in enumerate(trips):
        arrivals.append(pltpu.make_async_copy(source, stop, sem_in.at[n]))
        departures.append(pltpu.make_async_copy(stop, target, sem_out.at[n]))
    for copy in arrivals:
        copy.start()
    for arrival, departure in zip(arrivals, departures):
        arrival.wait()
        departure.start()
    for copy in departures:
        copy.wait()


def body(ends_in, ln_gains, ln_biases, qkv_w, qkv_bias, dense_w, up_w, up_bias, down_w, out_bias):
    cosine, sine = rotary_tables()
    vmem = pl.BlockSpec(memory_space=pltpu.VMEM)
    anywhere = pl.BlockSpec(memory_space=pl.ANY)

    def shape(*dims):
        return jax.ShapeDtypeStruct(dims, F32)

    def sems(*dims):
        return pltpu.SemaphoreType.DMA(dims)

    outs = pl.pallas_call(
        kernel,
        out_shape=[
            jax.ShapeDtypeStruct((2 * LEN, D), BF),
            shape(2, D),
            shape(2, D),
            shape(3, 128, 128),
            shape(3, 1, 128),
            shape(128, 128),
            shape(128, 512),
            shape(1, 512),
            shape(512, 128),
            shape(1, D),
        ],
        in_specs=[anywhere] + [vmem] * 9 + [anywhere] * 2,
        out_specs=[anywhere] + [vmem] * 9,
        scratch_shapes=[
            pltpu.VMEM((LEN, 2 * HD), F32),
            pltpu.VMEM((LEN, 2 * HD), F32),
            pltpu.VMEM((2 * LEN, D), BF),
            pltpu.VMEM((128, NALL), BF),
            pltpu.VMEM((8, 256), F32),
            pltpu.VMEM((2, 8, 8, 256), F32),
            pltpu.VMEM((2, 1, 1024), F32),
            pltpu.VMEM((2, 1, 1024), F32),
            pltpu.VMEM((2, D, NALL), BF),
            pltpu.VMEM((LEN, D), BF),
            pltpu.VMEM((2, LEN, D), BF),
            pltpu.VMEM((2, LEN, D), BF),
            pltpu.VMEM((LEN // 8, D), BF),
            pltpu.VMEM((LEN // 8, D), BF),
            pltpu.VMEM((2, LEN, NOUT), BF),
            pltpu.VMEM((2, LEN, 512), BF),
            pltpu.VMEM((2, LEN, 128), BF),
            pltpu.VMEM((2, LEN, 128), BF),
            pltpu.VMEM((2, LEN, 128), BF),
            pltpu.VMEM((2, 128, LEN), BF),
            pltpu.VMEM((128, LEN), BF),
            pltpu.VMEM((2, 10, BQ, 2 * BQ), BF),
            pltpu.VMEM((2, LEN // BQ, 2 * BQ), F32),
            pltpu.VMEM((2, 128, LEN), F32),
            pltpu.VMEM((LEN, 2 * BQ), F32),
            pltpu.VMEM((LEN, 128), BF),
            pltpu.VMEM((LEN, NIN), BF),
            pltpu.VMEM((2, LEN // 2, D), BF),
            pltpu.VMEM((2, 3, LEN // 8, D), BF),
            pltpu.VMEM((2, LEN // 8, D), BF),
            pltpu.VMEM((4, 2, 128, NALL), BF),
            pltpu.VMEM((2, 3, 4, ROWS_A, NALL), BF),
            pltpu.VMEM((2, 3, 2, ROWS_B, NALL), BF),
            pltpu.VMEM((2, 4, ROWS_A, NALL), BF),
            pltpu.VMEM((2, 2, ROWS_B, NALL), BF),
            pltpu.VMEM((4, ROWS_A, NALL), BF),
            pltpu.VMEM((4, ROWS_B, NALL), BF),
            pltpu.VMEM((128, NALL), F32),
            pltpu.VMEM((2, 8, D), F32),
            pltpu.VMEM((16, 8, D), F32),
            pltpu.VMEM((8, D), F32),
            pltpu.VMEM((3, 8, D), F32),
            pltpu.VMEM((8, D), F32),
            pltpu.VMEM((8, D), F32),
            sems(2),
            sems(NCH, 2),
            pltpu.SemaphoreType.DMA,
            pltpu.SemaphoreType.DMA,
            pltpu.SemaphoreType.DMA,
            sems(2, 2, 4),
            sems(2, 2, 2, 8),
            sems(2, 2, 4, 3),
            sems(2, 2, 2, 3),
            sems(16),
            sems(2, 8),
            sems(4, NCH, NB),
            sems(4, NCH, NB),
            sems(4, NCH, 3),
            sems(4, NCH, 3),
            sems(2, NCH, 3),
            sems(2, NCH, 3),
            sems(2, NCH, 4),
            sems(2, NCH, 4),
            sems(2, NCH, 4),
            sems(NCH, 8),
            sems(2, NCH),
            sems(NCH, 2),
            sems(NCH, 2, 3),
            sems(NCH, 2, 3),
            sems(2, 8),
            sems(16),
            sems(2, 2, 2),
            sems(2, 2, 3),
            sems(2, 2, 3),
            sems(2, 2, 3),
            sems(2, 2, 4),
            sems(2, 4),
            sems(2, 2, 2),
            sems(2, 4),
            sems(3),
            sems(3),
            pltpu.SemaphoreType.DMA,
            pltpu.SemaphoreType.DMA,
        ],
        compiler_params=pltpu.CompilerParams(
            collective_id=0, has_side_effects=True, vmem_limit_bytes=63 * 2**20
        ),
        cost_estimate=pl.CostEstimate(
            flops=22 * 10**9, bytes_accessed=20 * 10**6, transcendentals=4 * 10**6
        ),
    )(
        ends_in[0],
        qkv_w[0],
        dense_w[0],
        up_w[0],
        down_w[0],
        ln_gains[0],
        ln_biases[0],
        jnp.transpose(qkv_bias, (1, 0, 2)),
        up_bias,
        out_bias,
        jnp.asarray(cosine),
        jnp.asarray(sine),
    )
    outs = pl.pallas_call(
        settle,
        out_shape=[jax.ShapeDtypeStruct(out.shape, out.dtype) for out in outs],
        in_specs=[anywhere] * len(outs),
        out_specs=[anywhere] * len(outs),
        scratch_shapes=[pltpu.VMEM(out.shape, out.dtype) for out in outs]
        + [sems(len(outs) + 3), sems(len(outs) + 3)],
        compiler_params=pltpu.CompilerParams(vmem_limit_bytes=63 * 2**20),
        cost_estimate=pl.CostEstimate(flops=0, bytes_accessed=10 * 10**6, transcendentals=0),
    )(*outs)
    out, gains, offsets, d_qkv, d_qkv_b, d_dense, d_up, d_up_b, d_down, d_out_b = outs
    return (
        out[None],
        gains[None],
        offsets[None],
        d_qkv[None],
        jnp.transpose(d_qkv_b, (1, 0, 2)),
        d_dense[None],
        d_up[None],
        d_up_b,
        d_down[None],
        d_out_b,
    )


def solution(mesh):
    in_specs = (
        P("section", "dp", None),
        P("section", None, None),
        P("section", None, None),
        P("section", None, "dp", "tensor"),
        P("section", None, "tensor"),
        P("section", "tensor", "dp"),
        P("section", "dp", "tensor"),
        P("section", "tensor"),
        P("section", "tensor", "dp"),
        P("section", None),
    )
    out_specs = (
        P("section", "dp", None),
        P("section", None, None),
        P("section", None, None),
        P("section", None, "dp", "tensor"),
        P("section", None, "tensor"),
        P("section", "tensor", "dp"),
        P("section", "dp", "tensor"),
        P("section", "tensor"),
        P("section", "tensor", "dp"),
        P("section", None),
    )
    return jax.shard_map(body, mesh=mesh, in_specs=in_specs, out_specs=out_specs, check_vma=False)
```
